256 devices in a mesh: src: 32 (over z, x), tgt: 8 (over y, core).
Axes of the slice: x: 4, y: 4, z: 8, core: 2. Of those that a mesh axis runs over, the one named last changes fastest.
Arguments:
- source_embed: bfloat16 [512, 65536], P(None, 'src')
- target_embed: bfloat16 [512, 16384], P('src', 'tgt')
- source_labels: int32 [65536], P('src'), may hold values from 0 to 3, as said below
- target_labels: int32 [16384], P('tgt'), may hold values from 0 to 3, as said below
- pair_blocks: int32 [32, 8, 24, 2], P('src', 'tgt'), may hold values from 0 to 7, as said below
- pair_count: int32 [32, 8], P('src', 'tgt'), may hold values from 8 to 24, as said below
Outputs:
- source_potential: float32 [65536], P('src')
- target_potential: float32 [16384], P('tgt')
- label_cost: float32 [4, 4], replicated
The draws below stay inside these ranges and needn't reach their ends.
Inputs may be any that keep to these rules, and one draw needn't show every extreme that they name: `source_labels`: within each device's rows of 2048 samples, the first 4 samples have labels 0, 1, ... in order. `target_labels`: within each device's rows of 2048 samples, the first 4 samples have labels 0, 1, ... in order. `pair_blocks`: each device's list holds distinct pairs; its first 8 entries are the pairs (b, b) for b = 0, 1, ... in order; entries after the count are valid pairs and are ignored. `pair_count`: some device's count equals 24.
All inputs are finite; a program needn't handle non-finite values.
Results may differ from the reference program's by a relative error of at most 0.0003.
Values may be sent and summed in bfloat16 or wider, within the bound.
No kernel may reach another device: no remote copies, remote signals or barrier semaphores. Data moves between devices by JAX's collectives and lax.ppermute only.
A program may use at most 64 MiB of HBM per device.

```python
import math
import jax
import jax.numpy as jnp
from jax import lax

D = 512
CLASSES = 4
BLOCK = 256
ITERS = 2
ROWS = 2048
BLK = 8
MAXP = 24
NS = 65536
NT = 16384
N_SRC = 32
N_TGT = 8


def class_labels(key, count, salt):
    key = jax.random.fold_in(key, salt)
    labels = jax.random.randint(key, (count,), 0, CLASSES)
    local = jnp.arange(count, dtype=jnp.int32) % ROWS
    return jnp.where(local < CLASSES, local, labels).astype(jnp.int32)


def corpus_base(key, labels, count, devices):
    keys = jax.random.split(key, 2)
    centers = 0.03 * jax.random.normal(keys[0], (D, CLASSES), jnp.float32)
    device = (jnp.arange(count) // ROWS).astype(jnp.float32)
    device_scale = 0.04 * (1.0 + 2.0 * device / max(devices - 1, 1))
    class_scale = 0.7 + 0.6 * jnp.arange(CLASSES, dtype=jnp.float32) / (CLASSES - 1)
    noise = jax.random.normal(keys[1], (D, count), jnp.float32)
    scale = device_scale * class_scale[labels]
    return centers[:, labels] + noise * scale[None, :]


def draw_source_labels(key, part):
    return class_labels(key, NS, 77)


def draw_target_labels(key, part):
    return class_labels(key, NT, 78)


def draw_source_embed(key, part):
    labels = class_labels(key, NS, 77)
    key = jax.random.fold_in(key, 5)
    return corpus_base(key, labels, NS, N_SRC).astype(jnp.bfloat16)


def draw_target_embed(key, part):
    labels = class_labels(key, NT, 78)
    key = jax.random.fold_in(key, 6)
    return corpus_base(key, labels, NT, N_TGT).astype(jnp.bfloat16)


def draw_pair_blocks(key, part):
    key = jax.random.fold_in(key, 11)
    keys = jax.random.split(key, N_SRC * N_TGT)

    def one_list(device_key):
        index = jnp.arange(BLK * BLK, dtype=jnp.int32)
        diagonal = index // BLK == index % BLK
        shuffled = jax.random.permutation(device_key, BLK * BLK).astype(jnp.int32)
        score = jnp.where(diagonal, index // BLK, BLK + shuffled)
        order = jnp.argsort(score, stable=True)[:MAXP].astype(jnp.int32)
        return jnp.stack([order // BLK, order % BLK], axis=-1)
    return jax.vmap(one_list)(keys).reshape(N_SRC, N_TGT, MAXP, 2).astype(jnp.int32)


def draw_pair_count(key, part):
    key = jax.random.fold_in(key, 12)
    keys = jax.random.split(key, 4)
    shape = (N_SRC, N_TGT)
    base = jax.random.randint(keys[0], shape, BLK, (BLK + MAXP) // 2 + 1)
    heavy = jax.random.randint(keys[1], shape, 0, 8) == 0
    heavy_count = MAXP - jax.random.randint(keys[2], shape, 0, 2)
    counts = jnp.where(heavy, heavy_count, base).reshape(-1)
    full_at = jax.random.randint(keys[3], (), 0, N_SRC * N_TGT)
    counts = counts.at[full_at].set(MAXP)
    return counts.reshape(shape).astype(jnp.int32)


def setup_inputs(seed: int = 0) -> dict:
    streams_of = jax.random.split(jax.random.key(seed), 7)
    return {
        "source_embed": draw_source_embed(jax.random.fold_in(streams_of[6], 71), 0),
        "target_embed": draw_target_embed(jax.random.fold_in(streams_of[6], 71), 0),
        "source_labels": draw_source_labels(jax.random.fold_in(streams_of[6], 71), 0),
        "target_labels": draw_target_labels(jax.random.fold_in(streams_of[6], 71), 0),
        "pair_blocks": draw_pair_blocks(jax.random.fold_in(streams_of[6], 71), 0),
        "pair_count": draw_pair_count(jax.random.fold_in(streams_of[6], 71), 0),
    }


EPSILON = 0.05
LOWEST = -1e+30
HIGHEST = lax.Precision.HIGHEST

def class_onehot(labels):
    classes = jnp.arange(CLASSES, dtype=jnp.int32)
    return (labels[None, :] == classes[:, None]).astype(jnp.float32)

def class_moments(values, onehot):
    counts = lax.optimization_barrier(jnp.sum(onehot, axis=1))
    sums = jnp.einsum('cr,dr->cd', onehot, values, precision=HIGHEST)
    means = sums / counts[:, None]
    centered = values - jnp.dot(means.T, onehot, precision=HIGHEST)
    spread = jnp.einsum('cr,dr->cd', onehot, centered * centered, precision=HIGHEST)
    return (means, spread / counts[:, None])

def class_distance(src_mean, src_var, tgt_mean, tgt_var):
    gap = src_mean[:, None, :] - tgt_mean[None, :, :]
    roots = jnp.sqrt(src_var + 1e-06)[:, None, :] - jnp.sqrt(tgt_var + 1e-06)[None, :, :]
    return lax.optimization_barrier(jnp.sum(gap * gap + roots * roots, axis=2))

def cost_from_cross(cross, src_sq, tgt_sq, row_lab, tgt_onehot, row_block, col_block):
    row_start = row_block * BLOCK
    col_start = col_block * BLOCK
    lab_rows = lax.dynamic_slice_in_dim(row_lab, row_start, BLOCK, 1)
    lab_cols = lax.dynamic_slice_in_dim(tgt_onehot, col_start, BLOCK, 1)
    labels_tile = jnp.dot(lab_rows.T, lab_cols, precision=HIGHEST)
    row_sq = lax.dynamic_slice_in_dim(src_sq, row_start, BLOCK)
    col_sq = lax.dynamic_slice_in_dim(tgt_sq, col_start, BLOCK)
    return row_sq[:, None] + col_sq[None, :] - 2.0 * cross + labels_tile

def absorb(carry, scores, start, axis):
    maxima, totals = carry
    tile_max = lax.optimization_barrier(jnp.max(scores, axis=axis))
    tile_sum = lax.optimization_barrier(jnp.sum(jnp.exp(scores - jnp.expand_dims(tile_max, axis)), axis=axis))
    old_max = lax.dynamic_slice_in_dim(maxima, start, BLOCK)
    old_sum = lax.dynamic_slice_in_dim(totals, start, BLOCK)
    new_max = jnp.maximum(old_max, tile_max)
    new_sum = old_sum * jnp.exp(old_max - new_max) + tile_sum * jnp.exp(tile_max - new_max)
    maxima = lax.dynamic_update_slice_in_dim(maxima, new_max, start, 0)
    totals = lax.dynamic_update_slice_in_dim(totals, new_sum, start, 0)
    return (maxima, totals)

def device_pass(source_embed, target_embed, src_sq, tgt_sq, row_lab, tgt_onehot, pair_blocks, pair_count, src_pot, tgt_pot, by_rows):

    def one_device(device):
        src_dev = device // N_TGT
        tgt_dev = device % N_TGT
        src_start = (src_dev * ROWS).astype(jnp.int32)
        tgt_start = (tgt_dev * ROWS).astype(jnp.int32)
        source_part = lax.dynamic_slice_in_dim(source_embed, src_start, ROWS, 1)
        target_part = lax.dynamic_slice_in_dim(target_embed, tgt_start, ROWS, 1)
        src_sq_part = lax.dynamic_slice_in_dim(src_sq, src_start, ROWS)
        tgt_sq_part = lax.dynamic_slice_in_dim(tgt_sq, tgt_start, ROWS)
        lab_part = lax.dynamic_slice_in_dim(row_lab, src_start, ROWS, 1)
        onehot_part = lax.dynamic_slice_in_dim(tgt_onehot, tgt_start, ROWS, 1)
        src_pot_part = lax.dynamic_slice_in_dim(src_pot, src_start, ROWS)
        tgt_pot_part = lax.dynamic_slice_in_dim(tgt_pot, tgt_start, ROWS)
        pairs = pair_blocks[src_dev, tgt_dev]
        count = pair_count[src_dev, tgt_dev]

        def step(index, carry):
            row_block = pairs[index, 0]
            col_block = pairs[index, 1]
            source_tile = lax.dynamic_slice_in_dim(source_part, row_block * BLOCK, BLOCK, 1)
            target_tile = lax.dynamic_slice_in_dim(target_part, col_block * BLOCK, BLOCK, 1)
            cross = lax.dot_general(source_tile, target_tile, (((0,), (0,)), ((), ())), preferred_element_type=jnp.float32)
            cost_tile = cost_from_cross(cross, src_sq_part, tgt_sq_part, lab_part, onehot_part, row_block, col_block)
            if by_rows:
                column_pot = lax.dynamic_slice_in_dim(tgt_pot_part, col_block * BLOCK, BLOCK)
                scores = (column_pot[None, :] - cost_tile) / EPSILON
                return absorb(carry, scores, row_block * BLOCK, 1)
            row_pot = lax.dynamic_slice_in_dim(src_pot_part, row_block * BLOCK, BLOCK)
            scores = (row_pot[:, None] - cost_tile) / EPSILON
            return absorb(carry, scores, col_block * BLOCK, 0)
        start = (jnp.full((ROWS,), LOWEST, jnp.float32), jnp.zeros((ROWS,), jnp.float32))
        return lax.fori_loop(0, count, step, start)
    devices = jnp.arange(N_SRC * N_TGT, dtype=jnp.int32)
    maxima, totals = lax.map(one_device, devices)
    return (maxima.reshape(N_SRC, N_TGT, ROWS), totals.reshape(N_SRC, N_TGT, ROWS))

def reference(source_embed, target_embed, source_labels, target_labels, pair_blocks, pair_count):
    src_values = source_embed.astype(jnp.float32)
    tgt_values = target_embed.astype(jnp.float32)
    src_onehot = class_onehot(source_labels)
    tgt_onehot = class_onehot(target_labels)
    src_mean, src_var = class_moments(src_values, src_onehot)
    tgt_mean, tgt_var = class_moments(tgt_values, tgt_onehot)
    label_cost = class_distance(src_mean, src_var, tgt_mean, tgt_var)
    src_sq = lax.optimization_barrier(jnp.sum(src_values * src_values, axis=0))
    tgt_sq = lax.optimization_barrier(jnp.sum(tgt_values * tgt_values, axis=0))
    row_lab = jnp.dot(label_cost.T, src_onehot, precision=HIGHEST)
    src_pot = jnp.zeros((NS,), jnp.float32)
    tgt_pot = jnp.zeros((NT,), jnp.float32)
    for step in range(ITERS):
        maxima, totals = device_pass(source_embed, target_embed, src_sq, tgt_sq, row_lab, tgt_onehot, pair_blocks, pair_count, src_pot, tgt_pot, True)
        highest = lax.optimization_barrier(jnp.max(maxima, axis=1))
        summed = lax.optimization_barrier(jnp.sum(totals * jnp.exp(maxima - highest[:, None, :]), axis=1))
        src_pot = (-EPSILON * (highest + jnp.log(summed) - math.log(NT))).reshape(NS)
        maxima, totals = device_pass(source_embed, target_embed, src_sq, tgt_sq, row_lab, tgt_onehot, pair_blocks, pair_count, src_pot, tgt_pot, False)
        highest = lax.optimization_barrier(jnp.max(maxima, axis=0))
        summed = lax.optimization_barrier(jnp.sum(totals * jnp.exp(maxima - highest[None, :, :]), axis=0))
        tgt_pot = (-EPSILON * (highest + jnp.log(summed) - math.log(NS))).reshape(NT)
    return (src_pot, tgt_pot, label_cost)
```

```python
import functools
import math

import jax
import jax.numpy as jnp
import numpy as np
from jax import lax
from jax.experimental import pallas as pl
from jax.experimental.pallas import tpu as pltpu
from jax.sharding import Mesh, PartitionSpec as P

CLASSES = 4
BLOCK = 256
ROWS = 2048
BLK = ROWS // BLOCK
LANES = 128
CHUNKS = ROWS // LANES
MAXP = 24
WIDTH = 512

EPSILON = 0.05
LOWEST = -1e30
HIGHEST = lax.Precision.HIGHEST
LOG2E = 1.0 / math.log(2.0)
TO_LOG2 = LOG2E / EPSILON
TO_POT = EPSILON / LOG2E

SRC = ("z", "x")
TGT = ("y", "c")
VMEM_LIMIT = 40 * 1024 * 1024


def log2(x):
    return jnp.log(x) * LOG2E


def shared(x, axis):
    n = lax.axis_size(axis)
    return lax.all_to_all(jnp.broadcast_to(x[None], (n,) + x.shape), axis, 0, 0)


def class_onehot(labels):
    classes = jnp.arange(CLASSES, dtype=jnp.int32)
    return (labels[None, :] == classes[:, None]).astype(jnp.float32)


def local_moments(values, onehot, counts):
    sums = jnp.einsum("cr,dr->cd", onehot, values, precision=HIGHEST)
    means = sums / counts[:, None]
    centered = values - jnp.dot(means.T, onehot, precision=HIGHEST)
    spread = jnp.einsum("cr,dr->cd", onehot, centered * centered, precision=HIGHEST)
    return (means, spread)


def joined(counts, means, spreads):
    total = jnp.sum(counts, axis=0)
    share = counts / total[None]
    mean = jnp.sum(means * share[:, :, None], axis=0)
    delta = means - mean[None]
    spread = jnp.sum(spreads + delta * delta * counts[:, :, None], axis=0)
    return total, mean, spread


def class_distance(src_mean, src_var, tgt_mean, tgt_var):
    gap = src_mean[:, None, :] - tgt_mean[None, :, :]
    roots = jnp.sqrt(src_var + 1e-06)[:, None, :] - jnp.sqrt(tgt_var + 1e-06)[None, :, :]
    return jnp.sum(gap * gap + roots * roots, axis=2)


def packed(*parts):
    flat = jnp.concatenate([p.reshape(-1) for p in parts])
    rows = -(-flat.size // (8 * LANES)) * 8
    return jnp.pad(flat, (0, rows * LANES - flat.size)).reshape(rows, LANES)


def three_parts(v):
    hi = v.astype(jnp.bfloat16).astype(jnp.float32)
    rest = v - hi
    mid = rest.astype(jnp.bfloat16).astype(jnp.float32)
    return hi, mid, rest - mid


def joined_lse(g_ref):
    g = g_ref[...]
    top = jnp.max(g, axis=0)
    return top + log2(jnp.sum(jnp.exp2(g - top[None]), axis=0))


def row_finish(top, total, out_ref):
    lines = []
    for k in range(CHUNKS):
        at = pl.ds(k * LANES, LANES)
        lse = top[at, :] + log2(jnp.sum(total[at, :], axis=1, keepdims=True))
        lines.append(lse.T[0:1, :])
    line = jnp.concatenate(lines, axis=0)
    out_ref[...] = jnp.broadcast_to(line[None], out_ref.shape)


def widen_top(top):
    for k in range(CHUNKS):
        at = pl.ds(k * LANES, LANES)
        top[at, :] = jnp.broadcast_to(jnp.max(top[at, :], axis=1, keepdims=True), (LANES, LANES))


def block_at(pairs, index):
    row = pl.multiple_of(pairs[2 * index] * BLOCK, BLOCK)
    return row, pairs[2 * index + 1]


def cost_kernel(
    pairs, count, label_cost, xt, y, src_sq, src_lab, tgt_lab, tiles, out_ref, xa, ya, top, total
):
    row_id = lax.broadcasted_iota(jnp.int32, (16, 1), 0)
    part = row_id // CLASSES
    cls = row_id % CLASSES
    labels = src_lab[...]
    u = jnp.broadcast_to(src_sq[...], (16, ROWS))
    for a in range(CLASSES):
        line = jnp.zeros((16, 1), jnp.float32)
        for b in range(CLASSES):
            line = jnp.where(cls == b, label_cost[a * CLASSES + b], line)
        u = u + jnp.where(labels == a, line, 0.0)
    hi, mid, lo = three_parts(-0.5 * u)
    ones = jnp.where(row_id < 15, 1.0, 0.0)
    xa[...] = jnp.where(
        part == 0, hi, jnp.where(part == 1, mid, jnp.where(part == 2, lo, ones))
    ).astype(jnp.bfloat16)

    def square(k, acc):
        v = y[pl.ds(pl.multiple_of(k * 16, 16), 16), :].astype(jnp.float32)
        return acc + v * v

    tgt_sq = lax.fori_loop(0, WIDTH // 16, square, jnp.zeros((16, ROWS), jnp.float32))
    hi, mid, lo = three_parts(-0.5 * jnp.sum(tgt_sq, axis=0, keepdims=True))
    onehot = jnp.where(tgt_lab[...] == cls, 1.0, 0.0)
    ya[...] = jnp.where(
        part < 3,
        onehot,
        jnp.where(cls == 0, hi, jnp.where(cls == 1, mid, jnp.where(cls == 2, lo, 0.0))),
    ).astype(jnp.bfloat16)

    top[...] = jnp.full(top.shape, LOWEST, jnp.float32)
    total[...] = jnp.zeros(total.shape, jnp.float32)

    def build(index, _):
        row, col = block_at(pairs, index)
        rows = pl.ds(row, BLOCK)
        cols = pl.ds(pl.multiple_of(col * BLOCK, BLOCK), BLOCK)
        cross = jnp.dot(xt[rows, :], y[:, cols], preferred_element_type=jnp.float32)
        extra = lax.dot_general(
            xa[:, rows], ya[:, cols], (((0,), (0,)), ((), ())), preferred_element_type=jnp.float32
        )
        tile = (cross + extra) * (2.0 * TO_LOG2)
        tiles[index] = tile
        top[rows, :] = jnp.maximum(top[rows, :], jnp.maximum(tile[:, :LANES], tile[:, LANES:]))
        return 0

    lax.fori_loop(0, count[0], build, 0)
    widen_top(top)

    def add(index, _):
        row, _ = block_at(pairs, index)
        rows = pl.ds(row, BLOCK)
        high = top[rows, :]
        left = jnp.exp2(tiles[index, :, :LANES] - high)
        right = jnp.exp2(tiles[index, :, LANES:] - high)
        total[rows, :] = total[rows, :] + (left + right)
        return 0

    lax.fori_loop(0, count[0], add, 0)
    row_finish(top, total, out_ref)


def row_kernel(log_total, pairs, count, tiles, g_ref, out_ref, pot, top, total):
    pot[...] = log_total - joined_lse(g_ref)
    top[...] = jnp.full(top.shape, LOWEST, jnp.float32)
    total[...] = jnp.zeros(total.shape, jnp.float32)

    def scores(index, col):
        left = tiles[index, :, :LANES] + pot[pl.ds(2 * col, 1), :]
        right = tiles[index, :, LANES:] + pot[pl.ds(2 * col + 1, 1), :]
        return left, right

    def highest(index, _):
        row, col = block_at(pairs, index)
        rows = pl.ds(row, BLOCK)
        left, right = scores(index, col)
        top[rows, :] = jnp.maximum(top[rows, :], jnp.maximum(left, right))
        return 0

    lax.fori_loop(0, count[0], highest, 0)
    widen_top(top)

    def add(index, _):
        row, col = block_at(pairs, index)
        rows = pl.ds(row, BLOCK)
        left, right = scores(index, col)
        high = top[rows, :]
        total[rows, :] = total[rows, :] + (jnp.exp2(left - high) + jnp.exp2(right - high))
        return 0

    lax.fori_loop(0, count[0], add, 0)
    row_finish(top, total, out_ref)


def col_kernel(log_total, pairs, count, tiles, g_ref, out_ref, pot_ref, pot, top, total):
    line = log_total - joined_lse(g_ref)
    pot_ref[...] = line * TO_POT
    for k in range(CHUNKS):
        pot[pl.ds(k * LANES, LANES), :] = jnp.broadcast_to(line[k : k + 1, :], (LANES, LANES)).T
    top[...] = jnp.full(top.shape, LOWEST, jnp.float32)
    total[...] = jnp.zeros(total.shape, jnp.float32)

    def scores(index, row):
        rows = pl.ds(row, BLOCK)
        high = pot[rows, :]
        tile = tiles[index]
        return tile + jnp.concatenate([high, high], axis=1)

    def highest(index, _):
        row, col = block_at(pairs, index)
        score = scores(index, row)
        top[col] = jnp.maximum(top[col], jnp.max(score.reshape(BLOCK // 8, 8, BLOCK), axis=0))
        return 0

    lax.fori_loop(0, count[0], highest, 0)
    for k in range(BLK):
        top[k] = jnp.broadcast_to(jnp.max(top[k], axis=0, keepdims=True), (8, BLOCK))

    def add(index, _):
        row, col = block_at(pairs, index)
        score = scores(index, row).reshape(BLOCK // 8, 8, BLOCK)
        total[col] = total[col] + jnp.sum(jnp.exp2(score - top[col][None]), axis=0)
        return 0

    lax.fori_loop(0, count[0], add, 0)
    lines = []
    for k in range(BLK):
        lse = top[k][0:1] + log2(jnp.sum(total[k], axis=0, keepdims=True))
        lines += [lse[:, :LANES], lse[:, LANES:]]
    out = jnp.concatenate(lines, axis=0)
    out_ref[...] = jnp.broadcast_to(out[None], out_ref.shape)


def last_kernel(log_total, g_ref, pot_ref):
    pot_ref[...] = (log_total - joined_lse(g_ref)) * TO_POT


def smem():
    return pl.BlockSpec(memory_space=pltpu.SMEM)


def vmem():
    return pl.BlockSpec(memory_space=pltpu.VMEM)


def f32(*shape):
    return jax.ShapeDtypeStruct(shape, jnp.float32)


def params():
    return pltpu.CompilerParams(vmem_limit_bytes=VMEM_LIMIT)


def on_device(source_embed, target_embed, source_labels, target_labels, pair_blocks, pair_count):
    pairs = pair_blocks.reshape(-1)
    count = pair_count.reshape(-1)
    n_src, n_tgt = lax.axis_size(SRC), lax.axis_size(TGT)

    near = shared(target_embed, "x").reshape(-1, ROWS)
    target_full = lax.all_gather(near, "z", axis=0, tiled=True)

    src_onehot = class_onehot(source_labels)
    tgt_onehot = class_onehot(target_labels)
    src_counts = jnp.sum(src_onehot, axis=1)
    tgt_counts = jnp.sum(tgt_onehot, axis=1)
    src_values = source_embed.astype(jnp.float32)
    src_sq = jnp.sum(src_values * src_values, axis=0)
    tgt_values = target_embed.astype(jnp.float32)
    part = tgt_values.shape[0]
    tgt_mean, tgt_spread = local_moments(tgt_values, tgt_onehot, tgt_counts)
    got = shared(packed(tgt_mean, tgt_spread, tgt_counts), TGT).reshape(n_tgt, -1)
    size = CLASSES * part
    tgt_total, tgt_mean, tgt_spread = joined(
        got[:, 2 * size : 2 * size + CLASSES],
        got[:, :size].reshape(n_tgt, CLASSES, part),
        got[:, size : 2 * size].reshape(n_tgt, CLASSES, part),
    )
    tgt_slice = jnp.concatenate([tgt_mean, tgt_spread / tgt_total[:, None]], axis=0)
    src_mean, src_spread = local_moments(src_values, src_onehot, src_counts)
    full = CLASSES * WIDTH
    slices = tgt_slice[None]
    for axis in ("x", "z"):
        n = lax.axis_size(axis)
        got = shared(packed(src_mean, src_spread, slices, src_counts), axis).reshape(n, -1)
        width = slices.size
        src_counts, src_mean, src_spread = joined(
            got[:, 2 * full + width : 2 * full + width + CLASSES],
            got[:, :full].reshape(n, CLASSES, WIDTH),
            got[:, full : 2 * full].reshape(n, CLASSES, WIDTH),
        )
        slices = got[:, 2 * full : 2 * full + width].reshape(-1, 2 * CLASSES, part)
    tgt_both = slices.transpose(1, 0, 2).reshape(2 * CLASSES, WIDTH)
    label_cost = class_distance(
        src_mean, src_spread / src_counts[:, None], tgt_both[:CLASSES], tgt_both[CLASSES:]
    )

    tall = pltpu.VMEM((ROWS, LANES), jnp.float32)
    wide = pltpu.VMEM((BLK, 8, BLOCK), jnp.float32)
    log_src = math.log2(ROWS * n_src)
    log_tgt = math.log2(ROWS * n_tgt)
    tiles, sent = pl.pallas_call(
        cost_kernel,
        out_shape=(f32(MAXP, BLOCK, BLOCK), f32(n_tgt, CHUNKS, LANES)),
        in_specs=[smem(), smem(), smem(), vmem(), vmem(), vmem(), vmem(), vmem()],
        out_specs=(vmem(), vmem()),
        scratch_shapes=[
            pltpu.VMEM((16, ROWS), jnp.bfloat16),
            pltpu.VMEM((16, ROWS), jnp.bfloat16),
            tall,
            tall,
        ],
        compiler_params=params(),
        name="cost_rows",
    )(
        pairs,
        count,
        label_cost.reshape(-1),
        source_embed.T,
        target_full,
        src_sq[None],
        source_labels[None],
        target_labels[None],
    )

    def columns(got):
        return pl.pallas_call(
            functools.partial(col_kernel, log_tgt),
            out_shape=(f32(n_src, CHUNKS, LANES), f32(CHUNKS, LANES)),
            in_specs=[smem(), smem(), vmem(), vmem()],
            out_specs=(vmem(), vmem()),
            scratch_shapes=[tall, wide, wide],
            compiler_params=params(),
            name="columns",
        )(pairs, count, tiles, got)

    def rows(got):
        return pl.pallas_call(
            functools.partial(row_kernel, log_src),
            out_shape=f32(n_tgt, CHUNKS, LANES),
            in_specs=[smem(), smem(), vmem(), vmem()],
            out_specs=vmem(),
            scratch_shapes=[pltpu.VMEM((CHUNKS, LANES), jnp.float32), tall, tall],
            compiler_params=params(),
            name="rows",
        )(pairs, count, tiles, got)

    sent, _ = columns(lax.all_to_all(sent, TGT, 0, 0))
    sent = rows(lax.all_to_all(sent, SRC, 0, 0))
    sent, src_pot = columns(lax.all_to_all(sent, TGT, 0, 0))
    tgt_pot = pl.pallas_call(
        functools.partial(last_kernel, log_src),
        out_shape=f32(CHUNKS, LANES),
        in_specs=[vmem()],
        out_specs=vmem(),
        compiler_params=params(),
        name="last",
    )(lax.all_to_all(sent, SRC, 0, 0))
    return (src_pot.reshape(-1), tgt_pot.reshape(-1), label_cost)


def solution(mesh):
    fine = Mesh(np.asarray(mesh.devices).reshape(8, 4, 4, 2), SRC + TGT)
    return jax.shard_map(
        on_device,
        mesh=fine,
        in_specs=(
            P(None, SRC),
            P(SRC, TGT),
            P(SRC),
            P(TGT),
            P(SRC, TGT, None, None),
            P(SRC, TGT),
        ),
        out_specs=(P(SRC), P(TGT), P()),
        check_vma=False,
    )
```

```python
import functools
import math

import jax
import jax.numpy as jnp
import numpy as np
from jax import lax
from jax.experimental import pallas as pl
from jax.experimental.pallas import tpu as pltpu
from jax.sharding import Mesh, PartitionSpec as P

CLASSES = 4
BLOCK = 256
ROWS = 2048
BLK = ROWS // BLOCK
LANES = 128
CHUNKS = ROWS // LANES
MAXP = 24
UNROLL = 4
WIDTH = 512

EPSILON = 0.05
LOWEST = -1e30
LOG2E = 1.0 / math.log(2.0)
TO_LOG2 = LOG2E / EPSILON
TO_POT = EPSILON / LOG2E

SRC = ("z", "x")
TGT = ("y", "c")
VMEM_LIMIT = 40 * 1024 * 1024


def log2(x):
    return jnp.log(x) * LOG2E


def repeated_onehot(labels):
    row_id = lax.broadcasted_iota(jnp.int32, (16, 1), 0)
    return jnp.where(row_id < 12, jnp.where(labels == row_id % CLASSES, 1.0, 0.0), 0.0)


def across(onehot, values):
    return lax.dot_general(
        onehot, values, (((1,), (1,)), ((), ())), preferred_element_type=jnp.float32
    )


def class_group(values, onehot, counts):
    part = lax.broadcasted_iota(jnp.int32, (16, 1), 0) // CLASSES
    wide = values.astype(jnp.float32)
    mean = across(onehot, values) / counts
    hi, mid, lo = three_parts(mean)
    parts = jnp.where(
        part == 0, hi, jnp.where(part == 1, mid, jnp.where(part == 2, lo, 0.0))
    ).astype(jnp.bfloat16)
    center = lax.dot_general(
        parts, onehot, (((0,), (0,)), ((), ())), preferred_element_type=jnp.float32
    )
    centered = wide - center
    hi, mid, lo = three_parts(centered * centered)
    spread = sum(across(onehot, p.astype(jnp.bfloat16)) for p in (hi, mid, lo))
    return jnp.where(part == 0, mean, spread)[:8], wide


def target_group_kernel(embed, labels, out_ref):
    onehot = repeated_onehot(labels[...])
    counts = jnp.maximum(jnp.sum(onehot, axis=1, keepdims=True), 1.0)
    group, _ = class_group(embed[...], onehot.astype(jnp.bfloat16), counts)
    peers = out_ref.shape[0]
    out_ref[...] = jnp.zeros(out_ref.shape, jnp.float32)
    out_ref[:, 0:8, 0 : group.shape[1]] = jnp.broadcast_to(group[None], (peers,) + group.shape)
    out_ref[:, 8:16, :] = jnp.broadcast_to(counts[None, :8], (peers, 8, LANES))


def source_group_kernel(embed, labels, out_ref, sq_ref):
    onehot = repeated_onehot(labels[...])
    counts = jnp.maximum(jnp.sum(onehot, axis=1, keepdims=True), 1.0)
    onehot = onehot.astype(jnp.bfloat16)
    sq = jnp.zeros((1, ROWS), jnp.float32)
    for c in range(WIDTH // LANES):
        group, wide = class_group(embed[c * LANES : (c + 1) * LANES, :], onehot, counts)
        out_ref[8 * c : 8 * c + 8, :] = group
        sq = sq + jnp.sum(wide * wide, axis=0, keepdims=True)
    out_ref[32:40, :] = jnp.broadcast_to(counts[:8], (8, LANES))
    sq_ref[...] = sq


def joined_counts(counts):
    total = functools.reduce(jnp.add, counts)
    return total, [c / total for c in counts]


def joined_group(groups, counts, shares):
    row_id = lax.broadcasted_iota(jnp.int32, (8, LANES), 0)
    mean = functools.reduce(jnp.add, [g * w for g, w in zip(groups, shares)])
    between = functools.reduce(
        jnp.add, [(g - mean) * (g - mean) * c for g, c in zip(groups, counts)]
    )
    spread = functools.reduce(jnp.add, groups) + pltpu.roll(between, 4, 0)
    return jnp.where(row_id < CLASSES, mean, spread)


def near_kernel(tgt_got, src_group, out_ref):
    peers = tgt_got.shape[0]
    counts = [tgt_got[k, 8:16, :] for k in range(peers)]
    total, shares = joined_counts(counts)
    group = joined_group([tgt_got[k, 0:8, :] for k in range(peers)], counts, shares)
    row_id = lax.broadcasted_iota(jnp.int32, (8, LANES), 0)
    group = jnp.where(row_id < CLASSES, group, group / total)
    for k in range(out_ref.shape[0]):
        out_ref[k, 0:40, :] = src_group[...]
        out_ref[k, 40:48, :] = group


def source_joined(got):
    peers = got.shape[0]
    counts = [got[k, 32:40, :] for k in range(peers)]
    total, shares = joined_counts(counts)
    groups = [
        joined_group([got[k, 8 * c : 8 * c + 8, :] for k in range(peers)], counts, shares)
        for c in range(WIDTH // LANES)
    ]
    return groups, total


def middle_kernel(part, got, out_ref):
    groups, total = source_joined(got)
    tgt = got[0, 40:48, :]
    for k in range(1, got.shape[0]):
        tgt = tgt + pltpu.roll(got[k, 40:48, :], k * part, 1)
    for k in range(out_ref.shape[0]):
        for c, group in enumerate(groups):
            out_ref[k, 8 * c : 8 * c + 8, :] = group
        out_ref[k, 32:40, :] = total
        out_ref[k, 40:48, :] = tgt


def label_kernel(part, got, src_sq, src_lab, label_ref, xa_ref):
    groups, total = source_joined(got)
    row_id = lax.broadcasted_iota(jnp.int32, (8, LANES), 0)
    lane_id = lax.broadcasted_iota(jnp.int32, (8, LANES), 1)
    each = LANES // part
    sides = ([], [])
    for c, group in enumerate(groups):
        tgt = got[each * c, 40:48, :]
        for k in range(1, each):
            tgt = tgt + pltpu.roll(got[each * c + k, 40:48, :], k * part, 1)
        for side, stat in zip(sides, (jnp.where(row_id < CLASSES, group, group / total), tgt)):
            side.append(jnp.where(row_id < CLASSES, stat, jnp.sqrt(stat + 1e-06)))

    def distances(one, other):
        out = jnp.zeros((8, LANES), jnp.float32)
        for k in range(CLASSES):
            far = jnp.zeros((8, LANES), jnp.float32)
            for g, h in zip(one, other):
                gap = g - jnp.where(row_id < CLASSES, h[k : k + 1], h[CLASSES + k : CLASSES + k + 1])
                far = far + gap * gap
            far = far + pltpu.roll(far, 4, 0)
            out = jnp.where(lane_id == k, jnp.sum(far, axis=1, keepdims=True), out)
        return out

    label_ref[...] = distances(*sides)[:CLASSES, :CLASSES]
    by_target = distances(*sides[::-1])
    by_target = jnp.concatenate([by_target, by_target], axis=0)
    row_id = lax.broadcasted_iota(jnp.int32, (16, 1), 0)
    part_id = row_id // CLASSES
    labels = src_lab[...]
    u = jnp.broadcast_to(src_sq[...], (16, ROWS))
    for a in range(CLASSES):
        u = u + jnp.where(labels == a, by_target[:, a : a + 1], 0.0)
    hi, mid, lo = three_parts(-0.5 * u)
    ones = jnp.where(row_id < 15, 1.0, 0.0)
    xa_ref[...] = jnp.where(
        part_id == 0, hi, jnp.where(part_id == 1, mid, jnp.where(part_id == 2, lo, ones))
    ).astype(jnp.bfloat16)


def spread_kernel(x, out_ref):
    for k in range(out_ref.shape[0]):
        out_ref[k] = x[...]


def three_parts(v):
    hi = v.astype(jnp.bfloat16).astype(jnp.float32)
    rest = v - hi
    mid = rest.astype(jnp.bfloat16).astype(jnp.float32)
    return hi, mid, rest - mid


def joined_lse(g_ref):
    g = g_ref[...]
    top = jnp.max(g, axis=0)
    return top + log2(jnp.sum(jnp.exp2(g - top[None]), axis=0))


def row_finish(top, total, out_ref):
    lines = []
    for k in range(CHUNKS):
        at = pl.ds(k * LANES, LANES)
        lse = top[at, :] + log2(jnp.sum(total[at, :], axis=1, keepdims=True))
        lines.append(lse.T[0:1, :])
    line = jnp.concatenate(lines, axis=0)
    out_ref[...] = jnp.broadcast_to(line[None], out_ref.shape)


def widen_top(top):
    for k in range(CHUNKS):
        at = pl.ds(k * LANES, LANES)
        top[at, :] = jnp.broadcast_to(jnp.max(top[at, :], axis=1, keepdims=True), (LANES, LANES))


def over_pairs(count, body, unroll):
    def several(step, _):
        for k in range(unroll):
            body(step * unroll + k)
        return 0

    steps = (count[0] + UNROLL - 1) // UNROLL * (UNROLL // unroll)
    lax.fori_loop(0, steps, several, 0)


def block_at(pairs, index):
    row = pl.multiple_of(pairs[2 * index] * BLOCK, BLOCK)
    return row, pairs[2 * index + 1]


def cost_kernel(pairs, count, xa, xt, y, tgt_lab, tiles, out_ref, ya, top, total):
    row_id = lax.broadcasted_iota(jnp.int32, (16, 1), 0)
    part = row_id // CLASSES
    cls = row_id % CLASSES

    def square(k, acc):
        v = y[pl.ds(pl.multiple_of(k * 16, 16), 16), :].astype(jnp.float32)
        return acc + v * v

    tgt_sq = lax.fori_loop(0, WIDTH // 16, square, jnp.zeros((16, ROWS), jnp.float32))
    hi, mid, lo = three_parts(-0.5 * jnp.sum(tgt_sq, axis=0, keepdims=True))
    onehot = jnp.where(tgt_lab[...] == cls, 1.0, 0.0)
    ya[...] = jnp.where(
        part < 3,
        onehot,
        jnp.where(cls == 0, hi, jnp.where(cls == 1, mid, jnp.where(cls == 2, lo, 0.0))),
    ).astype(jnp.bfloat16)

    top[...] = jnp.full(top.shape, LOWEST, jnp.float32)
    total[...] = jnp.zeros(total.shape, jnp.float32)

    def build(index):
        row, col = block_at(pairs, index)
        rows = pl.ds(row, BLOCK)
        cols = pl.ds(pl.multiple_of(col * BLOCK, BLOCK), BLOCK)
        cross = jnp.dot(xt[rows, :], y[:, cols], preferred_element_type=jnp.float32)
        extra = lax.dot_general(
            xa[:, rows], ya[:, cols], (((0,), (0,)), ((), ())), preferred_element_type=jnp.float32
        )
        tile = (cross + extra) * (2.0 * TO_LOG2) + jnp.where(index < count[0], 0.0, LOWEST)
        tiles[index] = tile
        top[rows, :] = jnp.maximum(top[rows, :], jnp.maximum(tile[:, :LANES], tile[:, LANES:]))

    over_pairs(count, build, 2)
    widen_top(top)

    def add(index):
        row, _ = block_at(pairs, index)
        rows = pl.ds(row, BLOCK)
        high = top[rows, :]
        left = jnp.exp2(tiles[index, :, :LANES] - high)
        right = jnp.exp2(tiles[index, :, LANES:] - high)
        total[rows, :] = total[rows, :] + (left + right)

    over_pairs(count, add, 4)
    row_finish(top, total, out_ref)


def row_kernel(log_total, pairs, count, tiles, g_ref, out_ref, pot, top, total):
    pot[...] = log_total - joined_lse(g_ref)
    top[...] = jnp.full(top.shape, LOWEST, jnp.float32)
    total[...] = jnp.zeros(total.shape, jnp.float32)

    def scores(index, col):
        left = tiles[index, :, :LANES] + pot[pl.ds(2 * col, 1), :]
        right = tiles[index, :, LANES:] + pot[pl.ds(2 * col + 1, 1), :]
        return left, right

    def highest(index):
        row, col = block_at(pairs, index)
        rows = pl.ds(row, BLOCK)
        left, right = scores(index, col)
        top[rows, :] = jnp.maximum(top[rows, :], jnp.maximum(left, right))

    over_pairs(count, highest, 4)
    widen_top(top)

    def add(index):
        row, col = block_at(pairs, index)
        rows = pl.ds(row, BLOCK)
        left, right = scores(index, col)
        high = top[rows, :]
        total[rows, :] = total[rows, :] + (jnp.exp2(left - high) + jnp.exp2(right - high))

    over_pairs(count, add, 4)
    row_finish(top, total, out_ref)


def col_kernel(log_total, pairs, count, tiles, g_ref, out_ref, pot_ref, pot, top, total):
    line = log_total - joined_lse(g_ref)
    pot_ref[...] = line * TO_POT
    for k in range(CHUNKS):
        pot[pl.ds(k * LANES, LANES), :] = jnp.broadcast_to(line[k : k + 1, :], (LANES, LANES)).T
    top[...] = jnp.full(top.shape, LOWEST, jnp.float32)
    total[...] = jnp.zeros(total.shape, jnp.float32)

    def scores(index, row):
        rows = pl.ds(row, BLOCK)
        high = pot[rows, :]
        tile = tiles[index]
        return tile + jnp.concatenate([high, high], axis=1)

    def highest(index):
        row, col = block_at(pairs, index)
        score = scores(index, row)
        top[col] = jnp.maximum(top[col], jnp.max(score.reshape(BLOCK // 8, 8, BLOCK), axis=0))

    over_pairs(count, highest, 4)
    for k in range(BLK):
        top[k] = jnp.broadcast_to(jnp.max(top[k], axis=0, keepdims=True), (8, BLOCK))

    def add(index):
        row, col = block_at(pairs, index)
        score = scores(index, row).reshape(BLOCK // 8, 8, BLOCK)
        total[col] = total[col] + jnp.sum(jnp.exp2(score - top[col][None]), axis=0)

    over_pairs(count, add, 4)
    lines = []
    for k in range(BLK):
        lse = top[k][0:1] + log2(jnp.sum(total[k], axis=0, keepdims=True))
        lines += [lse[:, :LANES], lse[:, LANES:]]
    out = jnp.concatenate(lines, axis=0)
    out_ref[...] = jnp.broadcast_to(out[None], out_ref.shape)


def last_kernel(log_total, g_ref, pot_ref):
    pot_ref[...] = (log_total - joined_lse(g_ref)) * TO_POT


def smem():
    return pl.BlockSpec(memory_space=pltpu.SMEM)


def vmem():
    return pl.BlockSpec(memory_space=pltpu.VMEM)


def f32(*shape):
    return jax.ShapeDtypeStruct(shape, jnp.float32)


def params():
    return pltpu.CompilerParams(vmem_limit_bytes=VMEM_LIMIT)


def on_device(source_embed, target_embed, source_labels, target_labels, pair_blocks, pair_count):
    pairs = pair_blocks.reshape(-1)
    count = pair_count.reshape(-1)
    n_src, n_tgt = lax.axis_size(SRC), lax.axis_size(TGT)

    def call(kernel, out_shape, *args, name):
        return pl.pallas_call(
            kernel,
            out_shape=out_shape,
            in_specs=[vmem()] * len(args),
            out_specs=jax.tree.map(lambda _: vmem(), out_shape),
            compiler_params=params(),
            name=name,
        )(*args)

    n_x, n_z = lax.axis_size("x"), lax.axis_size("z")
    part = target_embed.shape[0]
    near = call(
        spread_kernel,
        jax.ShapeDtypeStruct((n_x,) + target_embed.shape, jnp.bfloat16),
        target_embed,
        name="spread",
    )
    tgt_group = call(
        target_group_kernel,
        f32(n_tgt, 16, LANES),
        target_embed,
        target_labels[None],
        name="target_group",
    )
    near = lax.all_to_all(near, "x", 0, 0)
    near, source_embed, tgt_group = lax.optimization_barrier((near, source_embed, tgt_group))
    target_full = lax.all_gather(near.reshape(-1, ROWS), "z", axis=0, tiled=True)

    tgt_got = lax.all_to_all(tgt_group, TGT, 0, 0)
    src_group, src_sq = call(
        source_group_kernel,
        (f32(40, LANES), f32(1, ROWS)),
        source_embed,
        source_labels[None],
        name="source_group",
    )
    stats = call(near_kernel, f32(n_x, 48, LANES), tgt_got, src_group, name="near")
    stats = lax.all_to_all(stats, "x", 0, 0)
    stats = call(
        functools.partial(middle_kernel, part), f32(n_z, 48, LANES), stats, name="middle"
    )
    stats = lax.all_to_all(stats, "z", 0, 0)
    label_cost, xa = call(
        functools.partial(label_kernel, part * n_x),
        (f32(CLASSES, CLASSES), jax.ShapeDtypeStruct((16, ROWS), jnp.bfloat16)),
        stats,
        src_sq,
        source_labels[None],
        name="label",
    )

    tall = pltpu.VMEM((ROWS, LANES), jnp.float32)
    wide = pltpu.VMEM((BLK, 8, BLOCK), jnp.float32)
    log_src = math.log2(ROWS * n_src)
    log_tgt = math.log2(ROWS * n_tgt)
    tiles, sent = pl.pallas_call(
        cost_kernel,
        out_shape=(f32(MAXP, BLOCK, BLOCK), f32(n_tgt, CHUNKS, LANES)),
        in_specs=[smem(), smem(), vmem(), vmem(), vmem(), vmem()],
        out_specs=(vmem(), vmem()),
        scratch_shapes=[
            pltpu.VMEM((16, ROWS), jnp.bfloat16),
            tall,
            tall,
        ],
        compiler_params=params(),
        name="cost_rows",
    )(
        pairs,
        count,
        xa,
        source_embed.T,
        target_full,
        target_labels[None],
    )

    def columns(got):
        return pl.pallas_call(
            functools.partial(col_kernel, log_tgt),
            out_shape=(f32(n_src, CHUNKS, LANES), f32(CHUNKS, LANES)),
            in_specs=[smem(), smem(), vmem(), vmem()],
            out_specs=(vmem(), vmem()),
            scratch_shapes=[tall, wide, wide],
            compiler_params=params(),
            name="columns",
        )(pairs, count, tiles, got)

    def rows(got):
        return pl.pallas_call(
            functools.partial(row_kernel, log_src),
            out_shape=f32(n_tgt, CHUNKS, LANES),
            in_specs=[smem(), smem(), vmem(), vmem()],
            out_specs=vmem(),
            scratch_shapes=[pltpu.VMEM((CHUNKS, LANES), jnp.float32), tall, tall],
            compiler_params=params(),
            name="rows",
        )(pairs, count, tiles, got)

    sent, _ = columns(lax.all_to_all(sent, TGT, 0, 0))
    sent = rows(lax.all_to_all(sent, SRC, 0, 0))
    sent, src_pot = columns(lax.all_to_all(sent, TGT, 0, 0))
    tgt_pot = pl.pallas_call(
        functools.partial(last_kernel, log_src),
        out_shape=f32(CHUNKS, LANES),
        in_specs=[vmem()],
        out_specs=vmem(),
        compiler_params=params(),
        name="last",
    )(lax.all_to_all(sent, SRC, 0, 0))
    return (src_pot.reshape(-1), tgt_pot.reshape(-1), label_cost)


def solution(mesh):
    fine = Mesh(np.asarray(mesh.devices).reshape(8, 4, 4, 2), SRC + TGT)
    return jax.shard_map(
        on_device,
        mesh=fine,
        in_specs=(
            P(None, SRC),
            P(SRC, TGT),
            P(SRC),
            P(TGT),
            P(SRC, TGT, None, None),
            P(SRC, TGT),
        ),
        out_specs=(P(SRC), P(TGT), P()),
        check_vma=False,
    )
```

```python
import functools
import math

import jax
import jax.numpy as jnp
import numpy as np
from jax import lax
from jax.experimental import pallas as pl
from jax.experimental.pallas import tpu as pltpu
from jax.sharding import Mesh, PartitionSpec as P

CLASSES = 4
BLOCK = 256
ROWS = 2048
BLK = ROWS // BLOCK
LANES = 128
CHUNKS = ROWS // LANES
MAXP = 24
UNROLL = 4
WIDTH = 512

EPSILON = 0.05
LOWEST = -1e30
LOG2E = 1.0 / math.log(2.0)
TO_LOG2 = LOG2E / EPSILON
TO_POT = EPSILON / LOG2E

SRC = ("z", "x")
TGT = ("y", "c")
VMEM_LIMIT = 24 * 1024 * 1024


def log2(x):
    return jnp.log(x) * LOG2E


def repeated_onehot(labels):
    row_id = lax.broadcasted_iota(jnp.int32, (16, 1), 0)
    return jnp.where(row_id < 12, jnp.where(labels == row_id % CLASSES, 1.0, 0.0), 0.0)


def across(onehot, values):
    return lax.dot_general(
        onehot, values, (((1,), (1,)), ((), ())), preferred_element_type=jnp.float32
    )


def class_group(values, onehot, counts):
    part = lax.broadcasted_iota(jnp.int32, (16, 1), 0) // CLASSES
    wide = values.astype(jnp.float32)
    mean = across(onehot, values) / counts
    hi, mid, lo = three_parts(mean)
    parts = jnp.where(
        part == 0, hi, jnp.where(part == 1, mid, jnp.where(part == 2, lo, 0.0))
    ).astype(jnp.bfloat16)
    center = lax.dot_general(
        parts, onehot, (((0,), (0,)), ((), ())), preferred_element_type=jnp.float32
    )
    centered = wide - center
    hi, mid, lo = three_parts(centered * centered)
    spread = sum(across(onehot, p.astype(jnp.bfloat16)) for p in (hi, mid, lo))
    return jnp.where(part == 0, mean, spread)[:8], wide


def target_group_kernel(embed, labels, out_ref):
    onehot = repeated_onehot(labels[...])
    counts = jnp.maximum(jnp.sum(onehot, axis=1, keepdims=True), 1.0)
    group, _ = class_group(embed[...], onehot.astype(jnp.bfloat16), counts)
    peers = out_ref.shape[0]
    out_ref[...] = jnp.zeros(out_ref.shape, jnp.float32)
    out_ref[:, 0:8, 0 : group.shape[1]] = jnp.broadcast_to(group[None], (peers,) + group.shape)
    out_ref[:, 8:16, :] = jnp.broadcast_to(counts[None, :8], (peers, 8, LANES))


def source_group_kernel(embed, labels, out_ref, sq_ref):
    onehot = repeated_onehot(labels[...])
    counts = jnp.maximum(jnp.sum(onehot, axis=1, keepdims=True), 1.0)
    onehot = onehot.astype(jnp.bfloat16)
    sq = jnp.zeros((1, ROWS), jnp.float32)
    for c in range(WIDTH // LANES):
        group, wide = class_group(embed[c * LANES : (c + 1) * LANES, :], onehot, counts)
        out_ref[8 * c : 8 * c + 8, :] = group
        sq = sq + jnp.sum(wide * wide, axis=0, keepdims=True)
    out_ref[32:40, :] = jnp.broadcast_to(counts[:8], (8, LANES))
    sq_ref[...] = sq


def joined_counts(counts):
    total = functools.reduce(jnp.add, counts)
    return total, [c / total for c in counts]


def joined_group(groups, counts, shares):
    row_id = lax.broadcasted_iota(jnp.int32, (8, LANES), 0)
    mean = functools.reduce(jnp.add, [g * w for g, w in zip(groups, shares)])
    between = functools.reduce(
        jnp.add, [(g - mean) * (g - mean) * c for g, c in zip(groups, counts)]
    )
    spread = functools.reduce(jnp.add, groups) + pltpu.roll(between, 4, 0)
    return jnp.where(row_id < CLASSES, mean, spread)


def near_kernel(tgt_got, src_group, out_ref):
    peers = tgt_got.shape[0]
    counts = [tgt_got[k, 8:16, :] for k in range(peers)]
    total, shares = joined_counts(counts)
    group = joined_group([tgt_got[k, 0:8, :] for k in range(peers)], counts, shares)
    row_id = lax.broadcasted_iota(jnp.int32, (8, LANES), 0)
    group = jnp.where(row_id < CLASSES, group, group / total)
    for k in range(out_ref.shape[0]):
        out_ref[k, 0:40, :] = src_group[...]
        out_ref[k, 40:48, :] = group


def source_joined(got):
    peers = got.shape[0]
    counts = [got[k, 32:40, :] for k in range(peers)]
    total, shares = joined_counts(counts)
    groups = [
        joined_group([got[k, 8 * c : 8 * c + 8, :] for k in range(peers)], counts, shares)
        for c in range(WIDTH // LANES)
    ]
    return groups, total


def middle_kernel(width, got, out_ref):
    groups, total = source_joined(got)
    each = LANES // width
    for c in range(WIDTH // LANES):
        tgt = got[each * c, 40:48, :]
        for k in range(1, each):
            tgt = tgt + pltpu.roll(got[each * c + k, 40:48, :], k * width, 1)
        for k in range(out_ref.shape[0]):
            out_ref[k, 8 * c : 8 * c + 8, :] = groups[c]
            out_ref[k, 40 + 8 * c : 48 + 8 * c, :] = tgt
    for k in range(out_ref.shape[0]):
        out_ref[k, 32:40, :] = total


def label_kernel(part, got, src_sq, src_lab, label_ref, xa_ref):
    groups, total = source_joined(got)
    row_id = lax.broadcasted_iota(jnp.int32, (8, LANES), 0)
    lane_id = lax.broadcasted_iota(jnp.int32, (8, LANES), 1)
    sides = ([], [])
    for c, group in enumerate(groups):
        at = slice(40 + 8 * c, 48 + 8 * c)
        tgt = got[0, at, :]
        for k in range(1, got.shape[0]):
            tgt = tgt + pltpu.roll(got[k, at, :], k * part, 1)
        for side, stat in zip(sides, (jnp.where(row_id < CLASSES, group, group / total), tgt)):
            side.append(jnp.where(row_id < CLASSES, stat, jnp.sqrt(stat + 1e-06)))

    def distances(one, other):
        out = jnp.zeros((8, LANES), jnp.float32)
        for k in range(CLASSES):
            far = jnp.zeros((8, LANES), jnp.float32)
            for g, h in zip(one, other):
                gap = g - jnp.where(row_id < CLASSES, h[k : k + 1], h[CLASSES + k : CLASSES + k + 1])
                far = far + gap * gap
            far = far + pltpu.roll(far, 4, 0)
            out = jnp.where(lane_id == k, jnp.sum(far, axis=1, keepdims=True), out)
        return out

    label_ref[...] = distances(*sides)[:CLASSES, :CLASSES]
    by_target = distances(*sides[::-1])
    by_target = jnp.concatenate([by_target, by_target], axis=0)
    row_id = lax.broadcasted_iota(jnp.int32, (16, 1), 0)
    part_id = row_id // CLASSES
    labels = src_lab[...]
    u = jnp.broadcast_to(src_sq[...], (16, ROWS))
    for a in range(CLASSES):
        u = u + jnp.where(labels == a, by_target[:, a : a + 1], 0.0)
    hi, mid, lo = three_parts(-0.5 * u)
    ones = jnp.where(row_id < 15, 1.0, 0.0)
    xa_ref[...] = jnp.where(
        part_id == 0, hi, jnp.where(part_id == 1, mid, jnp.where(part_id == 2, lo, ones))
    ).astype(jnp.bfloat16)


def spread_kernel(x, out_ref):
    for k in range(out_ref.shape[0]):
        out_ref[k] = x[...]


def three_parts(v):
    hi = v.astype(jnp.bfloat16).astype(jnp.float32)
    rest = v - hi
    mid = rest.astype(jnp.bfloat16).astype(jnp.float32)
    return hi, mid, rest - mid


def joined_lse(g_ref):
    g = g_ref[...]
    top = jnp.max(g, axis=0)
    return top + log2(jnp.sum(jnp.exp2(g - top[None]), axis=0))


def row_finish(top, total, out_ref):
    lines = []
    for k in range(CHUNKS):
        at = pl.ds(k * LANES, LANES)
        lse = top[at, :] + log2(jnp.sum(total[at, :], axis=1, keepdims=True))
        lines.append(lse.T[0:1, :])
    line = jnp.concatenate(lines, axis=0)
    out_ref[...] = jnp.broadcast_to(line[None], out_ref.shape)


def widen_top(top):
    for k in range(CHUNKS):
        at = pl.ds(k * LANES, LANES)
        top[at, :] = jnp.broadcast_to(jnp.max(top[at, :], axis=1, keepdims=True), (LANES, LANES))


def over_pairs(count, body, unroll):
    def several(step, _):
        for k in range(unroll):
            body(step * unroll + k)
        return 0

    steps = (count[0] + UNROLL - 1) // UNROLL * (UNROLL // unroll)
    lax.fori_loop(0, steps, several, 0)


def block_at(pairs, index):
    row = pl.multiple_of(pairs[2 * index] * BLOCK, BLOCK)
    return row, pairs[2 * index + 1]


def cost_kernel(n_x, pairs, count, place, xa, xt, *args):
    pieces, (tgt_lab, tiles, out_ref, y, ya, top, total) = args[:n_x], args[n_x:]
    row_id = lax.broadcasted_iota(jnp.int32, (16, 1), 0)
    part = row_id // CLASSES
    cls = row_id % CLASSES

    tgt_sq = jnp.zeros((16, ROWS), jnp.float32)
    for far, piece in enumerate(pieces):
        at = lax.rem(place[0] + far, n_x)
        for k in range(piece.shape[0]):
            y[pl.ds(pl.multiple_of((k * n_x + at) * 16, 16), 16), :] = piece[k]
            v = piece[k].astype(jnp.float32)
            tgt_sq = tgt_sq + v * v

    hi, mid, lo = three_parts(-0.5 * jnp.sum(tgt_sq, axis=0, keepdims=True))
    onehot = jnp.where(tgt_lab[...] == cls, 1.0, 0.0)
    ya[...] = jnp.where(
        part < 3,
        onehot,
        jnp.where(cls == 0, hi, jnp.where(cls == 1, mid, jnp.where(cls == 2, lo, 0.0))),
    ).astype(jnp.bfloat16)

    top[...] = jnp.full(top.shape, LOWEST, jnp.float32)
    total[...] = jnp.zeros(total.shape, jnp.float32)

    def build(index):
        row, col = block_at(pairs, index)
        rows = pl.ds(row, BLOCK)
        cols = pl.ds(pl.multiple_of(col * BLOCK, BLOCK), BLOCK)
        cross = jnp.dot(xt[rows, :], y[:, cols], preferred_element_type=jnp.float32)
        extra = lax.dot_general(
            xa[:, rows], ya[:, cols], (((0,), (0,)), ((), ())), preferred_element_type=jnp.float32
        )
        tile = (cross + extra) * (2.0 * TO_LOG2) + jnp.where(index < count[0], 0.0, LOWEST)
        tiles[index] = tile
        top[rows, :] = jnp.maximum(top[rows, :], jnp.maximum(tile[:, :LANES], tile[:, LANES:]))

    over_pairs(count, build, 2)
    widen_top(top)

    def add(index):
        row, _ = block_at(pairs, index)
        rows = pl.ds(row, BLOCK)
        high = top[rows, :]
        left = jnp.exp2(tiles[index, :, :LANES] - high)
        right = jnp.exp2(tiles[index, :, LANES:] - high)
        total[rows, :] = total[rows, :] + (left + right)

    over_pairs(count, add, 4)
    row_finish(top, total, out_ref)


def row_kernel(log_total, pairs, count, tiles, g_ref, out_ref, pot, top, total):
    pot[...] = log_total - joined_lse(g_ref)
    top[...] = jnp.full(top.shape, LOWEST, jnp.float32)
    total[...] = jnp.zeros(total.shape, jnp.float32)

    def scores(index, col):
        left = tiles[index, :, :LANES] + pot[pl.ds(2 * col, 1), :]
        right = tiles[index, :, LANES:] + pot[pl.ds(2 * col + 1, 1), :]
        return left, right

    def highest(index):
        row, col = block_at(pairs, index)
        rows = pl.ds(row, BLOCK)
        left, right = scores(index, col)
        top[rows, :] = jnp.maximum(top[rows, :], jnp.maximum(left, right))

    over_pairs(count, highest, 4)
    widen_top(top)

    def add(index):
        row, col = block_at(pairs, index)
        rows = pl.ds(row, BLOCK)
        left, right = scores(index, col)
        high = top[rows, :]
        total[rows, :] = total[rows, :] + (jnp.exp2(left - high) + jnp.exp2(right - high))

    over_pairs(count, add, 4)
    row_finish(top, total, out_ref)


def col_kernel(log_total, pairs, count, tiles, g_ref, out_ref, pot_ref, pot, top, total):
    line = log_total - joined_lse(g_ref)
    pot_ref[...] = line * TO_POT
    for k in range(CHUNKS):
        pot[pl.ds(k * LANES, LANES), :] = jnp.broadcast_to(line[k : k + 1, :], (LANES, LANES)).T
    top[...] = jnp.full(top.shape, LOWEST, jnp.float32)
    total[...] = jnp.zeros(total.shape, jnp.float32)

    def scores(index, row):
        rows = pl.ds(row, BLOCK)
        high = pot[rows, :]
        tile = tiles[index]
        return tile + jnp.concatenate([high, high], axis=1)

    def highest(index):
        row, col = block_at(pairs, index)
        score = scores(index, row)
        top[col] = jnp.maximum(top[col], jnp.max(score.reshape(BLOCK // 8, 8, BLOCK), axis=0))

    over_pairs(count, highest, 4)
    for k in range(BLK):
        top[k] = jnp.broadcast_to(jnp.max(top[k], axis=0, keepdims=True), (8, BLOCK))

    def add(index):
        row, col = block_at(pairs, index)
        score = scores(index, row).reshape(BLOCK // 8, 8, BLOCK)
        total[col] = total[col] + jnp.sum(jnp.exp2(score - top[col][None]), axis=0)

    over_pairs(count, add, 4)
    lines = []
    for k in range(BLK):
        lse = top[k][0:1] + log2(jnp.sum(total[k], axis=0, keepdims=True))
        lines += [lse[:, :LANES], lse[:, LANES:]]
    out = jnp.concatenate(lines, axis=0)
    out_ref[...] = jnp.broadcast_to(out[None], out_ref.shape)


def last_kernel(log_total, g_ref, pot_ref):
    pot_ref[...] = (log_total - joined_lse(g_ref)) * TO_POT


def smem():
    return pl.BlockSpec(memory_space=pltpu.SMEM)


def vmem():
    return pl.BlockSpec(memory_space=pltpu.VMEM)


def f32(*shape):
    return jax.ShapeDtypeStruct(shape, jnp.float32)


def params():
    return pltpu.CompilerParams(vmem_limit_bytes=VMEM_LIMIT)


def on_device(source_embed, target_embed, source_labels, target_labels, pair_blocks, pair_count):
    pairs = pair_blocks.reshape(-1)
    count = pair_count.reshape(-1)
    n_src, n_tgt = lax.axis_size(SRC), lax.axis_size(TGT)

    def call(kernel, out_shape, *args, name):
        return pl.pallas_call(
            kernel,
            out_shape=out_shape,
            in_specs=[vmem()] * len(args),
            out_specs=jax.tree.map(lambda _: vmem(), out_shape),
            compiler_params=params(),
            name=name,
        )(*args)

    n_x, n_z = lax.axis_size("x"), lax.axis_size("z")
    part = target_embed.shape[0]
    near = call(
        spread_kernel,
        jax.ShapeDtypeStruct((n_z,) + target_embed.shape, jnp.bfloat16),
        target_embed,
        name="spread",
    )
    tgt_group = call(
        target_group_kernel,
        f32(n_tgt, 16, LANES),
        target_embed,
        target_labels[None],
        name="target_group",
    )
    near = lax.all_to_all(near, "z", 0, 0)
    near, tgt_group = lax.optimization_barrier((near, tgt_group))
    pieces = [near] + [
        lax.ppermute(near, "x", [((i + far) % n_x, i) for i in range(n_x)])
        for far in range(1, n_x)
    ]

    tgt_got = lax.all_to_all(tgt_group, TGT, 0, 0)
    src_group, src_sq = call(
        source_group_kernel,
        (f32(40, LANES), f32(1, ROWS)),
        source_embed,
        source_labels[None],
        name="source_group",
    )
    stats = call(near_kernel, f32(n_z, 48, LANES), tgt_got, src_group, name="near")
    stats = lax.all_to_all(stats, "z", 0, 0)
    stats = call(
        functools.partial(middle_kernel, part * n_x), f32(n_x, 72, LANES), stats, name="middle"
    )
    stats = lax.all_to_all(stats, "x", 0, 0)
    label_cost, xa = call(
        functools.partial(label_kernel, part),
        (f32(CLASSES, CLASSES), jax.ShapeDtypeStruct((16, ROWS), jnp.bfloat16)),
        stats,
        src_sq,
        source_labels[None],
        name="label",
    )

    tall = pltpu.VMEM((ROWS, LANES), jnp.float32)
    wide = pltpu.VMEM((BLK, 8, BLOCK), jnp.float32)
    log_src = math.log2(ROWS * n_src)
    log_tgt = math.log2(ROWS * n_tgt)
    tiles, sent = pl.pallas_call(
        functools.partial(cost_kernel, n_x),
        out_shape=(f32(MAXP, BLOCK, BLOCK), f32(n_tgt, CHUNKS, LANES)),
        in_specs=[smem()] * 3 + [vmem()] * (3 + n_x),
        out_specs=(vmem(), vmem()),
        scratch_shapes=[
            pltpu.VMEM((WIDTH, ROWS), jnp.bfloat16),
            pltpu.VMEM((16, ROWS), jnp.bfloat16),
            tall,
            tall,
        ],
        compiler_params=params(),
        name="cost_rows",
    )(
        pairs,
        count,
        lax.axis_index("x").reshape(1),
        xa,
        source_embed.T,
        *pieces,
        target_labels[None],
    )

    def columns(got):
        return pl.pallas_call(
            functools.partial(col_kernel, log_tgt),
            out_shape=(f32(n_src, CHUNKS, LANES), f32(CHUNKS, LANES)),
            in_specs=[smem(), smem(), vmem(), vmem()],
            out_specs=(vmem(), vmem()),
            scratch_shapes=[tall, wide, wide],
            compiler_params=params(),
            name="columns",
        )(pairs, count, tiles, got)

    def rows(got):
        return pl.pallas_call(
            functools.partial(row_kernel, log_src),
            out_shape=f32(n_tgt, CHUNKS, LANES),
            in_specs=[smem(), smem(), vmem(), vmem()],
            out_specs=vmem(),
            scratch_shapes=[pltpu.VMEM((CHUNKS, LANES), jnp.float32), tall, tall],
            compiler_params=params(),
            name="rows",
        )(pairs, count, tiles, got)

    sent, _ = columns(lax.all_to_all(sent, TGT, 0, 0))
    sent = rows(lax.all_to_all(sent, SRC, 0, 0))
    sent, src_pot = columns(lax.all_to_all(sent, TGT, 0, 0))
    tgt_pot = pl.pallas_call(
        functools.partial(last_kernel, log_src),
        out_shape=f32(CHUNKS, LANES),
        in_specs=[vmem()],
        out_specs=vmem(),
        compiler_params=params(),
        name="last",
    )(lax.all_to_all(sent, SRC, 0, 0))
    return (src_pot.reshape(-1), tgt_pot.reshape(-1), label_cost)


def solution(mesh):
    fine = Mesh(np.asarray(mesh.devices).reshape(8, 4, 4, 2), SRC + TGT)
    return jax.shard_map(
        on_device,
        mesh=fine,
        in_specs=(
            P(None, SRC),
            P(SRC, TGT),
            P(SRC),
            P(TGT),
            P(SRC, TGT, None, None),
            P(SRC, TGT),
        ),
        out_specs=(P(SRC), P(TGT), P()),
        check_vma=False,
    )
```

```python
import functools
import math

import jax
import jax.numpy as jnp
import numpy as np
from jax import lax
from jax.experimental import pallas as pl
from jax.experimental.pallas import tpu as pltpu
from jax.sharding import Mesh, PartitionSpec as P

CLASSES = 4
BLOCK = 256
ROWS = 2048
BLK = ROWS // BLOCK
LANES = 128
CHUNKS = ROWS // LANES
MAXP = 24
UNROLL = 4
WIDTH = 512

EPSILON = 0.05
LOWEST = -1e30
LOG2E = 1.0 / math.log(2.0)
TO_LOG2 = LOG2E / EPSILON
TO_POT = EPSILON / LOG2E

SRC = ("z", "x")
TGT = ("y", "c")
VMEM_LIMIT = 24 * 1024 * 1024


def log2(x):
    return jnp.log(x) * LOG2E


def repeated_onehot(labels):
    row_id = lax.broadcasted_iota(jnp.int32, (16, 1), 0)
    return jnp.where(row_id < 12, jnp.where(labels == row_id % CLASSES, 1.0, 0.0), 0.0)


def across(onehot, values):
    return lax.dot_general(
        onehot, values, (((1,), (1,)), ((), ())), preferred_element_type=jnp.float32
    )


def class_group(values, onehot, counts):
    part = lax.broadcasted_iota(jnp.int32, (16, 1), 0) // CLASSES
    wide = values.astype(jnp.float32)
    mean = across(onehot, values) / counts
    hi, mid, lo = three_parts(mean)
    parts = jnp.where(
        part == 0, hi, jnp.where(part == 1, mid, jnp.where(part == 2, lo, 0.0))
    ).astype(jnp.bfloat16)
    center = lax.dot_general(
        parts, onehot, (((0,), (0,)), ((), ())), preferred_element_type=jnp.float32
    )
    centered = wide - center
    hi, mid, lo = three_parts(centered * centered)
    spread = sum(across(onehot, p.astype(jnp.bfloat16)) for p in (hi, mid, lo))
    return jnp.where(part == 0, mean, spread)[:8], wide


def target_group_kernel(embed, labels, out_ref):
    onehot = repeated_onehot(labels[...])
    counts = jnp.maximum(jnp.sum(onehot, axis=1, keepdims=True), 1.0)
    group, _ = class_group(embed[...], onehot.astype(jnp.bfloat16), counts)
    out_ref[...] = jnp.zeros(out_ref.shape, jnp.float32)
    out_ref[0:8, 0 : group.shape[1]] = group
    out_ref[8:16, :] = jnp.broadcast_to(counts[:8], (8, LANES))


def source_group_kernel(embed, labels, out_ref, sq_ref):
    onehot = repeated_onehot(labels[...])
    counts = jnp.maximum(jnp.sum(onehot, axis=1, keepdims=True), 1.0)
    onehot = onehot.astype(jnp.bfloat16)
    sq = jnp.zeros((1, ROWS), jnp.float32)
    for c in range(WIDTH // LANES):
        group, wide = class_group(embed[c * LANES : (c + 1) * LANES, :], onehot, counts)
        out_ref[8 * c : 8 * c + 8, :] = group
        sq = sq + jnp.sum(wide * wide, axis=0, keepdims=True)
    out_ref[32:40, :] = jnp.broadcast_to(counts[:8], (8, LANES))
    sq_ref[...] = sq


def joined_counts(counts):
    total = functools.reduce(jnp.add, counts)
    return total, [c / total for c in counts]


def joined_group(groups, counts, shares):
    row_id = lax.broadcasted_iota(jnp.int32, (8, LANES), 0)
    mean = functools.reduce(jnp.add, [g * w for g, w in zip(groups, shares)])
    between = functools.reduce(
        jnp.add, [(g - mean) * (g - mean) * c for g, c in zip(groups, counts)]
    )
    spread = functools.reduce(jnp.add, groups) + pltpu.roll(between, 4, 0)
    return jnp.where(row_id < CLASSES, mean, spread)


def target_joined(place, pieces, slots):
    n = len(pieces)
    for far, piece in enumerate(pieces):
        slots[lax.rem(place[0] + far, n)] = piece[...]
    counts = [slots[k, 8:16, :] for k in range(n)]
    total, shares = joined_counts(counts)
    return joined_group([slots[k, 0:8, :] for k in range(n)], counts, shares), total


def pair_kernel(place, *args):
    pieces, (out_ref, slots) = args[:-2], args[-2:]
    group, total = target_joined(place, pieces, slots)
    out_ref[0:8, :] = group
    out_ref[8:16, :] = total


def near_kernel(place, *args):
    pieces, (src_group, out_ref, slots) = args[:-3], args[-3:]
    group, total = target_joined(place, pieces, slots)
    row_id = lax.broadcasted_iota(jnp.int32, (8, LANES), 0)
    group = jnp.where(row_id < CLASSES, group, group / total)
    for k in range(out_ref.shape[0]):
        out_ref[k, 0:40, :] = src_group[...]
        out_ref[k, 40:48, :] = group


def source_joined(got):
    peers = got.shape[0]
    counts = [got[k, 32:40, :] for k in range(peers)]
    total, shares = joined_counts(counts)
    groups = [
        joined_group([got[k, 8 * c : 8 * c + 8, :] for k in range(peers)], counts, shares)
        for c in range(WIDTH // LANES)
    ]
    return groups, total


def middle_kernel(width, got, out_ref):
    groups, total = source_joined(got)
    each = LANES // width
    for c in range(WIDTH // LANES):
        tgt = got[each * c, 40:48, :]
        for k in range(1, each):
            tgt = tgt + pltpu.roll(got[each * c + k, 40:48, :], k * width, 1)
        for k in range(out_ref.shape[0]):
            out_ref[k, 8 * c : 8 * c + 8, :] = groups[c]
            out_ref[k, 40 + 8 * c : 48 + 8 * c, :] = tgt
    for k in range(out_ref.shape[0]):
        out_ref[k, 32:40, :] = total


def label_kernel(part, got, src_sq, src_lab, label_ref, xa_ref):
    groups, total = source_joined(got)
    row_id = lax.broadcasted_iota(jnp.int32, (8, LANES), 0)
    lane_id = lax.broadcasted_iota(jnp.int32, (8, LANES), 1)
    sides = ([], [])
    for c, group in enumerate(groups):
        at = slice(40 + 8 * c, 48 + 8 * c)
        tgt = got[0, at, :]
        for k in range(1, got.shape[0]):
            tgt = tgt + pltpu.roll(got[k, at, :], k * part, 1)
        for side, stat in zip(sides, (jnp.where(row_id < CLASSES, group, group / total), tgt)):
            side.append(jnp.where(row_id < CLASSES, stat, jnp.sqrt(stat + 1e-06)))

    def distances(one, other):
        out = jnp.zeros((8, LANES), jnp.float32)
        for k in range(CLASSES):
            far = jnp.zeros((8, LANES), jnp.float32)
            for g, h in zip(one, other):
                gap = g - jnp.where(row_id < CLASSES, h[k : k + 1], h[CLASSES + k : CLASSES + k + 1])
                far = far + gap * gap
            far = far + pltpu.roll(far, 4, 0)
            out = jnp.where(lane_id == k, jnp.sum(far, axis=1, keepdims=True), out)
        return out

    label_ref[...] = distances(*sides)[:CLASSES, :CLASSES]
    by_target = distances(*sides[::-1])
    by_target = jnp.concatenate([by_target, by_target], axis=0)
    row_id = lax.broadcasted_iota(jnp.int32, (16, 1), 0)
    part_id = row_id // CLASSES
    labels = src_lab[...]
    u = jnp.broadcast_to(src_sq[...], (16, ROWS))
    for a in range(CLASSES):
        u = u + jnp.where(labels == a, by_target[:, a : a + 1], 0.0)
    hi, mid, lo = three_parts(-0.5 * u)
    ones = jnp.where(row_id < 15, 1.0, 0.0)
    xa_ref[...] = jnp.where(
        part_id == 0, hi, jnp.where(part_id == 1, mid, jnp.where(part_id == 2, lo, ones))
    ).astype(jnp.bfloat16)


def spread_kernel(x, out_ref, sems):
    copies = [
        pltpu.make_async_copy(x, out_ref.at[k], sems.at[k]) for k in range(out_ref.shape[0])
    ]
    for copy in copies:
        copy.start()
    for copy in copies:
        copy.wait()


def three_parts(v):
    hi = v.astype(jnp.bfloat16).astype(jnp.float32)
    rest = v - hi
    mid = rest.astype(jnp.bfloat16).astype(jnp.float32)
    return hi, mid, rest - mid


def joined_lse(g_ref):
    g = g_ref[...]
    top = jnp.max(g, axis=0)
    return top + log2(jnp.sum(jnp.exp2(g - top[None]), axis=0))


def row_finish(top, total, out_ref):
    lines = []
    for k in range(CHUNKS):
        at = pl.ds(k * LANES, LANES)
        lse = top[at, :] + log2(jnp.sum(total[at, :], axis=1, keepdims=True))
        lines.append(lse.T[0:1, :])
    line = jnp.concatenate(lines, axis=0)
    out_ref[...] = jnp.broadcast_to(line[None], out_ref.shape)


def widen_top(top):
    for k in range(CHUNKS):
        at = pl.ds(k * LANES, LANES)
        top[at, :] = jnp.broadcast_to(jnp.max(top[at, :], axis=1, keepdims=True), (LANES, LANES))


def over_pairs(count, body, unroll):
    def several(step, _):
        for k in range(unroll):
            body(step * unroll + k)
        return 0

    steps = (count[0] + UNROLL - 1) // UNROLL * (UNROLL // unroll)
    lax.fori_loop(0, steps, several, 0)


def block_at(pairs, index):
    row = pl.multiple_of(pairs[2 * index] * BLOCK, BLOCK)
    return row, pairs[2 * index + 1]


def cost_kernel(n_x, pairs, count, place, xa, xt, *args):
    pieces, (tgt_lab, tiles, out_ref, y, ya, top, total) = args[:n_x], args[n_x:]
    row_id = lax.broadcasted_iota(jnp.int32, (16, 1), 0)
    part = row_id // CLASSES
    cls = row_id % CLASSES

    tgt_sq = jnp.zeros((16, ROWS), jnp.float32)
    for far, piece in enumerate(pieces):
        at = lax.rem(place[0] + far, n_x)
        for k in range(piece.shape[0]):
            y[pl.ds(pl.multiple_of((k * n_x + at) * 16, 16), 16), :] = piece[k]
            v = piece[k].astype(jnp.float32)
            tgt_sq = tgt_sq + v * v

    hi, mid, lo = three_parts(-0.5 * jnp.sum(tgt_sq, axis=0, keepdims=True))
    onehot = jnp.where(tgt_lab[...] == cls, 1.0, 0.0)
    ya[...] = jnp.where(
        part < 3,
        onehot,
        jnp.where(cls == 0, hi, jnp.where(cls == 1, mid, jnp.where(cls == 2, lo, 0.0))),
    ).astype(jnp.bfloat16)

    top[...] = jnp.full(top.shape, LOWEST, jnp.float32)
    total[...] = jnp.zeros(total.shape, jnp.float32)

    def build(index):
        row, col = block_at(pairs, index)
        rows = pl.ds(row, BLOCK)
        cols = pl.ds(pl.multiple_of(col * BLOCK, BLOCK), BLOCK)
        cross = jnp.dot(xt[rows, :], y[:, cols], preferred_element_type=jnp.float32)
        extra = lax.dot_general(
            xa[:, rows], ya[:, cols], (((0,), (0,)), ((), ())), preferred_element_type=jnp.float32
        )
        tile = (cross + extra) * (2.0 * TO_LOG2) + jnp.where(index < count[0], 0.0, LOWEST)
        tiles[index] = tile
        top[rows, :] = jnp.maximum(top[rows, :], jnp.maximum(tile[:, :LANES], tile[:, LANES:]))

    over_pairs(count, build, 4)
    widen_top(top)

    def add(index):
        row, _ = block_at(pairs, index)
        rows = pl.ds(row, BLOCK)
        high = top[rows, :]
        left = jnp.exp2(tiles[index, :, :LANES] - high)
        right = jnp.exp2(tiles[index, :, LANES:] - high)
        total[rows, :] = total[rows, :] + (left + right)

    over_pairs(count, add, 4)
    row_finish(top, total, out_ref)


def row_kernel(log_total, pairs, count, tiles, g_ref, out_ref, pot, top, total):
    pot[...] = log_total - joined_lse(g_ref)
    top[...] = jnp.full(top.shape, LOWEST, jnp.float32)
    total[...] = jnp.zeros(total.shape, jnp.float32)

    def scores(index, col):
        left = tiles[index, :, :LANES] + pot[pl.ds(2 * col, 1), :]
        right = tiles[index, :, LANES:] + pot[pl.ds(2 * col + 1, 1), :]
        return left, right

    def highest(index):
        row, col = block_at(pairs, index)
        rows = pl.ds(row, BLOCK)
        left, right = scores(index, col)
        top[rows, :] = jnp.maximum(top[rows, :], jnp.maximum(left, right))

    over_pairs(count, highest, 4)
    widen_top(top)

    def add(index):
        row, col = block_at(pairs, index)
        rows = pl.ds(row, BLOCK)
        left, right = scores(index, col)
        high = top[rows, :]
        total[rows, :] = total[rows, :] + (jnp.exp2(left - high) + jnp.exp2(right - high))

    over_pairs(count, add, 4)
    row_finish(top, total, out_ref)


def col_kernel(log_total, pairs, count, tiles, g_ref, out_ref, pot_ref, pot, top, total):
    line = log_total - joined_lse(g_ref)
    pot_ref[...] = line * TO_POT
    for k in range(CHUNKS):
        pot[pl.ds(k * LANES, LANES), :] = jnp.broadcast_to(line[k : k + 1, :], (LANES, LANES)).T
    top[...] = jnp.full(top.shape, LOWEST, jnp.float32)
    total[...] = jnp.zeros(total.shape, jnp.float32)

    def scores(index, row):
        rows = pl.ds(row, BLOCK)
        high = pot[rows, :]
        tile = tiles[index]
        return tile + jnp.concatenate([high, high], axis=1)

    def highest(index):
        row, col = block_at(pairs, index)
        score = scores(index, row)
        top[col] = jnp.maximum(top[col], jnp.max(score.reshape(BLOCK // 8, 8, BLOCK), axis=0))

    over_pairs(count, highest, 4)
    for k in range(BLK):
        top[k] = jnp.broadcast_to(jnp.max(top[k], axis=0, keepdims=True), (8, BLOCK))

    def add(index):
        row, col = block_at(pairs, index)
        score = scores(index, row).reshape(BLOCK // 8, 8, BLOCK)
        total[col] = total[col] + jnp.sum(jnp.exp2(score - top[col][None]), axis=0)

    over_pairs(count, add, 4)
    lines = []
    for k in range(BLK):
        lse = top[k][0:1] + log2(jnp.sum(total[k], axis=0, keepdims=True))
        lines += [lse[:, :LANES], lse[:, LANES:]]
    out = jnp.concatenate(lines, axis=0)
    out_ref[...] = jnp.broadcast_to(out[None], out_ref.shape)


def last_kernel(log_total, g_ref, pot_ref):
    pot_ref[...] = (log_total - joined_lse(g_ref)) * TO_POT


def smem():
    return pl.BlockSpec(memory_space=pltpu.SMEM)


def vmem():
    return pl.BlockSpec(memory_space=pltpu.VMEM)


def f32(*shape):
    return jax.ShapeDtypeStruct(shape, jnp.float32)


def params():
    return pltpu.CompilerParams(vmem_limit_bytes=VMEM_LIMIT)


def on_device(source_embed, target_embed, source_labels, target_labels, pair_blocks, pair_count):
    pairs = pair_blocks.reshape(-1)
    count = pair_count.reshape(-1)
    n_src, n_tgt = lax.axis_size(SRC), lax.axis_size(TGT)

    def call(kernel, out_shape, *args, name):
        return pl.pallas_call(
            kernel,
            out_shape=out_shape,
            in_specs=[vmem()] * len(args),
            out_specs=jax.tree.map(lambda _: vmem(), out_shape),
            compiler_params=params(),
            name=name,
        )(*args)

    n_x, n_z = lax.axis_size("x"), lax.axis_size("z")
    part = target_embed.shape[0]
    near = pl.pallas_call(
        spread_kernel,
        out_shape=jax.ShapeDtypeStruct((n_z,) + target_embed.shape, jnp.bfloat16),
        in_specs=[pl.BlockSpec(memory_space=pl.ANY)],
        out_specs=pl.BlockSpec(memory_space=pl.ANY),
        scratch_shapes=[pltpu.SemaphoreType.DMA((n_z,))],
        compiler_params=params(),
        name="spread",
    )(target_embed)
    near = lax.all_to_all(near, "z", 0, 0)

    def around(x, axis):
        n = lax.axis_size(axis)
        return [x] + [
            lax.ppermute(x, axis, [((i + far) % n, i) for i in range(n)]) for far in range(1, n)
        ]

    def join_targets(kernel, out_shape, x, axis, *more, name):
        pieces = around(x, axis)
        return pl.pallas_call(
            kernel,
            out_shape=out_shape,
            in_specs=[smem()] + [vmem()] * (len(pieces) + len(more)),
            out_specs=vmem(),
            scratch_shapes=[pltpu.VMEM((len(pieces), 16, LANES), jnp.float32)],
            compiler_params=params(),
            name=name,
        )(lax.axis_index(axis).reshape(1), *pieces, *more)

    tgt_group = call(
        target_group_kernel,
        f32(16, LANES),
        target_embed,
        target_labels[None],
        name="target_group",
    )
    tgt_group = join_targets(pair_kernel, f32(16, LANES), tgt_group, "c", name="pair")
    src_group, src_sq = call(
        source_group_kernel,
        (f32(40, LANES), f32(1, ROWS)),
        source_embed,
        source_labels[None],
        name="source_group",
    )
    stats = join_targets(
        near_kernel, f32(n_z, 48, LANES), tgt_group, "y", src_group, name="near"
    )
    near, stats, source_tall = lax.optimization_barrier((near, stats, source_embed.T))

    pieces = around(near, "x")
    stats = lax.all_to_all(stats, "z", 0, 0)
    stats = call(
        functools.partial(middle_kernel, part * n_x), f32(n_x, 72, LANES), stats, name="middle"
    )
    stats = lax.all_to_all(stats, "x", 0, 0)
    label_cost, xa = call(
        functools.partial(label_kernel, part),
        (f32(CLASSES, CLASSES), jax.ShapeDtypeStruct((16, ROWS), jnp.bfloat16)),
        stats,
        src_sq,
        source_labels[None],
        name="label",
    )

    tall = pltpu.VMEM((ROWS, LANES), jnp.float32)
    wide = pltpu.VMEM((BLK, 8, BLOCK), jnp.float32)
    log_src = math.log2(ROWS * n_src)
    log_tgt = math.log2(ROWS * n_tgt)
    tiles, sent = pl.pallas_call(
        functools.partial(cost_kernel, n_x),
        out_shape=(f32(MAXP, BLOCK, BLOCK), f32(n_tgt, CHUNKS, LANES)),
        in_specs=[smem()] * 3 + [vmem()] * (3 + n_x),
        out_specs=(vmem(), vmem()),
        scratch_shapes=[
            pltpu.VMEM((WIDTH, ROWS), jnp.bfloat16),
            pltpu.VMEM((16, ROWS), jnp.bfloat16),
            tall,
            tall,
        ],
        compiler_params=params(),
        name="cost_rows",
    )(
        pairs,
        count,
        lax.axis_index("x").reshape(1),
        xa,
        source_tall,
        *pieces,
        target_labels[None],
    )

    def columns(got):
        return pl.pallas_call(
            functools.partial(col_kernel, log_tgt),
            out_shape=(f32(n_src, CHUNKS, LANES), f32(CHUNKS, LANES)),
            in_specs=[smem(), smem(), vmem(), vmem()],
            out_specs=(vmem(), vmem()),
            scratch_shapes=[tall, wide, wide],
            compiler_params=params(),
            name="columns",
        )(pairs, count, tiles, got)

    def rows(got):
        return pl.pallas_call(
            functools.partial(row_kernel, log_src),
            out_shape=f32(n_tgt, CHUNKS, LANES),
            in_specs=[smem(), smem(), vmem(), vmem()],
            out_specs=vmem(),
            scratch_shapes=[pltpu.VMEM((CHUNKS, LANES), jnp.float32), tall, tall],
            compiler_params=params(),
            name="rows",
        )(pairs, count, tiles, got)

    sent, _ = columns(lax.all_to_all(sent, TGT, 0, 0))
    sent = rows(lax.all_to_all(sent, SRC, 0, 0))
    sent, src_pot = columns(lax.all_to_all(sent, TGT, 0, 0))
    tgt_pot = pl.pallas_call(
        functools.partial(last_kernel, log_src),
        out_shape=f32(CHUNKS, LANES),
        in_specs=[vmem()],
        out_specs=vmem(),
        compiler_params=params(),
        name="last",
    )(lax.all_to_all(sent, SRC, 0, 0))
    return (src_pot.reshape(-1), tgt_pot.reshape(-1), label_cost)


def solution(mesh):
    fine = Mesh(np.asarray(mesh.devices).reshape(8, 4, 4, 2), SRC + TGT)
    return jax.shard_map(
        on_device,
        mesh=fine,
        in_specs=(
            P(None, SRC),
            P(SRC, TGT),
            P(SRC),
            P(TGT),
            P(SRC, TGT, None, None),
            P(SRC, TGT),
        ),
        out_specs=(P(SRC), P(TGT), P()),
        check_vma=False,
    )
```

```python
import functools
import math

import jax
import jax.numpy as jnp
import numpy as np
from jax import lax
from jax.experimental import pallas as pl
from jax.experimental.pallas import tpu as pltpu
from jax.sharding import Mesh, PartitionSpec as P

CLASSES = 4
BLOCK = 256
ROWS = 2048
BLK = ROWS // BLOCK
LANES = 128
CHUNKS = ROWS // LANES
MAXP = 24
UNROLL = 4
WIDTH = 512

EPSILON = 0.05
LOWEST = -1e30
LOG2E = 1.0 / math.log(2.0)
TO_LOG2 = LOG2E / EPSILON
TO_POT = EPSILON / LOG2E

SRC = ("z", "x")
TGT = ("y", "c")
VMEM_LIMIT = 24 * 1024 * 1024


def log2(x):
    return jnp.log(x) * LOG2E


def repeated_onehot(labels):
    row_id = lax.broadcasted_iota(jnp.int32, (16, 1), 0)
    return jnp.where(row_id < 12, jnp.where(labels == row_id % CLASSES, 1.0, 0.0), 0.0)


def across(onehot, values):
    return lax.dot_general(
        onehot, values, (((1,), (1,)), ((), ())), preferred_element_type=jnp.float32
    )


def class_group(values, onehot, counts):
    part = lax.broadcasted_iota(jnp.int32, (16, 1), 0) // CLASSES
    wide = values.astype(jnp.float32)
    mean = across(onehot, values) / counts
    hi, mid, lo = three_parts(mean)
    parts = jnp.where(
        part == 0, hi, jnp.where(part == 1, mid, jnp.where(part == 2, lo, 0.0))
    ).astype(jnp.bfloat16)
    center = lax.dot_general(
        parts, onehot, (((0,), (0,)), ((), ())), preferred_element_type=jnp.float32
    )
    centered = wide - center
    hi, mid, lo = three_parts(centered * centered)
    spread = sum(across(onehot, p.astype(jnp.bfloat16)) for p in (hi, mid, lo))
    return jnp.where(part == 0, mean, spread)[:8], wide


def target_group_kernel(embed, labels, out_ref):
    onehot = repeated_onehot(labels[...])
    counts = jnp.maximum(jnp.sum(onehot, axis=1, keepdims=True), 1.0)
    group, _ = class_group(embed[...], onehot.astype(jnp.bfloat16), counts)
    out_ref[...] = jnp.zeros(out_ref.shape, jnp.float32)
    out_ref[0:8, 0 : group.shape[1]] = group
    out_ref[8:16, :] = jnp.broadcast_to(counts[:8], (8, LANES))


def source_group_kernel(embed, labels, out_ref, sq_ref):
    onehot = repeated_onehot(labels[...])
    counts = jnp.maximum(jnp.sum(onehot, axis=1, keepdims=True), 1.0)
    onehot = onehot.astype(jnp.bfloat16)
    sq = jnp.zeros((1, ROWS), jnp.float32)
    for c in range(WIDTH // LANES):
        group, wide = class_group(embed[c * LANES : (c + 1) * LANES, :], onehot, counts)
        out_ref[8 * c : 8 * c + 8, :] = group
        sq = sq + jnp.sum(wide * wide, axis=0, keepdims=True)
    out_ref[32:40, :] = jnp.broadcast_to(counts[:8], (8, LANES))
    sq_ref[...] = sq


def joined_counts(counts):
    total = functools.reduce(jnp.add, counts)
    return total, [c / total for c in counts]


def joined_group(groups, counts, shares):
    row_id = lax.broadcasted_iota(jnp.int32, (8, LANES), 0)
    mean = functools.reduce(jnp.add, [g * w for g, w in zip(groups, shares)])
    between = functools.reduce(
        jnp.add, [(g - mean) * (g - mean) * c for g, c in zip(groups, counts)]
    )
    spread = functools.reduce(jnp.add, groups) + pltpu.roll(between, 4, 0)
    return jnp.where(row_id < CLASSES, mean, spread)


def target_joined(place, pieces, slots):
    n = len(pieces)
    for far, piece in enumerate(pieces):
        slots[lax.rem(place[0] + far, n)] = piece[...]
    counts = [slots[k, 8:16, :] for k in range(n)]
    total, shares = joined_counts(counts)
    return joined_group([slots[k, 0:8, :] for k in range(n)], counts, shares), total


def pair_kernel(place, *args):
    pieces, (out_ref, slots) = args[:-2], args[-2:]
    group, total = target_joined(place, pieces, slots)
    out_ref[0:8, :] = group
    out_ref[8:16, :] = total


def lanes_of(shape):
    return lax.broadcasted_iota(jnp.int32, shape, len(shape) - 1)


def near_kernel(place, *args):
    pieces, (src_group, out_ref, slots) = args[:-3], args[-3:]
    group, total = target_joined(place, pieces, slots)
    row_id = lax.broadcasted_iota(jnp.int32, (8, LANES), 0)
    group = jnp.where(row_id < CLASSES, group, group / total)
    out_ref[0:32, :] = src_group[0:32, :]
    out_ref[32:40, :] = jnp.where(lanes_of((8, LANES)) < LANES // 2, group, src_group[32:40, :])


def source_joined(got):
    peers = got.shape[0]
    half = LANES // 2
    lower = lanes_of((8, LANES)) < half
    last = [got[k, 32:40, :] for k in range(peers)]
    targets = [jnp.where(lower, g, 0.0) for g in last]
    counts = [jnp.where(lower, pltpu.roll(g, half, 1), g) for g in last]
    total, shares = joined_counts(counts)
    groups = [
        joined_group([got[k, 8 * c : 8 * c + 8, :] for k in range(peers)], counts, shares)
        for c in range(WIDTH // LANES)
    ]
    return groups, total, targets


def side_by_side(targets, width):
    out = targets[0]
    for k, target in enumerate(targets[1:]):
        out = out + pltpu.roll(target, (k + 1) * width, 1)
    return out


def middle_kernel(part, place, *args):
    pieces, (out_ref, slots) = args[:-2], args[-2:]
    for far, piece in enumerate(pieces):
        slots[lax.rem(place[0] + far, len(pieces))] = piece[...]
    groups, total, targets = source_joined(slots)
    target = side_by_side(targets, part)
    target = jnp.where(lanes_of((8, LANES)) < LANES // 2, target, total)
    for k in range(out_ref.shape[0]):
        for c, group in enumerate(groups):
            out_ref[k, 8 * c : 8 * c + 8, :] = group
        out_ref[k, 32:40, :] = target


def label_kernel(width, got, src_sq, src_lab, label_ref, xa_ref):
    groups, total, targets = source_joined(got)
    row_id = lax.broadcasted_iota(jnp.int32, (8, LANES), 0)
    lane_id = lanes_of((8, LANES))
    each = LANES // width
    sides = ([], [])
    for c, group in enumerate(groups):
        tgt = side_by_side(targets[each * c : each * c + each], width)
        for side, stat in zip(sides, (jnp.where(row_id < CLASSES, group, group / total), tgt)):
            side.append(jnp.where(row_id < CLASSES, stat, jnp.sqrt(stat + 1e-06)))

    def distances(one, other):
        out = jnp.zeros((8, LANES), jnp.float32)
        for k in range(CLASSES):
            far = jnp.zeros((8, LANES), jnp.float32)
            for g, h in zip(one, other):
                gap = g - jnp.where(row_id < CLASSES, h[k : k + 1], h[CLASSES + k : CLASSES + k + 1])
                far = far + gap * gap
            far = far + pltpu.roll(far, 4, 0)
            out = jnp.where(lane_id == k, jnp.sum(far, axis=1, keepdims=True), out)
        return out

    label_ref[...] = distances(*sides)[:CLASSES, :CLASSES]
    by_target = distances(*sides[::-1])
    by_target = jnp.concatenate([by_target, by_target], axis=0)
    row_id = lax.broadcasted_iota(jnp.int32, (16, 1), 0)
    part_id = row_id // CLASSES
    labels = src_lab[...]
    u = jnp.broadcast_to(src_sq[...], (16, ROWS))
    for a in range(CLASSES):
        u = u + jnp.where(labels == a, by_target[:, a : a + 1], 0.0)
    hi, mid, lo = three_parts(-0.5 * u)
    ones = jnp.where(row_id < 15, 1.0, 0.0)
    xa_ref[...] = jnp.where(
        part_id == 0, hi, jnp.where(part_id == 1, mid, jnp.where(part_id == 2, lo, ones))
    ).astype(jnp.bfloat16)


def spread_kernel(x, out_ref, sems):
    copies = [
        pltpu.make_async_copy(x, out_ref.at[k], sems.at[k]) for k in range(out_ref.shape[0])
    ]
    for copy in copies:
        copy.start()
    for copy in copies:
        copy.wait()


def three_parts(v):
    hi = v.astype(jnp.bfloat16).astype(jnp.float32)
    rest = v - hi
    mid = rest.astype(jnp.bfloat16).astype(jnp.float32)
    return hi, mid, rest - mid


def joined_lse(g_ref):
    g = g_ref[...]
    top = jnp.max(g, axis=0)
    return top + log2(jnp.sum(jnp.exp2(g - top[None]), axis=0))


def row_finish(top, total, out_ref):
    lines = []
    for k in range(CHUNKS):
        at = pl.ds(k * LANES, LANES)
        lse = top[at, :] + log2(jnp.sum(total[at, :], axis=1, keepdims=True))
        lines.append(lse.T[0:1, :])
    line = jnp.concatenate(lines, axis=0)
    out_ref[...] = jnp.broadcast_to(line[None], out_ref.shape)


def widen_top(top):
    for k in range(CHUNKS):
        at = pl.ds(k * LANES, LANES)
        top[at, :] = jnp.broadcast_to(jnp.max(top[at, :], axis=1, keepdims=True), (LANES, LANES))


def over_pairs(count, body, unroll):
    def several(step, _):
        for k in range(unroll):
            body(step * unroll + k)
        return 0

    steps = (count[0] + UNROLL - 1) // UNROLL * (UNROLL // unroll)
    lax.fori_loop(0, steps, several, 0)


def block_at(pairs, index):
    row = pl.multiple_of(pairs[2 * index] * BLOCK, BLOCK)
    return row, pairs[2 * index + 1]


def cost_kernel(n_x, pairs, count, place, xa, xt, *args):
    pieces, (tgt_lab, tiles, out_ref, y, ya, top, total) = args[:n_x], args[n_x:]
    row_id = lax.broadcasted_iota(jnp.int32, (16, 1), 0)
    part = row_id // CLASSES
    cls = row_id % CLASSES

    tgt_sq = jnp.zeros((16, ROWS), jnp.float32)
    for far, piece in enumerate(pieces):
        at = lax.rem(place[0] + far, n_x)
        for k in range(piece.shape[0]):
            y[pl.ds(pl.multiple_of((k * n_x + at) * 16, 16), 16), :] = piece[k]
            v = piece[k].astype(jnp.float32)
            tgt_sq = tgt_sq + v * v

    hi, mid, lo = three_parts(-0.5 * jnp.sum(tgt_sq, axis=0, keepdims=True))
    onehot = jnp.where(tgt_lab[...] == cls, 1.0, 0.0)
    ya[...] = jnp.where(
        part < 3,
        onehot,
        jnp.where(cls == 0, hi, jnp.where(cls == 1, mid, jnp.where(cls == 2, lo, 0.0))),
    ).astype(jnp.bfloat16)

    top[...] = jnp.full(top.shape, LOWEST, jnp.float32)
    total[...] = jnp.zeros(total.shape, jnp.float32)

    def build(index):
        row, col = block_at(pairs, index)
        rows = pl.ds(row, BLOCK)
        cols = pl.ds(pl.multiple_of(col * BLOCK, BLOCK), BLOCK)
        cross = jnp.dot(xt[rows, :], y[:, cols], preferred_element_type=jnp.float32)
        extra = lax.dot_general(
            xa[:, rows], ya[:, cols], (((0,), (0,)), ((), ())), preferred_element_type=jnp.float32
        )
        tile = (cross + extra) * (2.0 * TO_LOG2) + jnp.where(index < count[0], 0.0, LOWEST)
        tiles[index] = tile
        top[rows, :] = jnp.maximum(top[rows, :], jnp.maximum(tile[:, :LANES], tile[:, LANES:]))

    over_pairs(count, build, 4)
    widen_top(top)

    def add(index):
        row, _ = block_at(pairs, index)
        rows = pl.ds(row, BLOCK)
        high = top[rows, :]
        left = jnp.exp2(tiles[index, :, :LANES] - high)
        right = jnp.exp2(tiles[index, :, LANES:] - high)
        total[rows, :] = total[rows, :] + (left + right)

    over_pairs(count, add, 4)
    row_finish(top, total, out_ref)


def row_kernel(log_total, pairs, count, tiles, g_ref, out_ref, pot, top, total):
    pot[...] = log_total - joined_lse(g_ref)
    top[...] = jnp.full(top.shape, LOWEST, jnp.float32)
    total[...] = jnp.zeros(total.shape, jnp.float32)

    def scores(index, col):
        left = tiles[index, :, :LANES] + pot[pl.ds(2 * col, 1), :]
        right = tiles[index, :, LANES:] + pot[pl.ds(2 * col + 1, 1), :]
        return left, right

    def highest(index):
        row, col = block_at(pairs, index)
        rows = pl.ds(row, BLOCK)
        left, right = scores(index, col)
        top[rows, :] = jnp.maximum(top[rows, :], jnp.maximum(left, right))

    over_pairs(count, highest, 4)
    widen_top(top)

    def add(index):
        row, col = block_at(pairs, index)
        rows = pl.ds(row, BLOCK)
        left, right = scores(index, col)
        high = top[rows, :]
        total[rows, :] = total[rows, :] + (jnp.exp2(left - high) + jnp.exp2(right - high))

    over_pairs(count, add, 4)
    row_finish(top, total, out_ref)


def col_kernel(log_total, pairs, count, tiles, g_ref, out_ref, pot_ref, pot, top, total):
    line = log_total - joined_lse(g_ref)
    pot_ref[...] = line * TO_POT
    for k in range(CHUNKS):
        pot[pl.ds(k * LANES, LANES), :] = jnp.broadcast_to(line[k : k + 1, :], (LANES, LANES)).T
    top[...] = jnp.full(top.shape, LOWEST, jnp.float32)
    total[...] = jnp.zeros(total.shape, jnp.float32)

    def scores(index, row):
        rows = pl.ds(row, BLOCK)
        high = pot[rows, :]
        tile = tiles[index]
        return tile + jnp.concatenate([high, high], axis=1)

    def highest(index):
        row, col = block_at(pairs, index)
        score = scores(index, row)
        top[col] = jnp.maximum(top[col], jnp.max(score.reshape(BLOCK // 8, 8, BLOCK), axis=0))

    over_pairs(count, highest, 4)
    for k in range(BLK):
        top[k] = jnp.broadcast_to(jnp.max(top[k], axis=0, keepdims=True), (8, BLOCK))

    def add(index):
        row, col = block_at(pairs, index)
        score = scores(index, row).reshape(BLOCK // 8, 8, BLOCK)
        total[col] = total[col] + jnp.sum(jnp.exp2(score - top[col][None]), axis=0)

    over_pairs(count, add, 4)
    lines = []
    for k in range(BLK):
        lse = top[k][0:1] + log2(jnp.sum(total[k], axis=0, keepdims=True))
        lines += [lse[:, :LANES], lse[:, LANES:]]
    out = jnp.concatenate(lines, axis=0)
    out_ref[...] = jnp.broadcast_to(out[None], out_ref.shape)


def last_kernel(log_total, g_ref, pot_ref):
    pot_ref[...] = (log_total - joined_lse(g_ref)) * TO_POT


def smem():
    return pl.BlockSpec(memory_space=pltpu.SMEM)


def vmem():
    return pl.BlockSpec(memory_space=pltpu.VMEM)


def f32(*shape):
    return jax.ShapeDtypeStruct(shape, jnp.float32)


def params():
    return pltpu.CompilerParams(vmem_limit_bytes=VMEM_LIMIT)


def on_device(source_embed, target_embed, source_labels, target_labels, pair_blocks, pair_count):
    pairs = pair_blocks.reshape(-1)
    count = pair_count.reshape(-1)
    n_src, n_tgt = lax.axis_size(SRC), lax.axis_size(TGT)

    def call(kernel, out_shape, *args, name):
        return pl.pallas_call(
            kernel,
            out_shape=out_shape,
            in_specs=[vmem()] * len(args),
            out_specs=jax.tree.map(lambda _: vmem(), out_shape),
            compiler_params=params(),
            name=name,
        )(*args)

    n_x, n_z = lax.axis_size("x"), lax.axis_size("z")
    part = target_embed.shape[0]
    near = pl.pallas_call(
        spread_kernel,
        out_shape=jax.ShapeDtypeStruct((n_z,) + target_embed.shape, jnp.bfloat16),
        in_specs=[pl.BlockSpec(memory_space=pl.ANY)],
        out_specs=pl.BlockSpec(memory_space=pl.ANY),
        scratch_shapes=[pltpu.SemaphoreType.DMA((n_z,))],
        compiler_params=params(),
        name="spread",
    )(target_embed)
    near = lax.all_to_all(near, "z", 0, 0)

    def around(x, axis):
        n = lax.axis_size(axis)
        return [x] + [
            lax.ppermute(x, axis, [((i + far) % n, i) for i in range(n)]) for far in range(1, n)
        ]

    def join_around(kernel, out_shape, x, axis, *more, name):
        pieces = around(x, axis)
        return pl.pallas_call(
            kernel,
            out_shape=out_shape,
            in_specs=[smem()] + [vmem()] * (len(pieces) + len(more)),
            out_specs=vmem(),
            scratch_shapes=[pltpu.VMEM((len(pieces),) + x.shape, jnp.float32)],
            compiler_params=params(),
            name=name,
        )(lax.axis_index(axis).reshape(1), *pieces, *more)

    tgt_group = call(
        target_group_kernel,
        f32(16, LANES),
        target_embed,
        target_labels[None],
        name="target_group",
    )
    tgt_group = join_around(pair_kernel, f32(16, LANES), tgt_group, "c", name="pair")
    src_group, src_sq = call(
        source_group_kernel,
        (f32(40, LANES), f32(1, ROWS)),
        source_embed,
        source_labels[None],
        name="source_group",
    )
    stats = join_around(near_kernel, f32(40, LANES), tgt_group, "y", src_group, name="near")
    near, stats = lax.optimization_barrier((near, stats))

    pieces = around(near, "x")
    stats = join_around(
        functools.partial(middle_kernel, part), f32(n_z, 40, LANES), stats, "x", name="middle"
    )
    stats = lax.all_to_all(stats, "z", 0, 0)
    label_cost, xa = call(
        functools.partial(label_kernel, part * n_x),
        (f32(CLASSES, CLASSES), jax.ShapeDtypeStruct((16, ROWS), jnp.bfloat16)),
        stats,
        src_sq,
        source_labels[None],
        name="label",
    )

    tall = pltpu.VMEM((ROWS, LANES), jnp.float32)
    wide = pltpu.VMEM((BLK, 8, BLOCK), jnp.float32)
    log_src = math.log2(ROWS * n_src)
    log_tgt = math.log2(ROWS * n_tgt)
    tiles, sent = pl.pallas_call(
        functools.partial(cost_kernel, n_x),
        out_shape=(f32(MAXP, BLOCK, BLOCK), f32(n_tgt, CHUNKS, LANES)),
        in_specs=[smem()] * 3 + [vmem()] * (3 + n_x),
        out_specs=(vmem(), vmem()),
        scratch_shapes=[
            pltpu.VMEM((WIDTH, ROWS), jnp.bfloat16),
            pltpu.VMEM((16, ROWS), jnp.bfloat16),
            tall,
            tall,
        ],
        compiler_params=params(),
        name="cost_rows",
    )(
        pairs,
        count,
        lax.axis_index("x").reshape(1),
        xa,
        source_embed.T,
        *pieces,
        target_labels[None],
    )

    def columns(got):
        return pl.pallas_call(
            functools.partial(col_kernel, log_tgt),
            out_shape=(f32(n_src, CHUNKS, LANES), f32(CHUNKS, LANES)),
            in_specs=[smem(), smem(), vmem(), vmem()],
            out_specs=(vmem(), vmem()),
            scratch_shapes=[tall, wide, wide],
            compiler_params=params(),
            name="columns",
        )(pairs, count, tiles, got)

    def rows(got):
        return pl.pallas_call(
            functools.partial(row_kernel, log_src),
            out_shape=f32(n_tgt, CHUNKS, LANES),
            in_specs=[smem(), smem(), vmem(), vmem()],
            out_specs=vmem(),
            scratch_shapes=[pltpu.VMEM((CHUNKS, LANES), jnp.float32), tall, tall],
            compiler_params=params(),
            name="rows",
        )(pairs, count, tiles, got)

    sent, _ = columns(lax.all_to_all(sent, TGT, 0, 0))
    sent = rows(lax.all_to_all(sent, SRC, 0, 0))
    sent, src_pot = columns(lax.all_to_all(sent, TGT, 0, 0))
    tgt_pot = pl.pallas_call(
        functools.partial(last_kernel, log_src),
        out_shape=f32(CHUNKS, LANES),
        in_specs=[vmem()],
        out_specs=vmem(),
        compiler_params=params(),
        name="last",
    )(lax.all_to_all(sent, SRC, 0, 0))
    return (src_pot.reshape(-1), tgt_pot.reshape(-1), label_cost)


def solution(mesh):
    fine = Mesh(np.asarray(mesh.devices).reshape(8, 4, 4, 2), SRC + TGT)
    return jax.shard_map(
        on_device,
        mesh=fine,
        in_specs=(
            P(None, SRC),
            P(SRC, TGT),
            P(SRC),
            P(TGT),
            P(SRC, TGT, None, None),
            P(SRC, TGT),
        ),
        out_specs=(P(SRC), P(TGT), P()),
        check_vma=False,
    )
```

```python
import functools
import math

import jax
import jax.numpy as jnp
import numpy as np
from jax import lax
from jax.experimental import pallas as pl
from jax.experimental.pallas import tpu as pltpu
from jax.sharding import Mesh, PartitionSpec as P

CLASSES = 4
BLOCK = 256
ROWS = 2048
BLK = ROWS // BLOCK
LANES = 128
CHUNKS = ROWS // LANES
MAXP = 24
UNROLL = 4
WIDTH = 512

EPSILON = 0.05
LOWEST = -1e30
LOG2E = 1.0 / math.log(2.0)
TO_LOG2 = LOG2E / EPSILON
TO_POT = EPSILON / LOG2E

SRC = ("z", "x")
TGT = ("y", "c")
VMEM_LIMIT = 24 * 1024 * 1024


def log2(x):
    return jnp.log(x) * LOG2E


def repeated_onehot(labels):
    row_id = lax.broadcasted_iota(jnp.int32, (16, 1), 0)
    return jnp.where(row_id < 12, jnp.where(labels == row_id % CLASSES, 1.0, 0.0), 0.0)


def across(onehot, values):
    return lax.dot_general(
        onehot, values, (((1,), (1,)), ((), ())), preferred_element_type=jnp.float32
    )


def class_group(values, onehot, counts):
    part = lax.broadcasted_iota(jnp.int32, (16, 1), 0) // CLASSES
    wide = values.astype(jnp.float32)
    mean = across(onehot, values) / counts
    hi, mid, lo = three_parts(mean)
    parts = jnp.where(
        part == 0, hi, jnp.where(part == 1, mid, jnp.where(part == 2, lo, 0.0))
    ).astype(jnp.bfloat16)
    center = lax.dot_general(
        parts, onehot, (((0,), (0,)), ((), ())), preferred_element_type=jnp.float32
    )
    centered = wide - center
    hi, mid, lo = three_parts(centered * centered)
    spread = sum(across(onehot, p.astype(jnp.bfloat16)) for p in (hi, mid, lo))
    return jnp.where(part == 0, mean, spread)[:8], wide


def first_kernel(embed, labels, near_ref, out_ref, held, held_labels, sems, out_sems):
    fetch = [
        pltpu.make_async_copy(embed, held, sems.at[0]),
        pltpu.make_async_copy(labels, held_labels, sems.at[1]),
    ]
    for copy in fetch:
        copy.start()
    for copy in fetch:
        copy.wait()
    copies = [
        pltpu.make_async_copy(held, near_ref.at[k], out_sems.at[k])
        for k in range(near_ref.shape[0])
    ]
    for copy in copies:
        copy.start()
    onehot = repeated_onehot(held_labels[...])
    counts = jnp.maximum(jnp.sum(onehot, axis=1, keepdims=True), 1.0)
    group, _ = class_group(held[...], onehot.astype(jnp.bfloat16), counts)
    out_ref[...] = jnp.zeros(out_ref.shape, jnp.float32)
    out_ref[0:8, 0 : group.shape[1]] = group
    out_ref[8:16, :] = jnp.broadcast_to(counts[:8], (8, LANES))
    for copy in copies:
        copy.wait()


def source_group_kernel(embed, labels, out_ref, sq_ref, held, held_labels, sems):
    chunks = WIDTH // LANES
    rows = [pl.ds(c * LANES, LANES) for c in range(chunks)]
    fetch = [pltpu.make_async_copy(labels, held_labels, sems.at[chunks])] + [
        pltpu.make_async_copy(embed.at[rows[c], :], held.at[rows[c], :], sems.at[c])
        for c in range(chunks)
    ]
    for copy in fetch:
        copy.start()
    fetch[0].wait()
    onehot = repeated_onehot(held_labels[...])
    counts = jnp.maximum(jnp.sum(onehot, axis=1, keepdims=True), 1.0)
    onehot = onehot.astype(jnp.bfloat16)
    sq = jnp.zeros((1, ROWS), jnp.float32)
    for c in range(chunks):
        fetch[1 + c].wait()
        group, wide = class_group(held[rows[c], :], onehot, counts)
        out_ref[8 * c : 8 * c + 8, :] = group
        sq = sq + jnp.sum(wide * wide, axis=0, keepdims=True)
    out_ref[32:40, :] = jnp.broadcast_to(counts[:8], (8, LANES))
    sq_ref[...] = sq


def joined_counts(counts):
    total = functools.reduce(jnp.add, counts)
    return total, [c / total for c in counts]


def joined_group(groups, counts, shares):
    row_id = lax.broadcasted_iota(jnp.int32, (8, LANES), 0)
    mean = functools.reduce(jnp.add, [g * w for g, w in zip(groups, shares)])
    between = functools.reduce(
        jnp.add, [(g - mean) * (g - mean) * c for g, c in zip(groups, counts)]
    )
    spread = functools.reduce(jnp.add, groups) + pltpu.roll(between, 4, 0)
    return jnp.where(row_id < CLASSES, mean, spread)


def target_joined(place, pieces, slots):
    n = len(pieces)
    for far, piece in enumerate(pieces):
        slots[lax.rem(place[0] + far, n)] = piece[...]
    counts = [slots[k, 8:16, :] for k in range(n)]
    total, shares = joined_counts(counts)
    return joined_group([slots[k, 0:8, :] for k in range(n)], counts, shares), total


def pair_kernel(place, *args):
    pieces, (out_ref, slots) = args[:-2], args[-2:]
    group, total = target_joined(place, pieces, slots)
    out_ref[0:8, :] = group
    out_ref[8:16, :] = total


def lanes_of(shape):
    return lax.broadcasted_iota(jnp.int32, shape, len(shape) - 1)


def near_kernel(place, *args):
    pieces, (src_group, out_ref, slots) = args[:-3], args[-3:]
    group, total = target_joined(place, pieces, slots)
    row_id = lax.broadcasted_iota(jnp.int32, (8, LANES), 0)
    group = jnp.where(row_id < CLASSES, group, group / total)
    out_ref[0:32, :] = src_group[0:32, :]
    out_ref[32:40, :] = jnp.where(lanes_of((8, LANES)) < LANES // 2, group, src_group[32:40, :])


def source_joined(got):
    peers = got.shape[0]
    half = LANES // 2
    lower = lanes_of((8, LANES)) < half
    last = [got[k, 32:40, :] for k in range(peers)]
    targets = [jnp.where(lower, g, 0.0) for g in last]
    counts = [jnp.where(lower, pltpu.roll(g, half, 1), g) for g in last]
    total, shares = joined_counts(counts)
    groups = [
        joined_group([got[k, 8 * c : 8 * c + 8, :] for k in range(peers)], counts, shares)
        for c in range(WIDTH // LANES)
    ]
    return groups, total, targets


def side_by_side(targets, width):
    out = targets[0]
    for k, target in enumerate(targets[1:]):
        out = out + pltpu.roll(target, (k + 1) * width, 1)
    return out


def middle_kernel(part, place, *args):
    pieces, (out_ref, slots) = args[:-2], args[-2:]
    for far, piece in enumerate(pieces):
        slots[lax.rem(place[0] + far, len(pieces))] = piece[...]
    groups, total, targets = source_joined(slots)
    target = side_by_side(targets, part)
    target = jnp.where(lanes_of((8, LANES)) < LANES // 2, target, total)
    for k in range(out_ref.shape[0]):
        for c, group in enumerate(groups):
            out_ref[k, 8 * c : 8 * c + 8, :] = group
        out_ref[k, 32:40, :] = target


def label_kernel(width, got, src_sq, src_lab, label_ref, xa_ref):
    groups, total, targets = source_joined(got)
    row_id = lax.broadcasted_iota(jnp.int32, (8, LANES), 0)
    lane_id = lanes_of((8, LANES))
    each = LANES // width
    sides = ([], [])
    for c, group in enumerate(groups):
        tgt = side_by_side(targets[each * c : each * c + each], width)
        for side, stat in zip(sides, (jnp.where(row_id < CLASSES, group, group / total), tgt)):
            side.append(jnp.where(row_id < CLASSES, stat, jnp.sqrt(stat + 1e-06)))

    def distances(one, other):
        out = jnp.zeros((8, LANES), jnp.float32)
        for k in range(CLASSES):
            far = jnp.zeros((8, LANES), jnp.float32)
            for g, h in zip(one, other):
                gap = g - jnp.where(row_id < CLASSES, h[k : k + 1], h[CLASSES + k : CLASSES + k + 1])
                far = far + gap * gap
            far = far + pltpu.roll(far, 4, 0)
            out = jnp.where(lane_id == k, jnp.sum(far, axis=1, keepdims=True), out)
        return out

    label_ref[...] = distances(*sides)[:CLASSES, :CLASSES]
    by_target = distances(*sides[::-1])
    by_target = jnp.concatenate([by_target, by_target], axis=0)
    row_id = lax.broadcasted_iota(jnp.int32, (16, 1), 0)
    part_id = row_id // CLASSES
    labels = src_lab[...]
    u = jnp.broadcast_to(src_sq[...], (16, ROWS))
    for a in range(CLASSES):
        u = u + jnp.where(labels == a, by_target[:, a : a + 1], 0.0)
    hi, mid, lo = three_parts(-0.5 * u)
    ones = jnp.where(row_id < 15, 1.0, 0.0)
    xa_ref[...] = jnp.where(
        part_id == 0, hi, jnp.where(part_id == 1, mid, jnp.where(part_id == 2, lo, ones))
    ).astype(jnp.bfloat16)


def three_parts(v):
    hi = v.astype(jnp.bfloat16).astype(jnp.float32)
    rest = v - hi
    mid = rest.astype(jnp.bfloat16).astype(jnp.float32)
    return hi, mid, rest - mid


def joined_lse(g_ref):
    g = g_ref[...]
    top = jnp.max(g, axis=0)
    return top + log2(jnp.sum(jnp.exp2(g - top[None]), axis=0))


def row_finish(top, total, out_ref):
    lines = []
    for k in range(CHUNKS):
        at = pl.ds(k * LANES, LANES)
        lse = top[at, :] + log2(jnp.sum(total[at, :], axis=1, keepdims=True))
        lines.append(lse.T[0:1, :])
    line = jnp.concatenate(lines, axis=0)
    out_ref[...] = jnp.broadcast_to(line[None], out_ref.shape)


def widen_top(top):
    for k in range(CHUNKS):
        at = pl.ds(k * LANES, LANES)
        top[at, :] = jnp.broadcast_to(jnp.max(top[at, :], axis=1, keepdims=True), (LANES, LANES))


def over_pairs(count, body, unroll):
    def several(step, _):
        for k in range(unroll):
            body(step * unroll + k)
        return 0

    steps = (count[0] + UNROLL - 1) // UNROLL * (UNROLL // unroll)
    lax.fori_loop(0, steps, several, 0)


def block_at(pairs, index):
    row = pl.multiple_of(pairs[2 * index] * BLOCK, BLOCK)
    return row, pairs[2 * index + 1]


def cost_kernel(n_x, pairs, count, place, xa, xt, *args):
    pieces, (tgt_lab, tiles, out_ref, y, ya, top, total) = args[:n_x], args[n_x:]
    row_id = lax.broadcasted_iota(jnp.int32, (16, 1), 0)
    part = row_id // CLASSES
    cls = row_id % CLASSES

    tgt_sq = jnp.zeros((16, ROWS), jnp.float32)
    for far, piece in enumerate(pieces):
        at = lax.rem(place[0] + far, n_x)
        for k in range(piece.shape[0]):
            y[pl.ds(pl.multiple_of((k * n_x + at) * 16, 16), 16), :] = piece[k]
            v = piece[k].astype(jnp.float32)
            tgt_sq = tgt_sq + v * v

    hi, mid, lo = three_parts(-0.5 * jnp.sum(tgt_sq, axis=0, keepdims=True))
    onehot = jnp.where(tgt_lab[...] == cls, 1.0, 0.0)
    ya[...] = jnp.where(
        part < 3,
        onehot,
        jnp.where(cls == 0, hi, jnp.where(cls == 1, mid, jnp.where(cls == 2, lo, 0.0))),
    ).astype(jnp.bfloat16)

    top[...] = jnp.full(top.shape, LOWEST, jnp.float32)
    total[...] = jnp.zeros(total.shape, jnp.float32)

    def build(index):
        row, col = block_at(pairs, index)
        rows = pl.ds(row, BLOCK)
        cols = pl.ds(pl.multiple_of(col * BLOCK, BLOCK), BLOCK)
        cross = jnp.dot(xt[rows, :], y[:, cols], preferred_element_type=jnp.float32)
        extra = lax.dot_general(
            xa[:, rows], ya[:, cols], (((0,), (0,)), ((), ())), preferred_element_type=jnp.float32
        )
        tile = (cross + extra) * (2.0 * TO_LOG2) + jnp.where(index < count[0], 0.0, LOWEST)
        tiles[index] = tile
        top[rows, :] = jnp.maximum(top[rows, :], jnp.maximum(tile[:, :LANES], tile[:, LANES:]))

    over_pairs(count, build, 4)
    widen_top(top)

    def add(index):
        row, _ = block_at(pairs, index)
        rows = pl.ds(row, BLOCK)
        high = top[rows, :]
        left = jnp.exp2(tiles[index, :, :LANES] - high)
        right = jnp.exp2(tiles[index, :, LANES:] - high)
        total[rows, :] = total[rows, :] + (left + right)

    over_pairs(count, add, 4)
    row_finish(top, total, out_ref)


def row_kernel(log_total, pairs, count, tiles, g_ref, out_ref, pot, top, total):
    pot[...] = log_total - joined_lse(g_ref)
    top[...] = jnp.full(top.shape, LOWEST, jnp.float32)
    total[...] = jnp.zeros(total.shape, jnp.float32)

    def scores(index, col):
        left = tiles[index, :, :LANES] + pot[pl.ds(2 * col, 1), :]
        right = tiles[index, :, LANES:] + pot[pl.ds(2 * col + 1, 1), :]
        return left, right

    def highest(index):
        row, col = block_at(pairs, index)
        rows = pl.ds(row, BLOCK)
        left, right = scores(index, col)
        top[rows, :] = jnp.maximum(top[rows, :], jnp.maximum(left, right))

    over_pairs(count, highest, 4)
    widen_top(top)

    def add(index):
        row, col = block_at(pairs, index)
        rows = pl.ds(row, BLOCK)
        left, right = scores(index, col)
        high = top[rows, :]
        total[rows, :] = total[rows, :] + (jnp.exp2(left - high) + jnp.exp2(right - high))

    over_pairs(count, add, 4)
    row_finish(top, total, out_ref)


def col_kernel(log_total, pairs, count, tiles, g_ref, out_ref, pot_ref, pot, top, total):
    line = log_total - joined_lse(g_ref)
    pot_ref[...] = line * TO_POT
    for k in range(CHUNKS):
        pot[pl.ds(k * LANES, LANES), :] = jnp.broadcast_to(line[k : k + 1, :], (LANES, LANES)).T
    top[...] = jnp.full(top.shape, LOWEST, jnp.float32)
    total[...] = jnp.zeros(total.shape, jnp.float32)

    def scores(index, row):
        rows = pl.ds(row, BLOCK)
        high = pot[rows, :]
        tile = tiles[index]
        return tile + jnp.concatenate([high, high], axis=1)

    def highest(index):
        row, col = block_at(pairs, index)
        score = scores(index, row)
        top[col] = jnp.maximum(top[col], jnp.max(score.reshape(BLOCK // 8, 8, BLOCK), axis=0))

    over_pairs(count, highest, 4)
    for k in range(BLK):
        top[k] = jnp.broadcast_to(jnp.max(top[k], axis=0, keepdims=True), (8, BLOCK))

    def add(index):
        row, col = block_at(pairs, index)
        score = scores(index, row).reshape(BLOCK // 8, 8, BLOCK)
        total[col] = total[col] + jnp.sum(jnp.exp2(score - top[col][None]), axis=0)

    over_pairs(count, add, 4)
    lines = []
    for k in range(BLK):
        lse = top[k][0:1] + log2(jnp.sum(total[k], axis=0, keepdims=True))
        lines += [lse[:, :LANES], lse[:, LANES:]]
    out = jnp.concatenate(lines, axis=0)
    out_ref[...] = jnp.broadcast_to(out[None], out_ref.shape)


def last_kernel(log_total, g_ref, pot_ref):
    pot_ref[...] = (log_total - joined_lse(g_ref)) * TO_POT


def smem():
    return pl.BlockSpec(memory_space=pltpu.SMEM)


def hbm():
    return pl.BlockSpec(memory_space=pltpu.HBM)


def vmem():
    return pl.BlockSpec(memory_space=pltpu.VMEM)


def f32(*shape):
    return jax.ShapeDtypeStruct(shape, jnp.float32)


def params():
    return pltpu.CompilerParams(vmem_limit_bytes=VMEM_LIMIT)


def on_device(source_embed, target_embed, source_labels, target_labels, pair_blocks, pair_count):
    pairs = pair_blocks.reshape(-1)
    count = pair_count.reshape(-1)
    n_src, n_tgt = lax.axis_size(SRC), lax.axis_size(TGT)

    def call(kernel, out_shape, *args, name):
        return pl.pallas_call(
            kernel,
            out_shape=out_shape,
            in_specs=[vmem()] * len(args),
            out_specs=jax.tree.map(lambda _: vmem(), out_shape),
            compiler_params=params(),
            name=name,
        )(*args)

    n_x, n_z = lax.axis_size("x"), lax.axis_size("z")
    part = target_embed.shape[0]
    near, tgt_group = pl.pallas_call(
        first_kernel,
        out_shape=(
            jax.ShapeDtypeStruct((n_z,) + target_embed.shape, jnp.bfloat16),
            f32(16, LANES),
        ),
        in_specs=[hbm(), hbm()],
        out_specs=(hbm(), vmem()),
        scratch_shapes=[
            pltpu.VMEM(target_embed.shape, jnp.bfloat16),
            pltpu.VMEM((1, ROWS), jnp.int32),
            pltpu.SemaphoreType.DMA((2,)),
            pltpu.SemaphoreType.DMA((n_z,)),
        ],
        compiler_params=params(),
        name="first",
    )(target_embed, target_labels[None])
    near = lax.all_to_all(near, "z", 0, 0)

    def around(x, axis):
        n = lax.axis_size(axis)
        return [x] + [
            lax.ppermute(x, axis, [((i + far) % n, i) for i in range(n)]) for far in range(1, n)
        ]

    def join_around(kernel, out_shape, pieces, axis, *more, name):
        x = pieces[0]
        return pl.pallas_call(
            kernel,
            out_shape=out_shape,
            in_specs=[smem()] + [vmem()] * (len(pieces) + len(more)),
            out_specs=vmem(),
            scratch_shapes=[pltpu.VMEM((len(pieces),) + x.shape, jnp.float32)],
            compiler_params=params(),
            name=name,
        )(lax.axis_index(axis).reshape(1), *pieces, *more)

    tgt_group = join_around(pair_kernel, f32(16, LANES), around(tgt_group, "c"), "c", name="pair")
    src_group, src_sq = pl.pallas_call(
        source_group_kernel,
        out_shape=(f32(40, LANES), f32(1, ROWS)),
        in_specs=[hbm(), hbm()],
        out_specs=(vmem(), vmem()),
        scratch_shapes=[
            pltpu.VMEM((WIDTH, ROWS), jnp.bfloat16),
            pltpu.VMEM((1, ROWS), jnp.int32),
            pltpu.SemaphoreType.DMA((WIDTH // LANES + 1,)),
        ],
        compiler_params=params(),
        name="source_group",
    )(source_embed, source_labels[None])
    stats = join_around(
        near_kernel, f32(40, LANES), around(tgt_group, "y"), "y", src_group, name="near"
    )

    near, stats = lax.optimization_barrier((near, around(stats, "x")))
    pieces = around(near, "x")
    stats = join_around(
        functools.partial(middle_kernel, part), f32(n_z, 40, LANES), stats, "x", name="middle"
    )
    stats = lax.all_to_all(stats, "z", 0, 0)
    label_cost, xa = call(
        functools.partial(label_kernel, part * n_x),
        (f32(CLASSES, CLASSES), jax.ShapeDtypeStruct((16, ROWS), jnp.bfloat16)),
        stats,
        src_sq,
        source_labels[None],
        name="label",
    )

    tall = pltpu.VMEM((ROWS, LANES), jnp.float32)
    wide = pltpu.VMEM((BLK, 8, BLOCK), jnp.float32)
    log_src = math.log2(ROWS * n_src)
    log_tgt = math.log2(ROWS * n_tgt)
    tiles, sent = pl.pallas_call(
        functools.partial(cost_kernel, n_x),
        out_shape=(f32(MAXP, BLOCK, BLOCK), f32(n_tgt, CHUNKS, LANES)),
        in_specs=[smem()] * 3 + [vmem()] * (3 + n_x),
        out_specs=(vmem(), vmem()),
        scratch_shapes=[
            pltpu.VMEM((WIDTH, ROWS), jnp.bfloat16),
            pltpu.VMEM((16, ROWS), jnp.bfloat16),
            tall,
            tall,
        ],
        compiler_params=params(),
        name="cost_rows",
    )(
        pairs,
        count,
        lax.axis_index("x").reshape(1),
        xa,
        source_embed.T,
        *pieces,
        target_labels[None],
    )

    def columns(got):
        return pl.pallas_call(
            functools.partial(col_kernel, log_tgt),
            out_shape=(f32(n_src, CHUNKS, LANES), f32(CHUNKS, LANES)),
            in_specs=[smem(), smem(), vmem(), vmem()],
            out_specs=(vmem(), vmem()),
            scratch_shapes=[tall, wide, wide],
            compiler_params=params(),
            name="columns",
        )(pairs, count, tiles, got)

    def rows(got):
        return pl.pallas_call(
            functools.partial(row_kernel, log_src),
            out_shape=f32(n_tgt, CHUNKS, LANES),
            in_specs=[smem(), smem(), vmem(), vmem()],
            out_specs=vmem(),
            scratch_shapes=[pltpu.VMEM((CHUNKS, LANES), jnp.float32), tall, tall],
            compiler_params=params(),
            name="rows",
        )(pairs, count, tiles, got)

    sent, _ = columns(lax.all_to_all(sent, TGT, 0, 0))
    sent = rows(lax.all_to_all(sent, SRC, 0, 0))
    sent, src_pot = columns(lax.all_to_all(sent, TGT, 0, 0))
    tgt_pot = pl.pallas_call(
        functools.partial(last_kernel, log_src),
        out_shape=f32(CHUNKS, LANES),
        in_specs=[vmem()],
        out_specs=vmem(),
        compiler_params=params(),
        name="last",
    )(lax.all_to_all(sent, SRC, 0, 0))
    return (src_pot.reshape(-1), tgt_pot.reshape(-1), label_cost)


def solution(mesh):
    fine = Mesh(np.asarray(mesh.devices).reshape(8, 4, 4, 2), SRC + TGT)
    return jax.shard_map(
        on_device,
        mesh=fine,
        in_specs=(
            P(None, SRC),
            P(SRC, TGT),
            P(SRC),
            P(TGT),
            P(SRC, TGT, None, None),
            P(SRC, TGT),
        ),
        out_specs=(P(SRC), P(TGT), P()),
        check_vma=False,
    )
```

```python
import functools
import math

import jax
import jax.numpy as jnp
import numpy as np
from jax import lax
from jax.experimental import pallas as pl
from jax.experimental.pallas import tpu as pltpu
from jax.sharding import Mesh, PartitionSpec as P

CLASSES = 4
BLOCK = 256
ROWS = 2048
BLK = ROWS // BLOCK
LANES = 128
CHUNKS = ROWS // LANES
MAXP = 24
UNROLL = 4
WIDTH = 512

EPSILON = 0.05
LOWEST = -1e30
LOG2E = 1.0 / math.log(2.0)
TO_LOG2 = LOG2E / EPSILON
TO_POT = EPSILON / LOG2E

SRC = ("z", "x")
TGT = ("y", "c")
VMEM_LIMIT = 24 * 1024 * 1024


def log2(x):
    return jnp.log(x) * LOG2E


def repeated_onehot(labels):
    row_id = lax.broadcasted_iota(jnp.int32, (16, 1), 0)
    return jnp.where(row_id < 12, jnp.where(labels == row_id % CLASSES, 1.0, 0.0), 0.0)


def across(onehot, values):
    return lax.dot_general(
        onehot, values, (((1,), (1,)), ((), ())), preferred_element_type=jnp.float32
    )


def class_group(values, onehot, counts):
    part = lax.broadcasted_iota(jnp.int32, (16, 1), 0) // CLASSES
    wide = values.astype(jnp.float32)
    mean = across(onehot, values) / counts
    hi, mid, lo = three_parts(mean)
    parts = jnp.where(
        part == 0, hi, jnp.where(part == 1, mid, jnp.where(part == 2, lo, 0.0))
    ).astype(jnp.bfloat16)
    center = lax.dot_general(
        parts, onehot, (((0,), (0,)), ((), ())), preferred_element_type=jnp.float32
    )
    centered = wide - center
    hi, mid, lo = three_parts(centered * centered)
    spread = sum(across(onehot, p.astype(jnp.bfloat16)) for p in (hi, mid, lo))
    return jnp.where(part == 0, mean, spread)[:8], wide


def first_kernel(embed, labels, near_ref, out_ref, sems):
    copies = [
        pltpu.make_async_copy(embed, near_ref.at[k], sems.at[k]) for k in range(near_ref.shape[0])
    ]
    for copy in copies:
        copy.start()
    onehot = repeated_onehot(labels[...])
    counts = jnp.maximum(jnp.sum(onehot, axis=1, keepdims=True), 1.0)
    group, _ = class_group(embed[...], onehot.astype(jnp.bfloat16), counts)
    out_ref[...] = jnp.zeros(out_ref.shape, jnp.float32)
    out_ref[0:8, 0 : group.shape[1]] = group
    out_ref[8:16, :] = jnp.broadcast_to(counts[:8], (8, LANES))
    for copy in copies:
        copy.wait()


def source_group_kernel(embed, labels, out_ref, sq_ref):
    onehot = repeated_onehot(labels[...])
    counts = jnp.maximum(jnp.sum(onehot, axis=1, keepdims=True), 1.0)
    onehot = onehot.astype(jnp.bfloat16)
    sq = jnp.zeros((1, ROWS), jnp.float32)
    for c in range(WIDTH // LANES):
        group, wide = class_group(embed[c * LANES : (c + 1) * LANES, :], onehot, counts)
        out_ref[8 * c : 8 * c + 8, :] = group
        sq = sq + jnp.sum(wide * wide, axis=0, keepdims=True)
    out_ref[32:40, :] = jnp.broadcast_to(counts[:8], (8, LANES))
    sq_ref[...] = sq


def joined_counts(counts):
    total = functools.reduce(jnp.add, counts)
    return total, [c / total for c in counts]


def joined_group(groups, counts, shares):
    row_id = lax.broadcasted_iota(jnp.int32, (8, LANES), 0)
    mean = functools.reduce(jnp.add, [g * w for g, w in zip(groups, shares)])
    between = functools.reduce(
        jnp.add, [(g - mean) * (g - mean) * c for g, c in zip(groups, counts)]
    )
    spread = functools.reduce(jnp.add, groups) + pltpu.roll(between, 4, 0)
    return jnp.where(row_id < CLASSES, mean, spread)


def target_joined(place, pieces, slots):
    n = len(pieces)
    for far, piece in enumerate(pieces):
        slots[lax.rem(place[0] + far, n)] = piece[...]
    counts = [slots[k, 8:16, :] for k in range(n)]
    total, shares = joined_counts(counts)
    return joined_group([slots[k, 0:8, :] for k in range(n)], counts, shares), total


def pair_kernel(place, *args):
    pieces, (out_ref, slots) = args[:-2], args[-2:]
    group, total = target_joined(place, pieces, slots)
    out_ref[0:8, :] = group
    out_ref[8:16, :] = total


def near_kernel(place, *args):
    pieces, (src_group, out_ref, slots) = args[:-3], args[-3:]
    group, total = target_joined(place, pieces, slots)
    row_id = lax.broadcasted_iota(jnp.int32, (8, LANES), 0)
    group = jnp.where(row_id < CLASSES, group, group / total)
    for k in range(out_ref.shape[0]):
        out_ref[k, 0:40, :] = src_group[...]
        out_ref[k, 40:48, :] = group


def source_joined(got):
    peers = got.shape[0]
    counts = [got[k, 32:40, :] for k in range(peers)]
    total, shares = joined_counts(counts)
    groups = [
        joined_group([got[k, 8 * c : 8 * c + 8, :] for k in range(peers)], counts, shares)
        for c in range(WIDTH // LANES)
    ]
    return groups, total


def middle_kernel(width, got, out_ref):
    groups, total = source_joined(got)
    each = LANES // width
    for c in range(WIDTH // LANES):
        tgt = got[each * c, 40:48, :]
        for k in range(1, each):
            tgt = tgt + pltpu.roll(got[each * c + k, 40:48, :], k * width, 1)
        for k in range(out_ref.shape[0]):
            out_ref[k, 8 * c : 8 * c + 8, :] = groups[c]
            out_ref[k, 40 + 8 * c : 48 + 8 * c, :] = tgt
    for k in range(out_ref.shape[0]):
        out_ref[k, 32:40, :] = total


def label_kernel(part, got, src_sq, src_lab, label_ref, xa_ref):
    groups, total = source_joined(got)
    row_id = lax.broadcasted_iota(jnp.int32, (8, LANES), 0)
    lane_id = lax.broadcasted_iota(jnp.int32, (8, LANES), 1)
    sides = ([], [])
    for c, group in enumerate(groups):
        at = slice(40 + 8 * c, 48 + 8 * c)
        tgt = got[0, at, :]
        for k in range(1, got.shape[0]):
            tgt = tgt + pltpu.roll(got[k, at, :], k * part, 1)
        for side, stat in zip(sides, (jnp.where(row_id < CLASSES, group, group / total), tgt)):
            side.append(jnp.where(row_id < CLASSES, stat, jnp.sqrt(stat + 1e-06)))

    def distances(one, other):
        out = jnp.zeros((8, LANES), jnp.float32)
        for k in range(CLASSES):
            far = jnp.zeros((8, LANES), jnp.float32)
            for g, h in zip(one, other):
                gap = g - jnp.where(row_id < CLASSES, h[k : k + 1], h[CLASSES + k : CLASSES + k + 1])
                far = far + gap * gap
            far = far + pltpu.roll(far, 4, 0)
            out = jnp.where(lane_id == k, jnp.sum(far, axis=1, keepdims=True), out)
        return out

    label_ref[...] = distances(*sides)[:CLASSES, :CLASSES]
    by_target = distances(*sides[::-1])
    by_target = jnp.concatenate([by_target, by_target], axis=0)
    row_id = lax.broadcasted_iota(jnp.int32, (16, 1), 0)
    part_id = row_id // CLASSES
    labels = src_lab[...]
    u = jnp.broadcast_to(src_sq[...], (16, ROWS))
    for a in range(CLASSES):
        u = u + jnp.where(labels == a, by_target[:, a : a + 1], 0.0)
    hi, mid, lo = three_parts(-0.5 * u)
    ones = jnp.where(row_id < 15, 1.0, 0.0)
    xa_ref[...] = jnp.where(
        part_id == 0, hi, jnp.where(part_id == 1, mid, jnp.where(part_id == 2, lo, ones))
    ).astype(jnp.bfloat16)


def three_parts(v):
    hi = v.astype(jnp.bfloat16).astype(jnp.float32)
    rest = v - hi
    mid = rest.astype(jnp.bfloat16).astype(jnp.float32)
    return hi, mid, rest - mid


def joined_lse(g_ref):
    g = g_ref[...]
    top = jnp.max(g, axis=0)
    return top + log2(jnp.sum(jnp.exp2(g - top[None]), axis=0))


def row_finish(top, total, out_ref):
    lines = []
    for k in range(CHUNKS):
        at = pl.ds(k * LANES, LANES)
        lse = top[at, :] + log2(jnp.sum(total[at, :], axis=1, keepdims=True))
        lines.append(lse.T[0:1, :])
    line = jnp.concatenate(lines, axis=0)
    out_ref[...] = jnp.broadcast_to(line[None], out_ref.shape)


def widen_top(top):
    for k in range(CHUNKS):
        at = pl.ds(k * LANES, LANES)
        top[at, :] = jnp.broadcast_to(jnp.max(top[at, :], axis=1, keepdims=True), (LANES, LANES))


def over_pairs(count, body, unroll):
    def several(step, _):
        for k in range(unroll):
            body(step * unroll + k)
        return 0

    steps = (count[0] + UNROLL - 1) // UNROLL * (UNROLL // unroll)
    lax.fori_loop(0, steps, several, 0)


def block_at(pairs, index):
    row = pl.multiple_of(pairs[2 * index] * BLOCK, BLOCK)
    return row, pairs[2 * index + 1]


def cost_kernel(n_x, pairs, count, place, xa, xt, *args):
    pieces, (tgt_lab, tiles, out_ref, y, ya, top, total) = args[:n_x], args[n_x:]
    row_id = lax.broadcasted_iota(jnp.int32, (16, 1), 0)
    part = row_id // CLASSES
    cls = row_id % CLASSES

    tgt_sq = jnp.zeros((16, ROWS), jnp.float32)
    for far, piece in enumerate(pieces):
        at = lax.rem(place[0] + far, n_x)
        for k in range(piece.shape[0]):
            y[pl.ds(pl.multiple_of((k * n_x + at) * 16, 16), 16), :] = piece[k]
            v = piece[k].astype(jnp.float32)
            tgt_sq = tgt_sq + v * v

    hi, mid, lo = three_parts(-0.5 * jnp.sum(tgt_sq, axis=0, keepdims=True))
    onehot = jnp.where(tgt_lab[...] == cls, 1.0, 0.0)
    ya[...] = jnp.where(
        part < 3,
        onehot,
        jnp.where(cls == 0, hi, jnp.where(cls == 1, mid, jnp.where(cls == 2, lo, 0.0))),
    ).astype(jnp.bfloat16)

    top[...] = jnp.full(top.shape, LOWEST, jnp.float32)
    total[...] = jnp.zeros(total.shape, jnp.float32)

    def build(index):
        row, col = block_at(pairs, index)
        rows = pl.ds(row, BLOCK)
        cols = pl.ds(pl.multiple_of(col * BLOCK, BLOCK), BLOCK)
        cross = jnp.dot(xt[rows, :], y[:, cols], preferred_element_type=jnp.float32)
        extra = lax.dot_general(
            xa[:, rows], ya[:, cols], (((0,), (0,)), ((), ())), preferred_element_type=jnp.float32
        )
        tile = (cross + extra) * (2.0 * TO_LOG2) + jnp.where(index < count[0], 0.0, LOWEST)
        tiles[index] = tile
        top[rows, :] = jnp.maximum(top[rows, :], jnp.maximum(tile[:, :LANES], tile[:, LANES:]))

    over_pairs(count, build, 4)
    widen_top(top)

    def add(index):
        row, _ = block_at(pairs, index)
        rows = pl.ds(row, BLOCK)
        high = top[rows, :]
        left = jnp.exp2(tiles[index, :, :LANES] - high)
        right = jnp.exp2(tiles[index, :, LANES:] - high)
        total[rows, :] = total[rows, :] + (left + right)

    over_pairs(count, add, 4)
    row_finish(top, total, out_ref)


def row_kernel(log_total, pairs, count, tiles, g_ref, out_ref, pot, top, total):
    pot[...] = log_total - joined_lse(g_ref)
    top[...] = jnp.full(top.shape, LOWEST, jnp.float32)
    total[...] = jnp.zeros(total.shape, jnp.float32)

    def scores(index, col):
        left = tiles[index, :, :LANES] + pot[pl.ds(2 * col, 1), :]
        right = tiles[index, :, LANES:] + pot[pl.ds(2 * col + 1, 1), :]
        return left, right

    def highest(index):
        row, col = block_at(pairs, index)
        rows = pl.ds(row, BLOCK)
        left, right = scores(index, col)
        top[rows, :] = jnp.maximum(top[rows, :], jnp.maximum(left, right))

    over_pairs(count, highest, 4)
    widen_top(top)

    def add(index):
        row, col = block_at(pairs, index)
        rows = pl.ds(row, BLOCK)
        left, right = scores(index, col)
        high = top[rows, :]
        total[rows, :] = total[rows, :] + (jnp.exp2(left - high) + jnp.exp2(right - high))

    over_pairs(count, add, 4)
    row_finish(top, total, out_ref)


def col_kernel(log_total, pairs, count, tiles, g_ref, out_ref, pot_ref, pot, top, total):
    line = log_total - joined_lse(g_ref)
    pot_ref[...] = line * TO_POT
    for k in range(CHUNKS):
        pot[pl.ds(k * LANES, LANES), :] = jnp.broadcast_to(line[k : k + 1, :], (LANES, LANES)).T
    top[...] = jnp.full(top.shape, LOWEST, jnp.float32)
    total[...] = jnp.zeros(total.shape, jnp.float32)

    def scores(index, row):
        rows = pl.ds(row, BLOCK)
        high = pot[rows, :]
        tile = tiles[index]
        return tile + jnp.concatenate([high, high], axis=1)

    def highest(index):
        row, col = block_at(pairs, index)
        score = scores(index, row)
        top[col] = jnp.maximum(top[col], jnp.max(score.reshape(BLOCK // 8, 8, BLOCK), axis=0))

    over_pairs(count, highest, 4)
    for k in range(BLK):
        top[k] = jnp.broadcast_to(jnp.max(top[k], axis=0, keepdims=True), (8, BLOCK))

    def add(index):
        row, col = block_at(pairs, index)
        score = scores(index, row).reshape(BLOCK // 8, 8, BLOCK)
        total[col] = total[col] + jnp.sum(jnp.exp2(score - top[col][None]), axis=0)

    over_pairs(count, add, 4)
    lines = []
    for k in range(BLK):
        lse = top[k][0:1] + log2(jnp.sum(total[k], axis=0, keepdims=True))
        lines += [lse[:, :LANES], lse[:, LANES:]]
    out = jnp.concatenate(lines, axis=0)
    out_ref[...] = jnp.broadcast_to(out[None], out_ref.shape)


def last_kernel(log_total, g_ref, pot_ref):
    pot_ref[...] = (log_total - joined_lse(g_ref)) * TO_POT


def smem():
    return pl.BlockSpec(memory_space=pltpu.SMEM)


def vmem():
    return pl.BlockSpec(memory_space=pltpu.VMEM)


def f32(*shape):
    return jax.ShapeDtypeStruct(shape, jnp.float32)


def params():
    return pltpu.CompilerParams(vmem_limit_bytes=VMEM_LIMIT)


def on_device(source_embed, target_embed, source_labels, target_labels, pair_blocks, pair_count):
    pairs = pair_blocks.reshape(-1)
    count = pair_count.reshape(-1)
    n_src, n_tgt = lax.axis_size(SRC), lax.axis_size(TGT)

    def call(kernel, out_shape, *args, name):
        return pl.pallas_call(
            kernel,
            out_shape=out_shape,
            in_specs=[vmem()] * len(args),
            out_specs=jax.tree.map(lambda _: vmem(), out_shape),
            compiler_params=params(),
            name=name,
        )(*args)

    n_x, n_z = lax.axis_size("x"), lax.axis_size("z")
    part = target_embed.shape[0]
    near, tgt_group = pl.pallas_call(
        first_kernel,
        out_shape=(
            jax.ShapeDtypeStruct((n_z,) + target_embed.shape, jnp.bfloat16),
            f32(16, LANES),
        ),
        in_specs=[vmem(), vmem()],
        out_specs=(pl.BlockSpec(memory_space=pl.ANY), vmem()),
        scratch_shapes=[pltpu.SemaphoreType.DMA((n_z,))],
        compiler_params=params(),
        name="first",
    )(target_embed, target_labels[None])
    near = lax.all_to_all(near, "z", 0, 0)

    def around(x, axis):
        n = lax.axis_size(axis)
        return [x] + [
            lax.ppermute(x, axis, [((i + far) % n, i) for i in range(n)]) for far in range(1, n)
        ]

    def join_targets(kernel, out_shape, x, axis, *more, name):
        pieces = around(x, axis)
        return pl.pallas_call(
            kernel,
            out_shape=out_shape,
            in_specs=[smem()] + [vmem()] * (len(pieces) + len(more)),
            out_specs=vmem(),
            scratch_shapes=[pltpu.VMEM((len(pieces), 16, LANES), jnp.float32)],
            compiler_params=params(),
            name=name,
        )(lax.axis_index(axis).reshape(1), *pieces, *more)

    tgt_group = join_targets(pair_kernel, f32(16, LANES), tgt_group, "c", name="pair")
    src_group, src_sq = call(
        source_group_kernel,
        (f32(40, LANES), f32(1, ROWS)),
        source_embed,
        source_labels[None],
        name="source_group",
    )
    stats = join_targets(
        near_kernel, f32(n_z, 48, LANES), tgt_group, "y", src_group, name="near"
    )
    near, stats = lax.optimization_barrier((near, stats))

    pieces = around(near, "x")
    stats = lax.all_to_all(stats, "z", 0, 0)
    stats = call(
        functools.partial(middle_kernel, part * n_x), f32(n_x, 72, LANES), stats, name="middle"
    )
    stats = lax.all_to_all(stats, "x", 0, 0)
    label_cost, xa = call(
        functools.partial(label_kernel, part),
        (f32(CLASSES, CLASSES), jax.ShapeDtypeStruct((16, ROWS), jnp.bfloat16)),
        stats,
        src_sq,
        source_labels[None],
        name="label",
    )

    tall = pltpu.VMEM((ROWS, LANES), jnp.float32)
    wide = pltpu.VMEM((BLK, 8, BLOCK), jnp.float32)
    log_src = math.log2(ROWS * n_src)
    log_tgt = math.log2(ROWS * n_tgt)
    tiles, sent = pl.pallas_call(
        functools.partial(cost_kernel, n_x),
        out_shape=(f32(MAXP, BLOCK, BLOCK), f32(n_tgt, CHUNKS, LANES)),
        in_specs=[smem()] * 3 + [vmem()] * (3 + n_x),
        out_specs=(vmem(), vmem()),
        scratch_shapes=[
            pltpu.VMEM((WIDTH, ROWS), jnp.bfloat16),
            pltpu.VMEM((16, ROWS), jnp.bfloat16),
            tall,
            tall,
        ],
        compiler_params=params(),
        name="cost_rows",
    )(
        pairs,
        count,
        lax.axis_index("x").reshape(1),
        xa,
        source_embed.T,
        *pieces,
        target_labels[None],
    )

    def columns(got):
        return pl.pallas_call(
            functools.partial(col_kernel, log_tgt),
            out_shape=(f32(n_src, CHUNKS, LANES), f32(CHUNKS, LANES)),
            in_specs=[smem(), smem(), vmem(), vmem()],
            out_specs=(vmem(), vmem()),
            scratch_shapes=[tall, wide, wide],
            compiler_params=params(),
            name="columns",
        )(pairs, count, tiles, got)

    def rows(got):
        return pl.pallas_call(
            functools.partial(row_kernel, log_src),
            out_shape=f32(n_tgt, CHUNKS, LANES),
            in_specs=[smem(), smem(), vmem(), vmem()],
            out_specs=vmem(),
            scratch_shapes=[pltpu.VMEM((CHUNKS, LANES), jnp.float32), tall, tall],
            compiler_params=params(),
            name="rows",
        )(pairs, count, tiles, got)

    sent, _ = columns(lax.all_to_all(sent, TGT, 0, 0))
    sent = rows(lax.all_to_all(sent, SRC, 0, 0))
    sent, src_pot = columns(lax.all_to_all(sent, TGT, 0, 0))
    tgt_pot = pl.pallas_call(
        functools.partial(last_kernel, log_src),
        out_shape=f32(CHUNKS, LANES),
        in_specs=[vmem()],
        out_specs=vmem(),
        compiler_params=params(),
        name="last",
    )(lax.all_to_all(sent, SRC, 0, 0))
    return (src_pot.reshape(-1), tgt_pot.reshape(-1), label_cost)


def solution(mesh):
    fine = Mesh(np.asarray(mesh.devices).reshape(8, 4, 4, 2), SRC + TGT)
    return jax.shard_map(
        on_device,
        mesh=fine,
        in_specs=(
            P(None, SRC),
            P(SRC, TGT),
            P(SRC),
            P(TGT),
            P(SRC, TGT, None, None),
            P(SRC, TGT),
        ),
        out_specs=(P(SRC), P(TGT), P()),
        check_vma=False,
    )
```

```python
import functools
import math

import jax
import jax.numpy as jnp
import numpy as np
from jax import lax
from jax.experimental import pallas as pl
from jax.experimental.pallas import tpu as pltpu
from jax.sharding import Mesh, PartitionSpec as P

CLASSES = 4
BLOCK = 256
ROWS = 2048
BLK = ROWS // BLOCK
LANES = 128
CHUNKS = ROWS // LANES
MAXP = 24
UNROLL = 4
WIDTH = 512

EPSILON = 0.05
LOWEST = -1e30
LOG2E = 1.0 / math.log(2.0)
TO_LOG2 = LOG2E / EPSILON
TO_POT = EPSILON / LOG2E

SRC = ("z", "x")
TGT = ("y", "c")
VMEM_LIMIT = 24 * 1024 * 1024


def log2(x):
    return jnp.log(x) * LOG2E


def repeated_onehot(labels):
    row_id = lax.broadcasted_iota(jnp.int32, (16, 1), 0)
    return jnp.where(row_id < 12, jnp.where(labels == row_id % CLASSES, 1.0, 0.0), 0.0)


def across(onehot, values):
    return lax.dot_general(
        onehot, values, (((1,), (1,)), ((), ())), preferred_element_type=jnp.float32
    )


def class_group(values, onehot, counts):
    part = lax.broadcasted_iota(jnp.int32, (16, 1), 0) // CLASSES
    wide = values.astype(jnp.float32)
    mean = across(onehot, values) / counts
    hi, mid, lo = three_parts(mean)
    parts = jnp.where(
        part == 0, hi, jnp.where(part == 1, mid, jnp.where(part == 2, lo, 0.0))
    ).astype(jnp.bfloat16)
    center = lax.dot_general(
        parts, onehot, (((0,), (0,)), ((), ())), preferred_element_type=jnp.float32
    )
    centered = wide - center
    hi, mid, lo = three_parts(centered * centered)
    spread = sum(across(onehot, p.astype(jnp.bfloat16)) for p in (hi, mid, lo))
    return jnp.where(part == 0, mean, spread)[:8], wide


def first_kernel(embed, labels, near_ref, out_ref, sems):
    copies = [
        pltpu.make_async_copy(embed, near_ref.at[k], sems.at[k]) for k in range(near_ref.shape[0])
    ]
    for copy in copies:
        copy.start()
    onehot = repeated_onehot(labels[...])
    counts = jnp.maximum(jnp.sum(onehot, axis=1, keepdims=True), 1.0)
    group, _ = class_group(embed[...], onehot.astype(jnp.bfloat16), counts)
    out_ref[...] = jnp.zeros(out_ref.shape, jnp.float32)
    out_ref[0:8, 0 : group.shape[1]] = group
    out_ref[8:16, :] = jnp.broadcast_to(counts[:8], (8, LANES))
    for copy in copies:
        copy.wait()


def source_group_kernel(embed, labels, out_ref, sq_ref):
    onehot = repeated_onehot(labels[...])
    counts = jnp.maximum(jnp.sum(onehot, axis=1, keepdims=True), 1.0)
    onehot = onehot.astype(jnp.bfloat16)
    sq = jnp.zeros((1, ROWS), jnp.float32)
    for c in range(WIDTH // LANES):
        group, wide = class_group(embed[c * LANES : (c + 1) * LANES, :], onehot, counts)
        out_ref[8 * c : 8 * c + 8, :] = group
        sq = sq + jnp.sum(wide * wide, axis=0, keepdims=True)
    out_ref[32:40, :] = jnp.broadcast_to(counts[:8], (8, LANES))
    sq_ref[...] = sq


def joined_counts(counts):
    total = functools.reduce(jnp.add, counts)
    return total, [c / total for c in counts]


def joined_group(groups, counts, shares):
    row_id = lax.broadcasted_iota(jnp.int32, (8, LANES), 0)
    mean = functools.reduce(jnp.add, [g * w for g, w in zip(groups, shares)])
    between = functools.reduce(
        jnp.add, [(g - mean) * (g - mean) * c for g, c in zip(groups, counts)]
    )
    spread = functools.reduce(jnp.add, groups) + pltpu.roll(between, 4, 0)
    return jnp.where(row_id < CLASSES, mean, spread)


def target_joined(place, pieces, slots):
    n = len(pieces)
    for far, piece in enumerate(pieces):
        slots[lax.rem(place[0] + far, n)] = piece[...]
    counts = [slots[k, 8:16, :] for k in range(n)]
    total, shares = joined_counts(counts)
    return joined_group([slots[k, 0:8, :] for k in range(n)], counts, shares), total


def pair_kernel(place, *args):
    pieces, (out_ref, slots) = args[:-2], args[-2:]
    group, total = target_joined(place, pieces, slots)
    out_ref[0:8, :] = group
    out_ref[8:16, :] = total


def near_kernel(place, *args):
    pieces, (src_group, out_ref, slots) = args[:-3], args[-3:]
    group, total = target_joined(place, pieces, slots)
    row_id = lax.broadcasted_iota(jnp.int32, (8, LANES), 0)
    group = jnp.where(row_id < CLASSES, group, group / total)
    for k in range(out_ref.shape[0]):
        out_ref[k, 0:40, :] = src_group[...]
        out_ref[k, 40:48, :] = group


def source_joined(got):
    peers = got.shape[0]
    counts = [got[k, 32:40, :] for k in range(peers)]
    total, shares = joined_counts(counts)
    groups = [
        joined_group([got[k, 8 * c : 8 * c + 8, :] for k in range(peers)], counts, shares)
        for c in range(WIDTH // LANES)
    ]
    return groups, total


def middle_kernel(width, got, out_ref):
    groups, total = source_joined(got)
    each = LANES // width
    for c in range(WIDTH // LANES):
        tgt = got[each * c, 40:48, :]
        for k in range(1, each):
            tgt = tgt + pltpu.roll(got[each * c + k, 40:48, :], k * width, 1)
        for k in range(out_ref.shape[0]):
            out_ref[k, 8 * c : 8 * c + 8, :] = groups[c]
            out_ref[k, 40 + 8 * c : 48 + 8 * c, :] = tgt
    for k in range(out_ref.shape[0]):
        out_ref[k, 32:40, :] = total


def label_kernel(part, got, src_sq, src_lab, label_ref, xa_ref):
    groups, total = source_joined(got)
    row_id = lax.broadcasted_iota(jnp.int32, (8, LANES), 0)
    lane_id = lax.broadcasted_iota(jnp.int32, (8, LANES), 1)
    sides = ([], [])
    for c, group in enumerate(groups):
        at = slice(40 + 8 * c, 48 + 8 * c)
        tgt = got[0, at, :]
        for k in range(1, got.shape[0]):
            tgt = tgt + pltpu.roll(got[k, at, :], k * part, 1)
        for side, stat in zip(sides, (jnp.where(row_id < CLASSES, group, group / total), tgt)):
            side.append(jnp.where(row_id < CLASSES, stat, jnp.sqrt(stat + 1e-06)))

    def distances(one, other):
        out = jnp.zeros((8, LANES), jnp.float32)
        for k in range(CLASSES):
            far = jnp.zeros((8, LANES), jnp.float32)
            for g, h in zip(one, other):
                gap = g - jnp.where(row_id < CLASSES, h[k : k + 1], h[CLASSES + k : CLASSES + k + 1])
                far = far + gap * gap
            far = far + pltpu.roll(far, 4, 0)
            out = jnp.where(lane_id == k, jnp.sum(far, axis=1, keepdims=True), out)
        return out

    label_ref[...] = distances(*sides)[:CLASSES, :CLASSES]
    by_target = distances(*sides[::-1])
    by_target = jnp.concatenate([by_target, by_target], axis=0)
    row_id = lax.broadcasted_iota(jnp.int32, (16, 1), 0)
    part_id = row_id // CLASSES
    labels = src_lab[...]
    u = jnp.broadcast_to(src_sq[...], (16, ROWS))
    for a in range(CLASSES):
        u = u + jnp.where(labels == a, by_target[:, a : a + 1], 0.0)
    hi, mid, lo = three_parts(-0.5 * u)
    ones = jnp.where(row_id < 15, 1.0, 0.0)
    xa_ref[...] = jnp.where(
        part_id == 0, hi, jnp.where(part_id == 1, mid, jnp.where(part_id == 2, lo, ones))
    ).astype(jnp.bfloat16)


def three_parts(v):
    hi = v.astype(jnp.bfloat16).astype(jnp.float32)
    rest = v - hi
    mid = rest.astype(jnp.bfloat16).astype(jnp.float32)
    return hi, mid, rest - mid


def joined_lse(g_ref):
    g = g_ref[...]
    top = jnp.max(g, axis=0)
    return top + log2(jnp.sum(jnp.exp2(g - top[None]), axis=0))


def row_finish(top, total, out_ref):
    lines = []
    for k in range(CHUNKS):
        at = pl.ds(k * LANES, LANES)
        lse = top[at, :] + log2(jnp.sum(total[at, :], axis=1, keepdims=True))
        lines.append(lse.T[0:1, :])
    line = jnp.concatenate(lines, axis=0)
    out_ref[...] = jnp.broadcast_to(line[None], out_ref.shape)


def widen_top(top):
    for k in range(CHUNKS):
        at = pl.ds(k * LANES, LANES)
        top[at, :] = jnp.broadcast_to(jnp.max(top[at, :], axis=1, keepdims=True), (LANES, LANES))


def over_pairs(count, body, unroll):
    def several(step, _):
        for k in range(unroll):
            body(step * unroll + k)
        return 0

    steps = (count[0] + UNROLL - 1) // UNROLL * (UNROLL // unroll)
    lax.fori_loop(0, steps, several, 0)


def block_at(pairs, index):
    row = pl.multiple_of(pairs[2 * index] * BLOCK, BLOCK)
    return row, pairs[2 * index + 1]


def cost_kernel(n_x, pairs, count, place, xa, xt, *args):
    pieces, (tgt_lab, tiles, out_ref, y, ya, top, total) = args[:n_x], args[n_x:]
    row_id = lax.broadcasted_iota(jnp.int32, (16, 1), 0)
    part = row_id // CLASSES
    cls = row_id % CLASSES

    tgt_sq = jnp.zeros((16, ROWS), jnp.float32)
    for far, piece in enumerate(pieces):
        at = lax.rem(place[0] + far, n_x)
        for k in range(piece.shape[0]):
            z = k + place[1] * (piece.shape[0] - 1 - 2 * k)
            y[pl.ds(pl.multiple_of((z * n_x + at) * 16, 16), 16), :] = piece[k]
            v = piece[k].astype(jnp.float32)
            tgt_sq = tgt_sq + v * v

    hi, mid, lo = three_parts(-0.5 * jnp.sum(tgt_sq, axis=0, keepdims=True))
    onehot = jnp.where(tgt_lab[...] == cls, 1.0, 0.0)
    ya[...] = jnp.where(
        part < 3,
        onehot,
        jnp.where(cls == 0, hi, jnp.where(cls == 1, mid, jnp.where(cls == 2, lo, 0.0))),
    ).astype(jnp.bfloat16)

    top[...] = jnp.full(top.shape, LOWEST, jnp.float32)
    total[...] = jnp.zeros(total.shape, jnp.float32)

    def build(index):
        row, col = block_at(pairs, index)
        rows = pl.ds(row, BLOCK)
        cols = pl.ds(pl.multiple_of(col * BLOCK, BLOCK), BLOCK)
        cross = jnp.dot(xt[rows, :], y[:, cols], preferred_element_type=jnp.float32)
        extra = lax.dot_general(
            xa[:, rows], ya[:, cols], (((0,), (0,)), ((), ())), preferred_element_type=jnp.float32
        )
        tile = (cross + extra) * (2.0 * TO_LOG2) + jnp.where(index < count[0], 0.0, LOWEST)
        tiles[index] = tile
        top[rows, :] = jnp.maximum(top[rows, :], jnp.maximum(tile[:, :LANES], tile[:, LANES:]))

    over_pairs(count, build, 4)
    widen_top(top)

    def add(index):
        row, _ = block_at(pairs, index)
        rows = pl.ds(row, BLOCK)
        high = top[rows, :]
        left = jnp.exp2(tiles[index, :, :LANES] - high)
        right = jnp.exp2(tiles[index, :, LANES:] - high)
        total[rows, :] = total[rows, :] + (left + right)

    over_pairs(count, add, 4)
    row_finish(top, total, out_ref)


def row_kernel(log_total, pairs, count, tiles, g_ref, out_ref, pot, top, total):
    pot[...] = log_total - joined_lse(g_ref)
    top[...] = jnp.full(top.shape, LOWEST, jnp.float32)
    total[...] = jnp.zeros(total.shape, jnp.float32)

    def scores(index, col):
        left = tiles[index, :, :LANES] + pot[pl.ds(2 * col, 1), :]
        right = tiles[index, :, LANES:] + pot[pl.ds(2 * col + 1, 1), :]
        return left, right

    def highest(index):
        row, col = block_at(pairs, index)
        rows = pl.ds(row, BLOCK)
        left, right = scores(index, col)
        top[rows, :] = jnp.maximum(top[rows, :], jnp.maximum(left, right))

    over_pairs(count, highest, 4)
    widen_top(top)

    def add(index):
        row, col = block_at(pairs, index)
        rows = pl.ds(row, BLOCK)
        left, right = scores(index, col)
        high = top[rows, :]
        total[rows, :] = total[rows, :] + (jnp.exp2(left - high) + jnp.exp2(right - high))

    over_pairs(count, add, 4)
    row_finish(top, total, out_ref)


def col_kernel(log_total, pairs, count, tiles, g_ref, out_ref, pot_ref, pot, top, total):
    line = log_total - joined_lse(g_ref)
    pot_ref[...] = line * TO_POT
    for k in range(CHUNKS):
        pot[pl.ds(k * LANES, LANES), :] = jnp.broadcast_to(line[k : k + 1, :], (LANES, LANES)).T
    top[...] = jnp.full(top.shape, LOWEST, jnp.float32)
    total[...] = jnp.zeros(total.shape, jnp.float32)

    def scores(index, row):
        rows = pl.ds(row, BLOCK)
        high = pot[rows, :]
        tile = tiles[index]
        return tile + jnp.concatenate([high, high], axis=1)

    def highest(index):
        row, col = block_at(pairs, index)
        score = scores(index, row)
        top[col] = jnp.maximum(top[col], jnp.max(score.reshape(BLOCK // 8, 8, BLOCK), axis=0))

    over_pairs(count, highest, 4)
    for k in range(BLK):
        top[k] = jnp.broadcast_to(jnp.max(top[k], axis=0, keepdims=True), (8, BLOCK))

    def add(index):
        row, col = block_at(pairs, index)
        score = scores(index, row).reshape(BLOCK // 8, 8, BLOCK)
        total[col] = total[col] + jnp.sum(jnp.exp2(score - top[col][None]), axis=0)

    over_pairs(count, add, 4)
    lines = []
    for k in range(BLK):
        lse = top[k][0:1] + log2(jnp.sum(total[k], axis=0, keepdims=True))
        lines += [lse[:, :LANES], lse[:, LANES:]]
    out = jnp.concatenate(lines, axis=0)
    out_ref[...] = jnp.broadcast_to(out[None], out_ref.shape)


def last_kernel(log_total, g_ref, pot_ref):
    pot_ref[...] = (log_total - joined_lse(g_ref)) * TO_POT


def smem():
    return pl.BlockSpec(memory_space=pltpu.SMEM)


def vmem():
    return pl.BlockSpec(memory_space=pltpu.VMEM)


def f32(*shape):
    return jax.ShapeDtypeStruct(shape, jnp.float32)


def params():
    return pltpu.CompilerParams(vmem_limit_bytes=VMEM_LIMIT)


def both_ways(x, axes):
    n = x.shape[0]
    groups = [[2 * k for k in range(n)], [2 * k + 1 for k in reversed(range(n))]]
    return lax.all_to_all(x, axes + ("c",), 0, 0, axis_index_groups=groups)


def on_device(source_embed, target_embed, source_labels, target_labels, pair_blocks, pair_count):
    pairs = pair_blocks.reshape(-1)
    count = pair_count.reshape(-1)
    n_src, n_tgt = lax.axis_size(SRC), lax.axis_size(TGT)

    def call(kernel, out_shape, *args, name):
        return pl.pallas_call(
            kernel,
            out_shape=out_shape,
            in_specs=[vmem()] * len(args),
            out_specs=jax.tree.map(lambda _: vmem(), out_shape),
            compiler_params=params(),
            name=name,
        )(*args)

    n_x, n_z = lax.axis_size("x"), lax.axis_size("z")
    part = target_embed.shape[0]
    near, tgt_group = pl.pallas_call(
        first_kernel,
        out_shape=(
            jax.ShapeDtypeStruct((n_z,) + target_embed.shape, jnp.bfloat16),
            f32(16, LANES),
        ),
        in_specs=[vmem(), vmem()],
        out_specs=(pl.BlockSpec(memory_space=pl.ANY), vmem()),
        scratch_shapes=[pltpu.SemaphoreType.DMA((n_z,))],
        compiler_params=params(),
        name="first",
    )(target_embed, target_labels[None])
    near = both_ways(near, ("z",))

    def around(x, axis):
        n = lax.axis_size(axis)
        return [x] + [
            lax.ppermute(x, axis, [((i + far) % n, i) for i in range(n)]) for far in range(1, n)
        ]

    def join_targets(kernel, out_shape, x, axis, *more, name):
        pieces = around(x, axis)
        return pl.pallas_call(
            kernel,
            out_shape=out_shape,
            in_specs=[smem()] + [vmem()] * (len(pieces) + len(more)),
            out_specs=vmem(),
            scratch_shapes=[pltpu.VMEM((len(pieces), 16, LANES), jnp.float32)],
            compiler_params=params(),
            name=name,
        )(lax.axis_index(axis).reshape(1), *pieces, *more)

    tgt_group = join_targets(pair_kernel, f32(16, LANES), tgt_group, "c", name="pair")
    src_group, src_sq = call(
        source_group_kernel,
        (f32(40, LANES), f32(1, ROWS)),
        source_embed,
        source_labels[None],
        name="source_group",
    )
    stats = join_targets(
        near_kernel, f32(n_z, 48, LANES), tgt_group, "y", src_group, name="near"
    )
    near, stats = lax.optimization_barrier((near, stats))

    pieces = around(near, "x")
    stats = lax.all_to_all(stats, "z", 0, 0)
    stats = call(
        functools.partial(middle_kernel, part * n_x), f32(n_x, 72, LANES), stats, name="middle"
    )
    stats = lax.all_to_all(stats, "x", 0, 0)
    label_cost, xa = call(
        functools.partial(label_kernel, part),
        (f32(CLASSES, CLASSES), jax.ShapeDtypeStruct((16, ROWS), jnp.bfloat16)),
        stats,
        src_sq,
        source_labels[None],
        name="label",
    )

    tall = pltpu.VMEM((ROWS, LANES), jnp.float32)
    wide = pltpu.VMEM((BLK, 8, BLOCK), jnp.float32)
    log_src = math.log2(ROWS * n_src)
    log_tgt = math.log2(ROWS * n_tgt)
    tiles, sent = pl.pallas_call(
        functools.partial(cost_kernel, n_x),
        out_shape=(f32(MAXP, BLOCK, BLOCK), f32(n_tgt, CHUNKS, LANES)),
        in_specs=[smem()] * 3 + [vmem()] * (3 + n_x),
        out_specs=(vmem(), vmem()),
        scratch_shapes=[
            pltpu.VMEM((WIDTH, ROWS), jnp.bfloat16),
            pltpu.VMEM((16, ROWS), jnp.bfloat16),
            tall,
            tall,
        ],
        compiler_params=params(),
        name="cost_rows",
    )(
        pairs,
        count,
        jnp.stack([lax.axis_index("x"), lax.axis_index("c")]),
        xa,
        source_embed.T,
        *pieces,
        target_labels[None],
    )

    def columns(got):
        return pl.pallas_call(
            functools.partial(col_kernel, log_tgt),
            out_shape=(f32(n_src, CHUNKS, LANES), f32(CHUNKS, LANES)),
            in_specs=[smem(), smem(), vmem(), vmem()],
            out_specs=(vmem(), vmem()),
            scratch_shapes=[tall, wide, wide],
            compiler_params=params(),
            name="columns",
        )(pairs, count, tiles, got)

    def rows(got):
        return pl.pallas_call(
            functools.partial(row_kernel, log_src),
            out_shape=f32(n_tgt, CHUNKS, LANES),
            in_specs=[smem(), smem(), vmem(), vmem()],
            out_specs=vmem(),
            scratch_shapes=[pltpu.VMEM((CHUNKS, LANES), jnp.float32), tall, tall],
            compiler_params=params(),
            name="rows",
        )(pairs, count, tiles, got)

    sent, _ = columns(lax.all_to_all(sent, TGT, 0, 0))
    sent = rows(both_ways(sent, SRC))
    sent, src_pot = columns(lax.all_to_all(sent, TGT, 0, 0))
    tgt_pot = pl.pallas_call(
        functools.partial(last_kernel, log_src),
        out_shape=f32(CHUNKS, LANES),
        in_specs=[vmem()],
        out_specs=vmem(),
        compiler_params=params(),
        name="last",
    )(both_ways(sent, SRC))
    return (src_pot.reshape(-1), tgt_pot.reshape(-1), label_cost)


def solution(mesh):
    fine = Mesh(np.asarray(mesh.devices).reshape(8, 4, 4, 2), SRC + TGT)
    return jax.shard_map(
        on_device,
        mesh=fine,
        in_specs=(
            P(None, SRC),
            P(SRC, TGT),
            P(SRC),
            P(TGT),
            P(SRC, TGT, None, None),
            P(SRC, TGT),
        ),
        out_specs=(P(SRC), P(TGT), P()),
        check_vma=False,
    )
```

```python
import functools
import math

import jax
import jax.numpy as jnp
import numpy as np
from jax import lax
from jax.experimental import pallas as pl
from jax.experimental.pallas import tpu as pltpu
from jax.sharding import Mesh, PartitionSpec as P

CLASSES = 4
BLOCK = 256
ROWS = 2048
BLK = ROWS // BLOCK
LANES = 128
CHUNKS = ROWS // LANES
MAXP = 24
UNROLL = 4
WIDTH = 512

EPSILON = 0.05
LOWEST = -1e30
LOG2E = 1.0 / math.log(2.0)
TO_LOG2 = LOG2E / EPSILON
TO_POT = EPSILON / LOG2E

SRC = ("z", "x")
TGT = ("y", "c")
VMEM_LIMIT = 24 * 1024 * 1024
FULL_VMEM = 64 * 1024 * 1024 - 32 * 1024


def log2(x):
    return jnp.log(x) * LOG2E


def repeated_onehot(labels):
    row_id = lax.broadcasted_iota(jnp.int32, (16, 1), 0)
    return jnp.where(row_id < 12, jnp.where(labels == row_id % CLASSES, 1.0, 0.0), 0.0)


def across(onehot, values):
    return lax.dot_general(
        onehot, values, (((1,), (1,)), ((), ())), preferred_element_type=jnp.float32
    )


def class_group(values, onehot, counts):
    part = lax.broadcasted_iota(jnp.int32, (16, 1), 0) // CLASSES
    wide = values.astype(jnp.float32)
    mean = across(onehot, values) / counts
    hi, mid, lo = three_parts(mean)
    parts = jnp.where(
        part == 0, hi, jnp.where(part == 1, mid, jnp.where(part == 2, lo, 0.0))
    ).astype(jnp.bfloat16)
    center = lax.dot_general(
        parts, onehot, (((0,), (0,)), ((), ())), preferred_element_type=jnp.float32
    )
    centered = wide - center
    hi, mid, lo = three_parts(centered * centered)
    spread = sum(across(onehot, p.astype(jnp.bfloat16)) for p in (hi, mid, lo))
    return jnp.where(part == 0, mean, spread)[:8], wide


def first_kernel(embed, labels, near_ref, out_ref, sems):
    copies = [
        pltpu.make_async_copy(embed, near_ref.at[k], sems.at[k]) for k in range(near_ref.shape[0])
    ]
    for copy in copies:
        copy.start()
    onehot = repeated_onehot(labels[...])
    counts = jnp.maximum(jnp.sum(onehot, axis=1, keepdims=True), 1.0)
    group, _ = class_group(embed[...], onehot.astype(jnp.bfloat16), counts)
    out_ref[...] = jnp.zeros(out_ref.shape, jnp.float32)
    out_ref[0:8, 0 : group.shape[1]] = group
    out_ref[8:16, :] = jnp.broadcast_to(counts[:8], (8, LANES))
    for copy in copies:
        copy.wait()


def source_group_kernel(embed, labels, out_ref, sq_ref):
    onehot = repeated_onehot(labels[...])
    counts = jnp.maximum(jnp.sum(onehot, axis=1, keepdims=True), 1.0)
    onehot = onehot.astype(jnp.bfloat16)
    sq = jnp.zeros((1, ROWS), jnp.float32)
    for c in range(WIDTH // LANES):
        group, wide = class_group(embed[c * LANES : (c + 1) * LANES, :], onehot, counts)
        out_ref[8 * c : 8 * c + 8, :] = group
        sq = sq + jnp.sum(wide * wide, axis=0, keepdims=True)
    out_ref[32:40, :] = jnp.broadcast_to(counts[:8], (8, LANES))
    sq_ref[...] = sq


def joined_counts(counts):
    total = functools.reduce(jnp.add, counts)
    return total, [c / total for c in counts]


def joined_group(groups, counts, shares):
    row_id = lax.broadcasted_iota(jnp.int32, (8, LANES), 0)
    mean = functools.reduce(jnp.add, [g * w for g, w in zip(groups, shares)])
    between = functools.reduce(
        jnp.add, [(g - mean) * (g - mean) * c for g, c in zip(groups, counts)]
    )
    spread = functools.reduce(jnp.add, groups) + pltpu.roll(between, 4, 0)
    return jnp.where(row_id < CLASSES, mean, spread)


def target_joined(place, pieces, slots):
    n = len(pieces)
    for far, piece in enumerate(pieces):
        slots[lax.rem(place[0] + far, n)] = piece[...]
    counts = [slots[k, 8:16, :] for k in range(n)]
    total, shares = joined_counts(counts)
    return joined_group([slots[k, 0:8, :] for k in range(n)], counts, shares), total


def pair_kernel(place, *args):
    pieces, (out_ref, slots) = args[:-2], args[-2:]
    group, total = target_joined(place, pieces, slots)
    out_ref[0:8, :] = group
    out_ref[8:16, :] = total


def near_kernel(place, *args):
    pieces, (src_group, out_ref, slots) = args[:-3], args[-3:]
    group, total = target_joined(place, pieces, slots)
    row_id = lax.broadcasted_iota(jnp.int32, (8, LANES), 0)
    group = jnp.where(row_id < CLASSES, group, group / total)
    for k in range(out_ref.shape[0]):
        out_ref[k, 0:40, :] = src_group[...]
        out_ref[k, 40:48, :] = group


def source_joined(got):
    peers = got.shape[0]
    counts = [got[k, 32:40, :] for k in range(peers)]
    total, shares = joined_counts(counts)
    groups = [
        joined_group([got[k, 8 * c : 8 * c + 8, :] for k in range(peers)], counts, shares)
        for c in range(WIDTH // LANES)
    ]
    return groups, total


def middle_kernel(width, got, out_ref):
    groups, total = source_joined(got)
    each = LANES // width
    for c in range(WIDTH // LANES):
        tgt = got[each * c, 40:48, :]
        for k in range(1, each):
            tgt = tgt + pltpu.roll(got[each * c + k, 40:48, :], k * width, 1)
        for k in range(out_ref.shape[0]):
            out_ref[k, 8 * c : 8 * c + 8, :] = groups[c]
            out_ref[k, 40 + 8 * c : 48 + 8 * c, :] = tgt
    for k in range(out_ref.shape[0]):
        out_ref[k, 32:40, :] = total


def label_rows(part, got, src_sq, src_lab, label_ref, xa_ref):
    groups, total = source_joined(got)
    row_id = lax.broadcasted_iota(jnp.int32, (8, LANES), 0)
    lane_id = lax.broadcasted_iota(jnp.int32, (8, LANES), 1)
    sides = ([], [])
    for c, group in enumerate(groups):
        at = slice(40 + 8 * c, 48 + 8 * c)
        tgt = got[0, at, :]
        for k in range(1, got.shape[0]):
            tgt = tgt + pltpu.roll(got[k, at, :], k * part, 1)
        for side, stat in zip(sides, (jnp.where(row_id < CLASSES, group, group / total), tgt)):
            side.append(jnp.where(row_id < CLASSES, stat, jnp.sqrt(stat + 1e-06)))

    def distances(one, other):
        out = jnp.zeros((8, LANES), jnp.float32)
        for k in range(CLASSES):
            far = jnp.zeros((8, LANES), jnp.float32)
            for g, h in zip(one, other):
                gap = g - jnp.where(row_id < CLASSES, h[k : k + 1], h[CLASSES + k : CLASSES + k + 1])
                far = far + gap * gap
            far = far + pltpu.roll(far, 4, 0)
            out = jnp.where(lane_id == k, jnp.sum(far, axis=1, keepdims=True), out)
        return out

    label_ref[...] = distances(*sides)[:CLASSES, :CLASSES]
    by_target = distances(*sides[::-1])
    by_target = jnp.concatenate([by_target, by_target], axis=0)
    row_id = lax.broadcasted_iota(jnp.int32, (16, 1), 0)
    part_id = row_id // CLASSES
    labels = src_lab[...]
    u = jnp.broadcast_to(src_sq[...], (16, ROWS))
    for a in range(CLASSES):
        u = u + jnp.where(labels == a, by_target[:, a : a + 1], 0.0)
    hi, mid, lo = three_parts(-0.5 * u)
    ones = jnp.where(row_id < 15, 1.0, 0.0)
    xa_ref[...] = jnp.where(
        part_id == 0, hi, jnp.where(part_id == 1, mid, jnp.where(part_id == 2, lo, ones))
    ).astype(jnp.bfloat16)


def three_parts(v):
    hi = v.astype(jnp.bfloat16).astype(jnp.float32)
    rest = v - hi
    mid = rest.astype(jnp.bfloat16).astype(jnp.float32)
    return hi, mid, rest - mid


def joined_lse(g_ref):
    g = g_ref[...]
    top = jnp.max(g, axis=0)
    return top + log2(jnp.sum(jnp.exp2(g - top[None]), axis=0))


def row_finish(top, total, out_ref):
    lines = []
    for k in range(CHUNKS):
        at = pl.ds(k * LANES, LANES)
        lse = top[at, :] + log2(jnp.sum(total[at, :], axis=1, keepdims=True))
        lines.append(lse.T[0:1, :])
    line = jnp.concatenate(lines, axis=0)
    out_ref[...] = jnp.broadcast_to(line[None], out_ref.shape)


def widen_top(top):
    for k in range(CHUNKS):
        at = pl.ds(k * LANES, LANES)
        top[at, :] = jnp.broadcast_to(jnp.max(top[at, :], axis=1, keepdims=True), (LANES, LANES))


def over_pairs(count, body, unroll):
    def several(step, _):
        for k in range(unroll):
            body(step * unroll + k)
        return 0

    steps = (count[0] + UNROLL - 1) // UNROLL * (UNROLL // unroll)
    lax.fori_loop(0, steps, several, 0)


def block_at(pairs, index):
    row = pl.multiple_of(pairs[2 * index] * BLOCK, BLOCK)
    return row, pairs[2 * index + 1]


def cost_kernel(n_x, n_f, pairs, count, place, got, src_sq, src_lab, xt, *args):
    pieces, (tgt_lab, label_ref, tiles, out_ref, xa, y, ya, top, total) = args[:n_x], args[n_x:]
    label_rows(n_f, got, src_sq, src_lab, label_ref, xa)
    row_id = lax.broadcasted_iota(jnp.int32, (16, 1), 0)
    part = row_id // CLASSES
    cls = row_id % CLASSES

    tgt_sq = jnp.zeros((16, ROWS), jnp.float32)
    for far, piece in enumerate(pieces):
        at = lax.rem(place[0] + far, n_x)
        for k in range(piece.shape[0]):
            z = k + place[1] * (piece.shape[0] - 1 - 2 * k)
            y[pl.ds(pl.multiple_of((z * n_x + at) * 16, 16), 16), :] = piece[k]
            v = piece[k].astype(jnp.float32)
            tgt_sq = tgt_sq + v * v

    hi, mid, lo = three_parts(-0.5 * jnp.sum(tgt_sq, axis=0, keepdims=True))
    onehot = jnp.where(tgt_lab[...] == cls, 1.0, 0.0)
    ya[...] = jnp.where(
        part < 3,
        onehot,
        jnp.where(cls == 0, hi, jnp.where(cls == 1, mid, jnp.where(cls == 2, lo, 0.0))),
    ).astype(jnp.bfloat16)

    top[...] = jnp.full(top.shape, LOWEST, jnp.float32)
    total[...] = jnp.zeros(total.shape, jnp.float32)

    def build(index):
        row, col = block_at(pairs, index)
        rows = pl.ds(row, BLOCK)
        cols = pl.ds(pl.multiple_of(col * BLOCK, BLOCK), BLOCK)
        cross = jnp.dot(xt[rows, :], y[:, cols], preferred_element_type=jnp.float32)
        extra = lax.dot_general(
            xa[:, rows], ya[:, cols], (((0,), (0,)), ((), ())), preferred_element_type=jnp.float32
        )
        tile = (cross + extra) * (2.0 * TO_LOG2) + jnp.where(index < count[0], 0.0, LOWEST)
        tiles[index] = tile
        top[rows, :] = jnp.maximum(top[rows, :], jnp.maximum(tile[:, :LANES], tile[:, LANES:]))

    over_pairs(count, build, 4)
    widen_top(top)

    def add(index):
        row, _ = block_at(pairs, index)
        rows = pl.ds(row, BLOCK)
        high = top[rows, :]
        left = jnp.exp2(tiles[index, :, :LANES] - high)
        right = jnp.exp2(tiles[index, :, LANES:] - high)
        total[rows, :] = total[rows, :] + (left + right)

    over_pairs(count, add, 4)
    row_finish(top, total, out_ref)


def row_kernel(log_total, pairs, count, tiles, g_ref, out_ref, pot, top, total):
    pot[...] = log_total - joined_lse(g_ref)
    top[...] = jnp.full(top.shape, LOWEST, jnp.float32)
    total[...] = jnp.zeros(total.shape, jnp.float32)

    def scores(index, col):
        left = tiles[index, :, :LANES] + pot[pl.ds(2 * col, 1), :]
        right = tiles[index, :, LANES:] + pot[pl.ds(2 * col + 1, 1), :]
        return left, right

    def highest(index):
        row, col = block_at(pairs, index)
        rows = pl.ds(row, BLOCK)
        left, right = scores(index, col)
        top[rows, :] = jnp.maximum(top[rows, :], jnp.maximum(left, right))

    over_pairs(count, highest, 4)
    widen_top(top)

    def add(index):
        row, col = block_at(pairs, index)
        rows = pl.ds(row, BLOCK)
        left, right = scores(index, col)
        high = top[rows, :]
        total[rows, :] = total[rows, :] + (jnp.exp2(left - high) + jnp.exp2(right - high))

    over_pairs(count, add, 4)
    row_finish(top, total, out_ref)


def col_kernel(log_total, pairs, count, tiles, g_ref, out_ref, pot_ref, pot, top, total):
    line = log_total - joined_lse(g_ref)
    pot_ref[...] = line * TO_POT
    for k in range(CHUNKS):
        pot[pl.ds(k * LANES, LANES), :] = jnp.broadcast_to(line[k : k + 1, :], (LANES, LANES)).T
    top[...] = jnp.full(top.shape, LOWEST, jnp.float32)
    total[...] = jnp.zeros(total.shape, jnp.float32)

    def scores(index, row):
        rows = pl.ds(row, BLOCK)
        high = pot[rows, :]
        tile = tiles[index]
        return tile + jnp.concatenate([high, high], axis=1)

    def highest(index):
        row, col = block_at(pairs, index)
        score = scores(index, row)
        top[col] = jnp.maximum(top[col], jnp.max(score.reshape(BLOCK // 8, 8, BLOCK), axis=0))

    over_pairs(count, highest, 4)
    for k in range(BLK):
        top[k] = jnp.broadcast_to(jnp.max(top[k], axis=0, keepdims=True), (8, BLOCK))

    def add(index):
        row, col = block_at(pairs, index)
        score = scores(index, row).reshape(BLOCK // 8, 8, BLOCK)
        total[col] = total[col] + jnp.sum(jnp.exp2(score - top[col][None]), axis=0)

    over_pairs(count, add, 4)
    lines = []
    for k in range(BLK):
        lse = top[k][0:1] + log2(jnp.sum(total[k], axis=0, keepdims=True))
        lines += [lse[:, :LANES], lse[:, LANES:]]
    out = jnp.concatenate(lines, axis=0)
    out_ref[...] = jnp.broadcast_to(out[None], out_ref.shape)


def last_kernel(log_total, g_ref, pot_ref):
    pot_ref[...] = (log_total - joined_lse(g_ref)) * TO_POT


def smem():
    return pl.BlockSpec(memory_space=pltpu.SMEM)


def vmem():
    return pl.BlockSpec(memory_space=pltpu.VMEM)


def f32(*shape):
    return jax.ShapeDtypeStruct(shape, jnp.float32)


def params(limit=VMEM_LIMIT):
    return pltpu.CompilerParams(vmem_limit_bytes=limit)


def both_ways(x, axes):
    n = x.shape[0]
    groups = [[2 * k for k in range(n)], [2 * k + 1 for k in reversed(range(n))]]
    return lax.all_to_all(x, axes + ("c",), 0, 0, axis_index_groups=groups)


def on_device(source_embed, target_embed, source_labels, target_labels, pair_blocks, pair_count):
    pairs = pair_blocks.reshape(-1)
    count = pair_count.reshape(-1)
    n_src, n_tgt = lax.axis_size(SRC), lax.axis_size(TGT)

    def call(kernel, out_shape, *args, name):
        return pl.pallas_call(
            kernel,
            out_shape=out_shape,
            in_specs=[vmem()] * len(args),
            out_specs=jax.tree.map(lambda _: vmem(), out_shape),
            compiler_params=params(),
            name=name,
        )(*args)

    n_x, n_z = lax.axis_size("x"), lax.axis_size("z")
    part = target_embed.shape[0]
    near, tgt_group = pl.pallas_call(
        first_kernel,
        out_shape=(
            jax.ShapeDtypeStruct((n_z,) + target_embed.shape, jnp.bfloat16),
            f32(16, LANES),
        ),
        in_specs=[vmem(), vmem()],
        out_specs=(pl.BlockSpec(memory_space=pl.ANY), vmem()),
        scratch_shapes=[pltpu.SemaphoreType.DMA((n_z,))],
        compiler_params=params(FULL_VMEM),
        name="first",
    )(target_embed, target_labels[None])
    near = both_ways(near, ("z",))

    def around(x, axis):
        n = lax.axis_size(axis)
        return [x] + [
            lax.ppermute(x, axis, [((i + far) % n, i) for i in range(n)]) for far in range(1, n)
        ]

    def join_targets(kernel, out_shape, x, axis, *more, name):
        pieces = around(x, axis)
        return pl.pallas_call(
            kernel,
            out_shape=out_shape,
            in_specs=[smem()] + [vmem()] * (len(pieces) + len(more)),
            out_specs=vmem(),
            scratch_shapes=[pltpu.VMEM((len(pieces), 16, LANES), jnp.float32)],
            compiler_params=params(),
            name=name,
        )(lax.axis_index(axis).reshape(1), *pieces, *more)

    tgt_group = join_targets(pair_kernel, f32(16, LANES), tgt_group, "c", name="pair")
    src_group, src_sq = call(
        source_group_kernel,
        (f32(40, LANES), f32(1, ROWS)),
        source_embed,
        source_labels[None],
        name="source_group",
    )
    stats = join_targets(
        near_kernel, f32(n_z, 48, LANES), tgt_group, "y", src_group, name="near"
    )
    near, stats = lax.optimization_barrier((near, stats))

    pieces = around(near, "x")
    stats = lax.all_to_all(stats, "z", 0, 0)
    stats = call(
        functools.partial(middle_kernel, part * n_x), f32(n_x, 72, LANES), stats, name="middle"
    )
    stats = lax.all_to_all(stats, "x", 0, 0)
    tall = pltpu.VMEM((ROWS, LANES), jnp.float32)
    wide = pltpu.VMEM((BLK, 8, BLOCK), jnp.float32)
    log_src = math.log2(ROWS * n_src)
    log_tgt = math.log2(ROWS * n_tgt)
    label_cost, tiles, sent = pl.pallas_call(
        functools.partial(cost_kernel, n_x, part),
        out_shape=(
            f32(CLASSES, CLASSES),
            f32(MAXP, BLOCK, BLOCK),
            f32(n_tgt, CHUNKS, LANES),
        ),
        in_specs=[smem()] * 3 + [vmem()] * (5 + n_x),
        out_specs=(vmem(), vmem(), vmem()),
        scratch_shapes=[
            pltpu.VMEM((16, ROWS), jnp.bfloat16),
            pltpu.VMEM((WIDTH, ROWS), jnp.bfloat16),
            pltpu.VMEM((16, ROWS), jnp.bfloat16),
            tall,
            tall,
        ],
        compiler_params=params(),
        name="cost_rows",
    )(
        pairs,
        count,
        jnp.stack([lax.axis_index("x"), lax.axis_index("c")]),
        stats,
        src_sq,
        source_labels[None],
        source_embed.T,
        *pieces,
        target_labels[None],
    )

    def columns(got):
        return pl.pallas_call(
            functools.partial(col_kernel, log_tgt),
            out_shape=(f32(n_src, CHUNKS, LANES), f32(CHUNKS, LANES)),
            in_specs=[smem(), smem(), vmem(), vmem()],
            out_specs=(vmem(), vmem()),
            scratch_shapes=[tall, wide, wide],
            compiler_params=params(),
            name="columns",
        )(pairs, count, tiles, got)

    def rows(got):
        return pl.pallas_call(
            functools.partial(row_kernel, log_src),
            out_shape=f32(n_tgt, CHUNKS, LANES),
            in_specs=[smem(), smem(), vmem(), vmem()],
            out_specs=vmem(),
            scratch_shapes=[pltpu.VMEM((CHUNKS, LANES), jnp.float32), tall, tall],
            compiler_params=params(),
            name="rows",
        )(pairs, count, tiles, got)

    sent, _ = columns(lax.all_to_all(sent, TGT, 0, 0))
    sent = rows(both_ways(sent, SRC))
    sent, src_pot = columns(lax.all_to_all(sent, TGT, 0, 0))
    tgt_pot = pl.pallas_call(
        functools.partial(last_kernel, log_src),
        out_shape=f32(CHUNKS, LANES),
        in_specs=[vmem()],
        out_specs=vmem(),
        compiler_params=params(),
        name="last",
    )(both_ways(sent, SRC))
    return (src_pot.reshape(-1), tgt_pot.reshape(-1), label_cost)


def solution(mesh):
    fine = Mesh(np.asarray(mesh.devices).reshape(8, 4, 4, 2), SRC + TGT)
    return jax.shard_map(
        on_device,
        mesh=fine,
        in_specs=(
            P(None, SRC),
            P(SRC, TGT),
            P(SRC),
            P(TGT),
            P(SRC, TGT, None, None),
            P(SRC, TGT),
        ),
        out_specs=(P(SRC), P(TGT), P()),
        check_vma=False,
    )
```

```python
import functools
import math

import jax
import jax.numpy as jnp
import numpy as np
from jax import lax
from jax.experimental import pallas as pl
from jax.experimental.pallas import tpu as pltpu
from jax.sharding import Mesh, PartitionSpec as P

CLASSES = 4
BLOCK = 256
ROWS = 2048
BLK = ROWS // BLOCK
LANES = 128
CHUNKS = ROWS // LANES
MAXP = 24
UNROLL = 4
WIDTH = 512

EPSILON = 0.05
LOWEST = -1e30
LOG2E = 1.0 / math.log(2.0)
TO_LOG2 = LOG2E / EPSILON
TO_POT = EPSILON / LOG2E

SRC = ("z", "x")
TGT = ("y", "c")
VMEM_LIMIT = 24 * 1024 * 1024
FULL_VMEM = 64 * 1024 * 1024 - 32 * 1024


def log2(x):
    return jnp.log(x) * LOG2E


def repeated_onehot(labels):
    row_id = lax.broadcasted_iota(jnp.int32, (16, 1), 0)
    return jnp.where(row_id < 12, jnp.where(labels == row_id % CLASSES, 1.0, 0.0), 0.0)


def across(onehot, values):
    return lax.dot_general(
        onehot, values, (((1,), (1,)), ((), ())), preferred_element_type=jnp.float32
    )


def class_group(values, onehot, counts):
    part = lax.broadcasted_iota(jnp.int32, (16, 1), 0) // CLASSES
    wide = values.astype(jnp.float32)
    mean = across(onehot, values) / counts
    hi, mid, lo = three_parts(mean)
    parts = jnp.where(
        part == 0, hi, jnp.where(part == 1, mid, jnp.where(part == 2, lo, 0.0))
    ).astype(jnp.bfloat16)
    center = lax.dot_general(
        parts, onehot, (((0,), (0,)), ((), ())), preferred_element_type=jnp.float32
    )
    centered = wide - center
    hi, mid, lo = three_parts(centered * centered)
    spread = sum(across(onehot, p.astype(jnp.bfloat16)) for p in (hi, mid, lo))
    return jnp.where(part == 0, mean, spread)[:8], wide


def first_kernel(embed, labels, near_ref, out_ref, sems):
    copies = [
        pltpu.make_async_copy(embed, near_ref.at[k], sems.at[k]) for k in range(near_ref.shape[0])
    ]
    for copy in copies:
        copy.start()
    onehot = repeated_onehot(labels[...])
    counts = jnp.maximum(jnp.sum(onehot, axis=1, keepdims=True), 1.0)
    group, _ = class_group(embed[...], onehot.astype(jnp.bfloat16), counts)
    out_ref[...] = jnp.zeros(out_ref.shape, jnp.float32)
    out_ref[0:8, 0 : group.shape[1]] = group
    out_ref[8:16, :] = jnp.broadcast_to(counts[:8], (8, LANES))
    for copy in copies:
        copy.wait()


def lower_lanes():
    return lax.broadcasted_iota(jnp.int32, (8, LANES), 1) < LANES // 2


def source_group_kernel(embed, labels, tgt_group, out_ref, sq_ref):
    onehot = repeated_onehot(labels[...])
    counts = jnp.maximum(jnp.sum(onehot, axis=1, keepdims=True), 1.0)
    onehot = onehot.astype(jnp.bfloat16)
    sq = jnp.zeros((1, ROWS), jnp.float32)
    for c in range(WIDTH // LANES):
        group, wide = class_group(embed[c * LANES : (c + 1) * LANES, :], onehot, counts)
        out_ref[8 * c : 8 * c + 8, :] = group
        sq = sq + jnp.sum(wide * wide, axis=0, keepdims=True)
    out_ref[32:40, :] = jnp.where(lower_lanes(), tgt_group[0:8, :], counts[:8])
    sq_ref[...] = sq


def joined_counts(counts):
    total = functools.reduce(jnp.add, counts)
    return total, [c / total for c in counts]


def joined_group(groups, counts, shares):
    row_id = lax.broadcasted_iota(jnp.int32, (8, LANES), 0)
    mean = functools.reduce(jnp.add, [g * w for g, w in zip(groups, shares)])
    between = functools.reduce(
        jnp.add, [(g - mean) * (g - mean) * c for g, c in zip(groups, counts)]
    )
    spread = functools.reduce(jnp.add, groups) + pltpu.roll(between, 4, 0)
    return jnp.where(row_id < CLASSES, mean, spread)


def source_joined(got):
    peers = got.shape[0]
    half = LANES // 2
    lower = lower_lanes()
    last = [got[k, 32:40, :] for k in range(peers)]
    targets = [jnp.where(lower, g, 0.0) for g in last]
    counts = [jnp.where(lower, pltpu.roll(g, half, 1), g) for g in last]
    total, shares = joined_counts(counts)
    groups = [
        joined_group([got[k, 8 * c : 8 * c + 8, :] for k in range(peers)], counts, shares)
        for c in range(WIDTH // LANES)
    ]
    return groups, total, targets


def side_by_side(targets, width):
    out = targets[0]
    for k, target in enumerate(targets[1:]):
        out = out + pltpu.roll(target, (k + 1) * width, 1)
    return out


def near_kernel(part, place, *args):
    pieces, (tgt_group, src_ref, tgt_ref, slots) = args[:-4], args[-4:]
    for far, piece in enumerate(pieces):
        slots[lax.rem(place[0] + far, len(pieces))] = piece[...]
    groups, total, targets = source_joined(slots)
    for c, group in enumerate(groups):
        src_ref[8 * c : 8 * c + 8, :] = group
    src_ref[32:40, :] = total
    target = jnp.where(lower_lanes(), side_by_side(targets, part), tgt_group[8:16, :])
    for k in range(tgt_ref.shape[0]):
        tgt_ref[k] = target


def middle_kernel(got, src, out_ref):
    half = LANES // 2
    lower = lower_lanes()
    row_id = lax.broadcasted_iota(jnp.int32, (8, LANES), 0)
    each = [got[k] for k in range(got.shape[0])]
    counts = [jnp.where(lower, pltpu.roll(g, half, 1), g) for g in each]
    total, shares = joined_counts(counts)
    group = joined_group([jnp.where(lower, g, 0.0) for g in each], counts, shares)
    group = jnp.where(row_id < CLASSES, group, group / total)
    last = jnp.where(lower, group, src[32:40, :])
    for k in range(out_ref.shape[0]):
        out_ref[k, 0:32, :] = src[0:32, :]
        out_ref[k, 32:40, :] = last


def label_rows(width, got, src_sq, src_lab, label_ref, xa_ref):
    groups, total, targets = source_joined(got)
    row_id = lax.broadcasted_iota(jnp.int32, (8, LANES), 0)
    lane_id = lax.broadcasted_iota(jnp.int32, (8, LANES), 1)
    each = LANES // width
    sides = ([], [])
    for c, group in enumerate(groups):
        tgt = side_by_side(targets[each * c : each * c + each], width)
        for side, stat in zip(sides, (jnp.where(row_id < CLASSES, group, group / total), tgt)):
            side.append(jnp.where(row_id < CLASSES, stat, jnp.sqrt(stat + 1e-06)))

    def distances(one, other):
        out = jnp.zeros((8, LANES), jnp.float32)
        for k in range(CLASSES):
            far = jnp.zeros((8, LANES), jnp.float32)
            for g, h in zip(one, other):
                gap = g - jnp.where(row_id < CLASSES, h[k : k + 1], h[CLASSES + k : CLASSES + k + 1])
                far = far + gap * gap
            far = far + pltpu.roll(far, 4, 0)
            out = jnp.where(lane_id == k, jnp.sum(far, axis=1, keepdims=True), out)
        return out

    label_ref[...] = distances(*sides)[:CLASSES, :CLASSES]
    by_target = distances(*sides[::-1])
    by_target = jnp.concatenate([by_target, by_target], axis=0)
    row_id = lax.broadcasted_iota(jnp.int32, (16, 1), 0)
    part_id = row_id // CLASSES
    labels = src_lab[...]
    u = jnp.broadcast_to(src_sq[...], (16, ROWS))
    for a in range(CLASSES):
        u = u + jnp.where(labels == a, by_target[:, a : a + 1], 0.0)
    hi, mid, lo = three_parts(-0.5 * u)
    ones = jnp.where(row_id < 15, 1.0, 0.0)
    xa_ref[...] = jnp.where(
        part_id == 0, hi, jnp.where(part_id == 1, mid, jnp.where(part_id == 2, lo, ones))
    ).astype(jnp.bfloat16)


def three_parts(v):
    hi = v.astype(jnp.bfloat16).astype(jnp.float32)
    rest = v - hi
    mid = rest.astype(jnp.bfloat16).astype(jnp.float32)
    return hi, mid, rest - mid


def joined_lse(g_ref):
    g = g_ref[...]
    top = jnp.max(g, axis=0)
    return top + log2(jnp.sum(jnp.exp2(g - top[None]), axis=0))


def row_finish(top, total, out_ref):
    lines = []
    for k in range(CHUNKS):
        at = pl.ds(k * LANES, LANES)
        lse = top[at, :] + log2(jnp.sum(total[at, :], axis=1, keepdims=True))
        lines.append(lse.T[0:1, :])
    line = jnp.concatenate(lines, axis=0)
    out_ref[...] = jnp.broadcast_to(line[None], out_ref.shape)


def widen_top(top):
    for k in range(CHUNKS):
        at = pl.ds(k * LANES, LANES)
        top[at, :] = jnp.broadcast_to(jnp.max(top[at, :], axis=1, keepdims=True), (LANES, LANES))


def over_pairs(count, body, unroll):
    def several(step, _):
        for k in range(unroll):
            body(step * unroll + k)
        return 0

    steps = (count[0] + UNROLL - 1) // UNROLL * (UNROLL // unroll)
    lax.fori_loop(0, steps, several, 0)


def block_at(pairs, index):
    row = pl.multiple_of(pairs[2 * index] * BLOCK, BLOCK)
    return row, pairs[2 * index + 1]


def cost_kernel(n_x, n_f, pairs, count, place, got, src_sq, src_lab, xt, *args):
    pieces, (tgt_lab, label_ref, tiles, out_ref, xa, y, ya, top, total) = args[:n_x], args[n_x:]
    label_rows(n_f, got, src_sq, src_lab, label_ref, xa)
    row_id = lax.broadcasted_iota(jnp.int32, (16, 1), 0)
    part = row_id // CLASSES
    cls = row_id % CLASSES

    tgt_sq = jnp.zeros((16, ROWS), jnp.float32)
    for far, piece in enumerate(pieces):
        at = lax.rem(place[0] + far, n_x)
        for k in range(piece.shape[0]):
            z = k + place[1] * (piece.shape[0] - 1 - 2 * k)
            y[pl.ds(pl.multiple_of((z * n_x + at) * 16, 16), 16), :] = piece[k]
            v = piece[k].astype(jnp.float32)
            tgt_sq = tgt_sq + v * v

    hi, mid, lo = three_parts(-0.5 * jnp.sum(tgt_sq, axis=0, keepdims=True))
    onehot = jnp.where(tgt_lab[...] == cls, 1.0, 0.0)
    ya[...] = jnp.where(
        part < 3,
        onehot,
        jnp.where(cls == 0, hi, jnp.where(cls == 1, mid, jnp.where(cls == 2, lo, 0.0))),
    ).astype(jnp.bfloat16)

    top[...] = jnp.full(top.shape, LOWEST, jnp.float32)
    total[...] = jnp.zeros(total.shape, jnp.float32)

    def build(index):
        row, col = block_at(pairs, index)
        rows = pl.ds(row, BLOCK)
        cols = pl.ds(pl.multiple_of(col * BLOCK, BLOCK), BLOCK)
        cross = jnp.dot(xt[rows, :], y[:, cols], preferred_element_type=jnp.float32)
        extra = lax.dot_general(
            xa[:, rows], ya[:, cols], (((0,), (0,)), ((), ())), preferred_element_type=jnp.float32
        )
        tile = (cross + extra) * (2.0 * TO_LOG2) + jnp.where(index < count[0], 0.0, LOWEST)
        tiles[index] = tile
        top[rows, :] = jnp.maximum(top[rows, :], jnp.maximum(tile[:, :LANES], tile[:, LANES:]))

    over_pairs(count, build, 4)
    widen_top(top)

    def add(index):
        row, _ = block_at(pairs, index)
        rows = pl.ds(row, BLOCK)
        high = top[rows, :]
        left = jnp.exp2(tiles[index, :, :LANES] - high)
        right = jnp.exp2(tiles[index, :, LANES:] - high)
        total[rows, :] = total[rows, :] + (left + right)

    over_pairs(count, add, 4)
    row_finish(top, total, out_ref)


def row_kernel(log_total, pairs, count, tiles, g_ref, out_ref, pot, top, total):
    pot[...] = log_total - joined_lse(g_ref)
    top[...] = jnp.full(top.shape, LOWEST, jnp.float32)
    total[...] = jnp.zeros(total.shape, jnp.float32)

    def scores(index, col):
        left = tiles[index, :, :LANES] + pot[pl.ds(2 * col, 1), :]
        right = tiles[index, :, LANES:] + pot[pl.ds(2 * col + 1, 1), :]
        return left, right

    def highest(index):
        row, col = block_at(pairs, index)
        rows = pl.ds(row, BLOCK)
        left, right = scores(index, col)
        top[rows, :] = jnp.maximum(top[rows, :], jnp.maximum(left, right))

    over_pairs(count, highest, 4)
    widen_top(top)

    def add(index):
        row, col = block_at(pairs, index)
        rows = pl.ds(row, BLOCK)
        left, right = scores(index, col)
        high = top[rows, :]
        total[rows, :] = total[rows, :] + (jnp.exp2(left - high) + jnp.exp2(right - high))

    over_pairs(count, add, 4)
    row_finish(top, total, out_ref)


def col_kernel(log_total, pairs, count, tiles, g_ref, out_ref, pot_ref, pot, top, total):
    line = log_total - joined_lse(g_ref)
    pot_ref[...] = line * TO_POT
    for k in range(CHUNKS):
        pot[pl.ds(k * LANES, LANES), :] = jnp.broadcast_to(line[k : k + 1, :], (LANES, LANES)).T
    top[...] = jnp.full(top.shape, LOWEST, jnp.float32)
    total[...] = jnp.zeros(total.shape, jnp.float32)

    def scores(index, row):
        rows = pl.ds(row, BLOCK)
        high = pot[rows, :]
        tile = tiles[index]
        return tile + jnp.concatenate([high, high], axis=1)

    def highest(index):
        row, col = block_at(pairs, index)
        score = scores(index, row)
        top[col] = jnp.maximum(top[col], jnp.max(score.reshape(BLOCK // 8, 8, BLOCK), axis=0))

    over_pairs(count, highest, 4)
    for k in range(BLK):
        top[k] = jnp.broadcast_to(jnp.max(top[k], axis=0, keepdims=True), (8, BLOCK))

    def add(index):
        row, col = block_at(pairs, index)
        score = scores(index, row).reshape(BLOCK // 8, 8, BLOCK)
        total[col] = total[col] + jnp.sum(jnp.exp2(score - top[col][None]), axis=0)

    over_pairs(count, add, 4)
    lines = []
    for k in range(BLK):
        lse = top[k][0:1] + log2(jnp.sum(total[k], axis=0, keepdims=True))
        lines += [lse[:, :LANES], lse[:, LANES:]]
    out = jnp.concatenate(lines, axis=0)
    out_ref[...] = jnp.broadcast_to(out[None], out_ref.shape)


def last_kernel(log_total, g_ref, pot_ref):
    pot_ref[...] = (log_total - joined_lse(g_ref)) * TO_POT


def smem():
    return pl.BlockSpec(memory_space=pltpu.SMEM)


def vmem():
    return pl.BlockSpec(memory_space=pltpu.VMEM)


def f32(*shape):
    return jax.ShapeDtypeStruct(shape, jnp.float32)


def params(limit=VMEM_LIMIT):
    return pltpu.CompilerParams(vmem_limit_bytes=limit)


def both_ways(x, axes):
    n = x.shape[0]
    groups = [[2 * k for k in range(n)], [2 * k + 1 for k in reversed(range(n))]]
    return lax.all_to_all(x, axes + ("c",), 0, 0, axis_index_groups=groups)


def on_device(source_embed, target_embed, source_labels, target_labels, pair_blocks, pair_count):
    pairs = pair_blocks.reshape(-1)
    count = pair_count.reshape(-1)
    n_src, n_tgt = lax.axis_size(SRC), lax.axis_size(TGT)

    def call(kernel, out_shape, *args, name):
        return pl.pallas_call(
            kernel,
            out_shape=out_shape,
            in_specs=[vmem()] * len(args),
            out_specs=jax.tree.map(lambda _: vmem(), out_shape),
            compiler_params=params(),
            name=name,
        )(*args)

    n_x, n_z = lax.axis_size("x"), lax.axis_size("z")
    part = target_embed.shape[0]
    near, tgt_group = pl.pallas_call(
        first_kernel,
        out_shape=(
            jax.ShapeDtypeStruct((n_z,) + target_embed.shape, jnp.bfloat16),
            f32(16, LANES),
        ),
        in_specs=[vmem(), vmem()],
        out_specs=(pl.BlockSpec(memory_space=pl.ANY), vmem()),
        scratch_shapes=[pltpu.SemaphoreType.DMA((n_z,))],
        compiler_params=params(FULL_VMEM),
        name="first",
    )(target_embed, target_labels[None])
    near = both_ways(near, ("z",))

    def around(x, axis):
        n = lax.axis_size(axis)
        return [x] + [
            lax.ppermute(x, axis, [((i + far) % n, i) for i in range(n)]) for far in range(1, n)
        ]

    src_group, src_sq = call(
        source_group_kernel,
        (f32(40, LANES), f32(1, ROWS)),
        source_embed,
        source_labels[None],
        tgt_group,
        name="source_group",
    )

    near, packets = lax.optimization_barrier((near, around(src_group, "x")))
    pieces = around(near, "x")
    src_group, tgt_near = pl.pallas_call(
        functools.partial(near_kernel, part),
        out_shape=(f32(40, LANES), f32(n_tgt, 8, LANES)),
        in_specs=[smem()] + [vmem()] * (n_x + 1),
        out_specs=(vmem(), vmem()),
        scratch_shapes=[pltpu.VMEM((n_x, 40, LANES), jnp.float32)],
        compiler_params=params(),
        name="near",
    )(lax.axis_index("x").reshape(1), *packets, tgt_group)
    tgt_near = lax.all_to_all(tgt_near, TGT, 0, 0)
    stats = call(middle_kernel, f32(n_z, 40, LANES), tgt_near, src_group, name="middle")
    stats = lax.all_to_all(stats, "z", 0, 0)

    tall = pltpu.VMEM((ROWS, LANES), jnp.float32)
    wide = pltpu.VMEM((BLK, 8, BLOCK), jnp.float32)
    log_src = math.log2(ROWS * n_src)
    log_tgt = math.log2(ROWS * n_tgt)
    label_cost, tiles, sent = pl.pallas_call(
        functools.partial(cost_kernel, n_x, part * n_x),
        out_shape=(
            f32(CLASSES, CLASSES),
            f32(MAXP, BLOCK, BLOCK),
            f32(n_tgt, CHUNKS, LANES),
        ),
        in_specs=[smem()] * 3 + [vmem()] * (5 + n_x),
        out_specs=(vmem(), vmem(), vmem()),
        scratch_shapes=[
            pltpu.VMEM((16, ROWS), jnp.bfloat16),
            pltpu.VMEM((WIDTH, ROWS), jnp.bfloat16),
            pltpu.VMEM((16, ROWS), jnp.bfloat16),
            tall,
            tall,
        ],
        compiler_params=params(),
        name="cost_rows",
    )(
        pairs,
        count,
        jnp.stack([lax.axis_index("x"), lax.axis_index("c")]),
        stats,
        src_sq,
        source_labels[None],
        source_embed.T,
        *pieces,
        target_labels[None],
    )

    def columns(got):
        return pl.pallas_call(
            functools.partial(col_kernel, log_tgt),
            out_shape=(f32(n_src, CHUNKS, LANES), f32(CHUNKS, LANES)),
            in_specs=[smem(), smem(), vmem(), vmem()],
            out_specs=(vmem(), vmem()),
            scratch_shapes=[tall, wide, wide],
            compiler_params=params(),
            name="columns",
        )(pairs, count, tiles, got)

    def rows(got):
        return pl.pallas_call(
            functools.partial(row_kernel, log_src),
            out_shape=f32(n_tgt, CHUNKS, LANES),
            in_specs=[smem(), smem(), vmem(), vmem()],
            out_specs=vmem(),
            scratch_shapes=[pltpu.VMEM((CHUNKS, LANES), jnp.float32), tall, tall],
            compiler_params=params(),
            name="rows",
        )(pairs, count, tiles, got)

    sent, _ = columns(lax.all_to_all(sent, TGT, 0, 0))
    sent = rows(both_ways(sent, SRC))
    sent, src_pot = columns(lax.all_to_all(sent, TGT, 0, 0))
    tgt_pot = pl.pallas_call(
        functools.partial(last_kernel, log_src),
        out_shape=f32(CHUNKS, LANES),
        in_specs=[vmem()],
        out_specs=vmem(),
        compiler_params=params(),
        name="last",
    )(both_ways(sent, SRC))
    return (src_pot.reshape(-1), tgt_pot.reshape(-1), label_cost)


def solution(mesh):
    fine = Mesh(np.asarray(mesh.devices).reshape(8, 4, 4, 2), SRC + TGT)
    return jax.shard_map(
        on_device,
        mesh=fine,
        in_specs=(
            P(None, SRC),
            P(SRC, TGT),
            P(SRC),
            P(TGT),
            P(SRC, TGT, None, None),
            P(SRC, TGT),
        ),
        out_specs=(P(SRC), P(TGT), P()),
        check_vma=False,
    )
```

```python
import functools
import math

import jax
import jax.numpy as jnp
import numpy as np
from jax import lax
from jax.experimental import pallas as pl
from jax.experimental.pallas import tpu as pltpu
from jax.sharding import Mesh, PartitionSpec as P

CLASSES = 4
BLOCK = 256
ROWS = 2048
BLK = ROWS // BLOCK
LANES = 128
CHUNKS = ROWS // LANES
MAXP = 24
UNROLL = 4
WIDTH = 512

EPSILON = 0.05
LOWEST = -1e30
LOG2E = 1.0 / math.log(2.0)
TO_LOG2 = LOG2E / EPSILON
TO_POT = EPSILON / LOG2E

SRC = ("z", "x")
TGT = ("y", "c")
VMEM_LIMIT = 24 * 1024 * 1024
FULL_VMEM = 64 * 1024 * 1024 - 32 * 1024


def log2(x):
    return jnp.log(x) * LOG2E


def repeated_onehot(labels):
    row_id = lax.broadcasted_iota(jnp.int32, (16, 1), 0)
    return jnp.where(row_id < 12, jnp.where(labels == row_id % CLASSES, 1.0, 0.0), 0.0)


def across(onehot, values):
    return lax.dot_general(
        onehot, values, (((1,), (1,)), ((), ())), preferred_element_type=jnp.float32
    )


def class_group(values, onehot, counts):
    part = lax.broadcasted_iota(jnp.int32, (16, 1), 0) // CLASSES
    wide = values.astype(jnp.float32)
    mean = across(onehot, values) / counts
    hi, mid, lo = three_parts(mean)
    parts = jnp.where(
        part == 0, hi, jnp.where(part == 1, mid, jnp.where(part == 2, lo, 0.0))
    ).astype(jnp.bfloat16)
    center = lax.dot_general(
        parts, onehot, (((0,), (0,)), ((), ())), preferred_element_type=jnp.float32
    )
    centered = wide - center
    hi, mid, lo = three_parts(centered * centered)
    spread = sum(across(onehot, p.astype(jnp.bfloat16)) for p in (hi, mid, lo))
    return jnp.where(part == 0, mean, spread)[:8], wide


def first_kernel(embed, labels, near_ref, out_ref, sems):
    copies = [
        pltpu.make_async_copy(embed, near_ref.at[k], sems.at[k]) for k in range(near_ref.shape[0])
    ]
    for copy in copies:
        copy.start()
    onehot = repeated_onehot(labels[...])
    counts = jnp.maximum(jnp.sum(onehot, axis=1, keepdims=True), 1.0)
    group, _ = class_group(embed[...], onehot.astype(jnp.bfloat16), counts)
    out_ref[...] = jnp.zeros(out_ref.shape, jnp.float32)
    out_ref[0:8, 0 : group.shape[1]] = group
    out_ref[8:16, :] = jnp.broadcast_to(counts[:8], (8, LANES))
    for copy in copies:
        copy.wait()


def lower_lanes():
    return lax.broadcasted_iota(jnp.int32, (8, LANES), 1) < LANES // 2


def source_group_kernel(embed, labels, tgt_group, out_ref, sq_ref):
    onehot = repeated_onehot(labels[...])
    counts = jnp.maximum(jnp.sum(onehot, axis=1, keepdims=True), 1.0)
    onehot = onehot.astype(jnp.bfloat16)
    sq = jnp.zeros((1, ROWS), jnp.float32)
    for c in range(WIDTH // LANES):
        group, wide = class_group(embed[c * LANES : (c + 1) * LANES, :], onehot, counts)
        out_ref[8 * c : 8 * c + 8, :] = group
        sq = sq + jnp.sum(wide * wide, axis=0, keepdims=True)
    out_ref[32:40, :] = jnp.where(lower_lanes(), tgt_group[0:8, :], counts[:8])
    sq_ref[...] = sq


def joined_counts(counts):
    total = functools.reduce(jnp.add, counts)
    return total, [c / total for c in counts]


def joined_group(groups, counts, shares):
    row_id = lax.broadcasted_iota(jnp.int32, (8, LANES), 0)
    mean = functools.reduce(jnp.add, [g * w for g, w in zip(groups, shares)])
    between = functools.reduce(
        jnp.add, [(g - mean) * (g - mean) * c for g, c in zip(groups, counts)]
    )
    spread = functools.reduce(jnp.add, groups) + pltpu.roll(between, 4, 0)
    return jnp.where(row_id < CLASSES, mean, spread)


def source_joined(got, order=None):
    peers = got.shape[0]
    order = range(peers) if order is None else order
    half = LANES // 2
    lower = lower_lanes()
    last = [got[k, 32:40, :] for k in order]
    targets = [jnp.where(lower, g, 0.0) for g in last]
    counts = [jnp.where(lower, pltpu.roll(g, half, 1), g) for g in last]
    total, shares = joined_counts(counts)
    groups = [
        joined_group([got[k, 8 * c : 8 * c + 8, :] for k in order], counts, shares)
        for c in range(WIDTH // LANES)
    ]
    return groups, total, targets


def side_by_side(targets, width):
    out = targets[0]
    for k, target in enumerate(targets[1:]):
        out = out + pltpu.roll(target, (k + 1) * width, 1)
    return out


def near_kernel(part, place, *args):
    pieces, (tgt_group, src_ref, tgt_ref, slots) = args[:-4], args[-4:]
    for far, piece in enumerate(pieces):
        slots[lax.rem(place[0] + far, len(pieces))] = piece[...]
    groups, total, targets = source_joined(slots)
    for c, group in enumerate(groups):
        src_ref[8 * c : 8 * c + 8, :] = group
    src_ref[32:40, :] = total
    target = jnp.where(lower_lanes(), side_by_side(targets, part), tgt_group[8:16, :])
    for k in range(tgt_ref.shape[0]):
        tgt_ref[k] = target


def middle_kernel(got, src, out_ref):
    half = LANES // 2
    lower = lower_lanes()
    row_id = lax.broadcasted_iota(jnp.int32, (8, LANES), 0)
    each = [got[k] for k in range(got.shape[0])]
    counts = [jnp.where(lower, pltpu.roll(g, half, 1), g) for g in each]
    total, shares = joined_counts(counts)
    group = joined_group([jnp.where(lower, g, 0.0) for g in each], counts, shares)
    group = jnp.where(row_id < CLASSES, group, group / total)
    last = jnp.where(lower, group, src[32:40, :])
    for k in range(out_ref.shape[0]):
        out_ref[k, 0:32, :] = src[0:32, :]
        out_ref[k, 32:40, :] = last


def label_rows(width, core, got, src_sq, src_lab, label_ref, xa_ref):
    peers = got.shape[0]
    groups, total, targets = source_joined(
        got, [k + core * (peers - 1 - 2 * k) for k in range(peers)]
    )
    row_id = lax.broadcasted_iota(jnp.int32, (8, LANES), 0)
    lane_id = lax.broadcasted_iota(jnp.int32, (8, LANES), 1)
    each = LANES // width
    sides = ([], [])
    for c, group in enumerate(groups):
        tgt = side_by_side(targets[each * c : each * c + each], width)
        for side, stat in zip(sides, (jnp.where(row_id < CLASSES, group, group / total), tgt)):
            side.append(jnp.where(row_id < CLASSES, stat, jnp.sqrt(stat + 1e-06)))

    def distances(one, other):
        out = jnp.zeros((8, LANES), jnp.float32)
        for k in range(CLASSES):
            far = jnp.zeros((8, LANES), jnp.float32)
            for g, h in zip(one, other):
                gap = g - jnp.where(row_id < CLASSES, h[k : k + 1], h[CLASSES + k : CLASSES + k + 1])
                far = far + gap * gap
            far = far + pltpu.roll(far, 4, 0)
            out = jnp.where(lane_id == k, jnp.sum(far, axis=1, keepdims=True), out)
        return out

    label_ref[...] = distances(*sides)[:CLASSES, :CLASSES]
    by_target = distances(*sides[::-1])
    by_target = jnp.concatenate([by_target, by_target], axis=0)
    row_id = lax.broadcasted_iota(jnp.int32, (16, 1), 0)
    part_id = row_id // CLASSES
    labels = src_lab[...]
    u = jnp.broadcast_to(src_sq[...], (16, ROWS))
    for a in range(CLASSES):
        u = u + jnp.where(labels == a, by_target[:, a : a + 1], 0.0)
    hi, mid, lo = three_parts(-0.5 * u)
    ones = jnp.where(row_id < 15, 1.0, 0.0)
    xa_ref[...] = jnp.where(
        part_id == 0, hi, jnp.where(part_id == 1, mid, jnp.where(part_id == 2, lo, ones))
    ).astype(jnp.bfloat16)


def three_parts(v):
    hi = v.astype(jnp.bfloat16).astype(jnp.float32)
    rest = v - hi
    mid = rest.astype(jnp.bfloat16).astype(jnp.float32)
    return hi, mid, rest - mid


def joined_lse(g_ref):
    g = g_ref[...]
    top = jnp.max(g, axis=0)
    return top + log2(jnp.sum(jnp.exp2(g - top[None]), axis=0))


def row_finish(top, total, out_ref):
    lines = []
    for k in range(CHUNKS):
        at = pl.ds(k * LANES, LANES)
        lse = top[at, :] + log2(jnp.sum(total[at, :], axis=1, keepdims=True))
        lines.append(lse.T[0:1, :])
    line = jnp.concatenate(lines, axis=0)
    out_ref[...] = jnp.broadcast_to(line[None], out_ref.shape)


def widen_top(top):
    for k in range(CHUNKS):
        at = pl.ds(k * LANES, LANES)
        top[at, :] = jnp.broadcast_to(jnp.max(top[at, :], axis=1, keepdims=True), (LANES, LANES))


def over_pairs(count, body, unroll):
    def several(step, _):
        for k in range(unroll):
            body(step * unroll + k)
        return 0

    steps = (count[0] + UNROLL - 1) // UNROLL * (UNROLL // unroll)
    lax.fori_loop(0, steps, several, 0)


def block_at(pairs, index):
    row = pl.multiple_of(pairs[2 * index] * BLOCK, BLOCK)
    return row, pairs[2 * index + 1]


def cost_kernel(n_x, n_f, pairs, count, place, got, src_sq, src_lab, xt, *args):
    pieces, (tgt_lab, label_ref, tiles, out_ref, xa, y, ya, top, total) = args[:n_x], args[n_x:]
    label_rows(n_f, place[1], got, src_sq, src_lab, label_ref, xa)
    row_id = lax.broadcasted_iota(jnp.int32, (16, 1), 0)
    part = row_id // CLASSES
    cls = row_id % CLASSES

    tgt_sq = jnp.zeros((16, ROWS), jnp.float32)
    for far, piece in enumerate(pieces):
        at = lax.rem(place[0] + far, n_x)
        for k in range(piece.shape[0]):
            z = k + place[1] * (piece.shape[0] - 1 - 2 * k)
            y[pl.ds(pl.multiple_of((z * n_x + at) * 16, 16), 16), :] = piece[k]
            v = piece[k].astype(jnp.float32)
            tgt_sq = tgt_sq + v * v

    hi, mid, lo = three_parts(-0.5 * jnp.sum(tgt_sq, axis=0, keepdims=True))
    onehot = jnp.where(tgt_lab[...] == cls, 1.0, 0.0)
    ya[...] = jnp.where(
        part < 3,
        onehot,
        jnp.where(cls == 0, hi, jnp.where(cls == 1, mid, jnp.where(cls == 2, lo, 0.0))),
    ).astype(jnp.bfloat16)

    top[...] = jnp.full(top.shape, LOWEST, jnp.float32)
    total[...] = jnp.zeros(total.shape, jnp.float32)

    def build(index):
        row, col = block_at(pairs, index)
        rows = pl.ds(row, BLOCK)
        cols = pl.ds(pl.multiple_of(col * BLOCK, BLOCK), BLOCK)
        cross = jnp.dot(xt[rows, :], y[:, cols], preferred_element_type=jnp.float32)
        extra = lax.dot_general(
            xa[:, rows], ya[:, cols], (((0,), (0,)), ((), ())), preferred_element_type=jnp.float32
        )
        tile = (cross + extra) * (2.0 * TO_LOG2) + jnp.where(index < count[0], 0.0, LOWEST)
        tiles[index] = tile
        top[rows, :] = jnp.maximum(top[rows, :], jnp.maximum(tile[:, :LANES], tile[:, LANES:]))

    over_pairs(count, build, 4)
    widen_top(top)

    def add(index):
        row, _ = block_at(pairs, index)
        rows = pl.ds(row, BLOCK)
        high = top[rows, :]
        left = jnp.exp2(tiles[index, :, :LANES] - high)
        right = jnp.exp2(tiles[index, :, LANES:] - high)
        total[rows, :] = total[rows, :] + (left + right)

    over_pairs(count, add, 4)
    row_finish(top, total, out_ref)


def row_kernel(log_total, pairs, count, tiles, g_ref, out_ref, pot, top, total):
    pot[...] = log_total - joined_lse(g_ref)
    top[...] = jnp.full(top.shape, LOWEST, jnp.float32)
    total[...] = jnp.zeros(total.shape, jnp.float32)

    def scores(index, col):
        left = tiles[index, :, :LANES] + pot[pl.ds(2 * col, 1), :]
        right = tiles[index, :, LANES:] + pot[pl.ds(2 * col + 1, 1), :]
        return left, right

    def highest(index):
        row, col = block_at(pairs, index)
        rows = pl.ds(row, BLOCK)
        left, right = scores(index, col)
        top[rows, :] = jnp.maximum(top[rows, :], jnp.maximum(left, right))

    over_pairs(count, highest, 4)
    widen_top(top)

    def add(index):
        row, col = block_at(pairs, index)
        rows = pl.ds(row, BLOCK)
        left, right = scores(index, col)
        high = top[rows, :]
        total[rows, :] = total[rows, :] + (jnp.exp2(left - high) + jnp.exp2(right - high))

    over_pairs(count, add, 4)
    row_finish(top, total, out_ref)


def col_kernel(log_total, pairs, count, tiles, g_ref, out_ref, pot_ref, pot, top, total):
    line = log_total - joined_lse(g_ref)
    pot_ref[...] = line * TO_POT
    for k in range(CHUNKS):
        pot[pl.ds(k * LANES, LANES), :] = jnp.broadcast_to(line[k : k + 1, :], (LANES, LANES)).T
    top[...] = jnp.full(top.shape, LOWEST, jnp.float32)
    total[...] = jnp.zeros(total.shape, jnp.float32)

    def scores(index, row):
        rows = pl.ds(row, BLOCK)
        high = pot[rows, :]
        tile = tiles[index]
        return tile + jnp.concatenate([high, high], axis=1)

    def highest(index):
        row, col = block_at(pairs, index)
        score = scores(index, row)
        top[col] = jnp.maximum(top[col], jnp.max(score.reshape(BLOCK // 8, 8, BLOCK), axis=0))

    over_pairs(count, highest, 4)
    for k in range(BLK):
        top[k] = jnp.broadcast_to(jnp.max(top[k], axis=0, keepdims=True), (8, BLOCK))

    def add(index):
        row, col = block_at(pairs, index)
        score = scores(index, row).reshape(BLOCK // 8, 8, BLOCK)
        total[col] = total[col] + jnp.sum(jnp.exp2(score - top[col][None]), axis=0)

    over_pairs(count, add, 4)
    lines = []
    for k in range(BLK):
        lse = top[k][0:1] + log2(jnp.sum(total[k], axis=0, keepdims=True))
        lines += [lse[:, :LANES], lse[:, LANES:]]
    out = jnp.concatenate(lines, axis=0)
    out_ref[...] = jnp.broadcast_to(out[None], out_ref.shape)


def last_kernel(log_total, g_ref, pot_ref):
    pot_ref[...] = (log_total - joined_lse(g_ref)) * TO_POT


def smem():
    return pl.BlockSpec(memory_space=pltpu.SMEM)


def vmem():
    return pl.BlockSpec(memory_space=pltpu.VMEM)


def f32(*shape):
    return jax.ShapeDtypeStruct(shape, jnp.float32)


def params(limit=VMEM_LIMIT):
    return pltpu.CompilerParams(vmem_limit_bytes=limit)


def both_ways(x, axes):
    n = x.shape[0]
    groups = [[2 * k for k in range(n)], [2 * k + 1 for k in reversed(range(n))]]
    return lax.all_to_all(x, axes + ("c",), 0, 0, axis_index_groups=groups)


def on_device(source_embed, target_embed, source_labels, target_labels, pair_blocks, pair_count):
    pairs = pair_blocks.reshape(-1)
    count = pair_count.reshape(-1)
    n_src, n_tgt = lax.axis_size(SRC), lax.axis_size(TGT)

    def call(kernel, out_shape, *args, name):
        return pl.pallas_call(
            kernel,
            out_shape=out_shape,
            in_specs=[vmem()] * len(args),
            out_specs=jax.tree.map(lambda _: vmem(), out_shape),
            compiler_params=params(),
            name=name,
        )(*args)

    n_x, n_z = lax.axis_size("x"), lax.axis_size("z")
    part = target_embed.shape[0]
    near, tgt_group = pl.pallas_call(
        first_kernel,
        out_shape=(
            jax.ShapeDtypeStruct((n_z,) + target_embed.shape, jnp.bfloat16),
            f32(16, LANES),
        ),
        in_specs=[vmem(), vmem()],
        out_specs=(pl.BlockSpec(memory_space=pl.ANY), vmem()),
        scratch_shapes=[pltpu.SemaphoreType.DMA((n_z,))],
        compiler_params=params(FULL_VMEM),
        name="first",
    )(target_embed, target_labels[None])
    near = both_ways(near, ("z",))

    def around(x, axis):
        n = lax.axis_size(axis)
        return [x] + [
            lax.ppermute(x, axis, [((i + far) % n, i) for i in range(n)]) for far in range(1, n)
        ]

    src_group, src_sq = call(
        source_group_kernel,
        (f32(40, LANES), f32(1, ROWS)),
        source_embed,
        source_labels[None],
        tgt_group,
        name="source_group",
    )

    near, packets = lax.optimization_barrier((near, around(src_group, "x")))
    pieces = around(near, "x")
    src_group, tgt_near = pl.pallas_call(
        functools.partial(near_kernel, part),
        out_shape=(f32(40, LANES), f32(n_tgt, 8, LANES)),
        in_specs=[smem()] + [vmem()] * (n_x + 1),
        out_specs=(vmem(), vmem()),
        scratch_shapes=[pltpu.VMEM((n_x, 40, LANES), jnp.float32)],
        compiler_params=params(),
        name="near",
    )(lax.axis_index("x").reshape(1), *packets, tgt_group)
    tgt_near = lax.all_to_all(tgt_near, TGT, 0, 0)
    tgt_near, source_tall = lax.optimization_barrier((tgt_near, source_embed.T))
    stats = call(middle_kernel, f32(n_z, 40, LANES), tgt_near, src_group, name="middle")
    stats = both_ways(stats, ("z",))

    tall = pltpu.VMEM((ROWS, LANES), jnp.float32)
    wide = pltpu.VMEM((BLK, 8, BLOCK), jnp.float32)
    log_src = math.log2(ROWS * n_src)
    log_tgt = math.log2(ROWS * n_tgt)
    label_cost, tiles, sent = pl.pallas_call(
        functools.partial(cost_kernel, n_x, part * n_x),
        out_shape=(
            f32(CLASSES, CLASSES),
            f32(MAXP, BLOCK, BLOCK),
            f32(n_tgt, CHUNKS, LANES),
        ),
        in_specs=[smem()] * 3 + [vmem()] * (5 + n_x),
        out_specs=(vmem(), vmem(), vmem()),
        scratch_shapes=[
            pltpu.VMEM((16, ROWS), jnp.bfloat16),
            pltpu.VMEM((WIDTH, ROWS), jnp.bfloat16),
            pltpu.VMEM((16, ROWS), jnp.bfloat16),
            tall,
            tall,
        ],
        compiler_params=params(),
        name="cost_rows",
    )(
        pairs,
        count,
        jnp.stack([lax.axis_index("x"), lax.axis_index("c")]),
        stats,
        src_sq,
        source_labels[None],
        source_tall,
        *pieces,
        target_labels[None],
    )

    def columns(got):
        return pl.pallas_call(
            functools.partial(col_kernel, log_tgt),
            out_shape=(f32(n_src, CHUNKS, LANES), f32(CHUNKS, LANES)),
            in_specs=[smem(), smem(), vmem(), vmem()],
            out_specs=(vmem(), vmem()),
            scratch_shapes=[tall, wide, wide],
            compiler_params=params(),
            name="columns",
        )(pairs, count, tiles, got)

    def rows(got):
        return pl.pallas_call(
            functools.partial(row_kernel, log_src),
            out_shape=f32(n_tgt, CHUNKS, LANES),
            in_specs=[smem(), smem(), vmem(), vmem()],
            out_specs=vmem(),
            scratch_shapes=[pltpu.VMEM((CHUNKS, LANES), jnp.float32), tall, tall],
            compiler_params=params(),
            name="rows",
        )(pairs, count, tiles, got)

    sent, _ = columns(lax.all_to_all(sent, TGT, 0, 0))
    sent = rows(both_ways(sent, SRC))
    sent, src_pot = columns(lax.all_to_all(sent, TGT, 0, 0))
    tgt_pot = pl.pallas_call(
        functools.partial(last_kernel, log_src),
        out_shape=f32(CHUNKS, LANES),
        in_specs=[vmem()],
        out_specs=vmem(),
        compiler_params=params(),
        name="last",
    )(both_ways(sent, SRC))
    return (src_pot.reshape(-1), tgt_pot.reshape(-1), label_cost)


def solution(mesh):
    fine = Mesh(np.asarray(mesh.devices).reshape(8, 4, 4, 2), SRC + TGT)
    return jax.shard_map(
        on_device,
        mesh=fine,
        in_specs=(
            P(None, SRC),
            P(SRC, TGT),
            P(SRC),
            P(TGT),
            P(SRC, TGT, None, None),
            P(SRC, TGT),
        ),
        out_specs=(P(SRC), P(TGT), P()),
        check_vma=False,
    )
```

```python
import functools
import math

import jax
import jax.numpy as jnp
import numpy as np
from jax import lax
from jax.experimental import pallas as pl
from jax.experimental.pallas import tpu as pltpu
from jax.sharding import Mesh, PartitionSpec as P

CLASSES = 4
BLOCK = 256
ROWS = 2048
BLK = ROWS // BLOCK
LANES = 128
CHUNKS = ROWS // LANES
MAXP = 24
UNROLL = 4
WIDTH = 512

EPSILON = 0.05
LOWEST = -1e30
LOG2E = 1.0 / math.log(2.0)
TO_LOG2 = LOG2E / EPSILON
TO_POT = EPSILON / LOG2E

SRC = ("z", "x")
Z_ORDER = (0, 4, 2, 6, 1, 5, 3, 7)
X_ORDER = (0, 2, 1, 3)
TGT = ("y", "c")
VMEM_LIMIT = 24 * 1024 * 1024
FULL_VMEM = 64 * 1024 * 1024 - 32 * 1024


def log2(x):
    return jnp.log(x) * LOG2E


def repeated_onehot(labels):
    row_id = lax.broadcasted_iota(jnp.int32, (16, 1), 0)
    return jnp.where(row_id < 12, jnp.where(labels == row_id % CLASSES, 1.0, 0.0), 0.0)


def across(onehot, values):
    return lax.dot_general(
        onehot, values, (((1,), (1,)), ((), ())), preferred_element_type=jnp.float32
    )


def class_group(values, onehot, counts):
    part = lax.broadcasted_iota(jnp.int32, (16, 1), 0) // CLASSES
    wide = values.astype(jnp.float32)
    mean = across(onehot, values) / counts
    hi, mid, lo = three_parts(mean)
    parts = jnp.where(
        part == 0, hi, jnp.where(part == 1, mid, jnp.where(part == 2, lo, 0.0))
    ).astype(jnp.bfloat16)
    center = lax.dot_general(
        parts, onehot, (((0,), (0,)), ((), ())), preferred_element_type=jnp.float32
    )
    centered = wide - center
    hi, mid, lo = three_parts(centered * centered)
    spread = sum(across(onehot, p.astype(jnp.bfloat16)) for p in (hi, mid, lo))
    return jnp.where(part == 0, mean, spread)[:8], wide


def first_kernel(embed, labels, near_ref, out_ref, sems):
    copies = [
        pltpu.make_async_copy(embed, near_ref.at[k], sems.at[k]) for k in range(near_ref.shape[0])
    ]
    for copy in copies:
        copy.start()
    onehot = repeated_onehot(labels[...])
    counts = jnp.maximum(jnp.sum(onehot, axis=1, keepdims=True), 1.0)
    group, _ = class_group(embed[...], onehot.astype(jnp.bfloat16), counts)
    out_ref[...] = jnp.zeros(out_ref.shape, jnp.float32)
    out_ref[0:8, 0 : group.shape[1]] = group
    out_ref[8:16, :] = jnp.broadcast_to(counts[:8], (8, LANES))
    for copy in copies:
        copy.wait()


def lower_lanes():
    return lax.broadcasted_iota(jnp.int32, (8, LANES), 1) < LANES // 2


def source_group_kernel(embed, labels, tgt_group, out_ref, sq_ref):
    onehot = repeated_onehot(labels[...])
    counts = jnp.maximum(jnp.sum(onehot, axis=1, keepdims=True), 1.0)
    onehot = onehot.astype(jnp.bfloat16)
    sq = jnp.zeros((1, ROWS), jnp.float32)
    for c in range(WIDTH // LANES):
        group, wide = class_group(embed[c * LANES : (c + 1) * LANES, :], onehot, counts)
        out_ref[8 * c : 8 * c + 8, :] = group
        sq = sq + jnp.sum(wide * wide, axis=0, keepdims=True)
    out_ref[32:40, :] = jnp.where(lower_lanes(), tgt_group[0:8, :], counts[:8])
    sq_ref[...] = sq


def joined_counts(counts):
    total = functools.reduce(jnp.add, counts)
    return total, [c / total for c in counts]


def joined_group(groups, counts, shares):
    row_id = lax.broadcasted_iota(jnp.int32, (8, LANES), 0)
    mean = functools.reduce(jnp.add, [g * w for g, w in zip(groups, shares)])
    between = functools.reduce(
        jnp.add, [(g - mean) * (g - mean) * c for g, c in zip(groups, counts)]
    )
    spread = functools.reduce(jnp.add, groups) + pltpu.roll(between, 4, 0)
    return jnp.where(row_id < CLASSES, mean, spread)


def source_joined(got, order=None):
    peers = got.shape[0]
    order = range(peers) if order is None else order
    half = LANES // 2
    lower = lower_lanes()
    last = [got[k, 32:40, :] for k in order]
    targets = [jnp.where(lower, g, 0.0) for g in last]
    counts = [jnp.where(lower, pltpu.roll(g, half, 1), g) for g in last]
    total, shares = joined_counts(counts)
    groups = [
        joined_group([got[k, 8 * c : 8 * c + 8, :] for k in order], counts, shares)
        for c in range(WIDTH // LANES)
    ]
    return groups, total, targets


def side_by_side(targets, width):
    out = targets[0]
    for k, target in enumerate(targets[1:]):
        out = out + pltpu.roll(target, (k + 1) * width, 1)
    return out


def near_kernel(part, place, *args):
    pieces, (tgt_group, src_ref, tgt_ref, slots) = args[:-4], args[-4:]
    for far, piece in enumerate(pieces):
        slots[lax.rem(place[0] + far, len(pieces))] = piece[...]
    groups, total, targets = source_joined(slots)
    for c, group in enumerate(groups):
        src_ref[8 * c : 8 * c + 8, :] = group
    src_ref[32:40, :] = total
    target = jnp.where(lower_lanes(), side_by_side(targets, part), tgt_group[8:16, :])
    for k in range(tgt_ref.shape[0]):
        tgt_ref[k] = target


def middle_kernel(got, src, out_ref):
    half = LANES // 2
    lower = lower_lanes()
    row_id = lax.broadcasted_iota(jnp.int32, (8, LANES), 0)
    each = [got[k] for k in range(got.shape[0])]
    counts = [jnp.where(lower, pltpu.roll(g, half, 1), g) for g in each]
    total, shares = joined_counts(counts)
    group = joined_group([jnp.where(lower, g, 0.0) for g in each], counts, shares)
    group = jnp.where(row_id < CLASSES, group, group / total)
    last = jnp.where(lower, group, src[32:40, :])
    for k in range(out_ref.shape[0]):
        out_ref[k, 0:32, :] = src[0:32, :]
        out_ref[k, 32:40, :] = last


def label_rows(width, core, got, src_sq, src_lab, label_ref, xa_ref):
    order = []
    for z in range(got.shape[0]):
        first, second = (peer_order(("z",), c).index(z) for c in range(2))
        order.append(first + core * (second - first))
    groups, total, targets = source_joined(got, order)
    row_id = lax.broadcasted_iota(jnp.int32, (8, LANES), 0)
    lane_id = lax.broadcasted_iota(jnp.int32, (8, LANES), 1)
    each = LANES // width
    sides = ([], [])
    for c, group in enumerate(groups):
        tgt = side_by_side(targets[each * c : each * c + each], width)
        for side, stat in zip(sides, (jnp.where(row_id < CLASSES, group, group / total), tgt)):
            side.append(jnp.where(row_id < CLASSES, stat, jnp.sqrt(stat + 1e-06)))

    def distances(one, other):
        out = jnp.zeros((8, LANES), jnp.float32)
        for k in range(CLASSES):
            far = jnp.zeros((8, LANES), jnp.float32)
            for g, h in zip(one, other):
                gap = g - jnp.where(row_id < CLASSES, h[k : k + 1], h[CLASSES + k : CLASSES + k + 1])
                far = far + gap * gap
            far = far + pltpu.roll(far, 4, 0)
            out = jnp.where(lane_id == k, jnp.sum(far, axis=1, keepdims=True), out)
        return out

    label_ref[...] = distances(*sides)[:CLASSES, :CLASSES]
    by_target = distances(*sides[::-1])
    by_target = jnp.concatenate([by_target, by_target], axis=0)
    row_id = lax.broadcasted_iota(jnp.int32, (16, 1), 0)
    part_id = row_id // CLASSES
    labels = src_lab[...]
    u = jnp.broadcast_to(src_sq[...], (16, ROWS))
    for a in range(CLASSES):
        u = u + jnp.where(labels == a, by_target[:, a : a + 1], 0.0)
    hi, mid, lo = three_parts(-0.5 * u)
    ones = jnp.where(row_id < 15, 1.0, 0.0)
    xa_ref[...] = jnp.where(
        part_id == 0, hi, jnp.where(part_id == 1, mid, jnp.where(part_id == 2, lo, ones))
    ).astype(jnp.bfloat16)


def three_parts(v):
    hi = v.astype(jnp.bfloat16).astype(jnp.float32)
    rest = v - hi
    mid = rest.astype(jnp.bfloat16).astype(jnp.float32)
    return hi, mid, rest - mid


def joined_lse(g_ref):
    g = g_ref[...]
    top = jnp.max(g, axis=0)
    return top + log2(jnp.sum(jnp.exp2(g - top[None]), axis=0))


def row_finish(top, total, out_ref):
    lines = []
    for k in range(CHUNKS):
        at = pl.ds(k * LANES, LANES)
        lse = top[at, :] + log2(jnp.sum(total[at, :], axis=1, keepdims=True))
        lines.append(lse.T[0:1, :])
    line = jnp.concatenate(lines, axis=0)
    out_ref[...] = jnp.broadcast_to(line[None], out_ref.shape)


def widen_top(top):
    for k in range(CHUNKS):
        at = pl.ds(k * LANES, LANES)
        top[at, :] = jnp.broadcast_to(jnp.max(top[at, :], axis=1, keepdims=True), (LANES, LANES))


def over_pairs(count, body, unroll):
    def several(step, _):
        for k in range(unroll):
            body(step * unroll + k)
        return 0

    steps = (count[0] + UNROLL - 1) // UNROLL * (UNROLL // unroll)
    lax.fori_loop(0, steps, several, 0)


def block_at(pairs, index):
    row = pl.multiple_of(pairs[2 * index] * BLOCK, BLOCK)
    return row, pairs[2 * index + 1]


def cost_kernel(n_x, n_f, pairs, count, place, got, src_sq, src_lab, xt, *args):
    pieces, (tgt_lab, label_ref, tiles, out_ref, xa, y, ya, top, total) = args[:n_x], args[n_x:]
    label_rows(n_f, place[1], got, src_sq, src_lab, label_ref, xa)
    row_id = lax.broadcasted_iota(jnp.int32, (16, 1), 0)
    part = row_id // CLASSES
    cls = row_id % CLASSES

    tgt_sq = jnp.zeros((16, ROWS), jnp.float32)
    for far, piece in enumerate(pieces):
        at = lax.rem(place[0] + far, n_x)
        for k in range(piece.shape[0]):
            first, second = (peer_order(("z",), core)[k] for core in range(2))
            z = first + place[1] * (second - first)
            y[pl.ds(pl.multiple_of((z * n_x + at) * 16, 16), 16), :] = piece[k]
            v = piece[k].astype(jnp.float32)
            tgt_sq = tgt_sq + v * v

    hi, mid, lo = three_parts(-0.5 * jnp.sum(tgt_sq, axis=0, keepdims=True))
    onehot = jnp.where(tgt_lab[...] == cls, 1.0, 0.0)
    ya[...] = jnp.where(
        part < 3,
        onehot,
        jnp.where(cls == 0, hi, jnp.where(cls == 1, mid, jnp.where(cls == 2, lo, 0.0))),
    ).astype(jnp.bfloat16)

    top[...] = jnp.full(top.shape, LOWEST, jnp.float32)
    total[...] = jnp.zeros(total.shape, jnp.float32)

    def build(index):
        row, col = block_at(pairs, index)
        rows = pl.ds(row, BLOCK)
        cols = pl.ds(pl.multiple_of(col * BLOCK, BLOCK), BLOCK)
        cross = jnp.dot(xt[rows, :], y[:, cols], preferred_element_type=jnp.float32)
        extra = lax.dot_general(
            xa[:, rows], ya[:, cols], (((0,), (0,)), ((), ())), preferred_element_type=jnp.float32
        )
        tile = (cross + extra) * (2.0 * TO_LOG2) + jnp.where(index < count[0], 0.0, LOWEST)
        tiles[index] = tile
        top[rows, :] = jnp.maximum(top[rows, :], jnp.maximum(tile[:, :LANES], tile[:, LANES:]))

    over_pairs(count, build, 4)
    widen_top(top)

    def add(index):
        row, _ = block_at(pairs, index)
        rows = pl.ds(row, BLOCK)
        high = top[rows, :]
        left = jnp.exp2(tiles[index, :, :LANES] - high)
        right = jnp.exp2(tiles[index, :, LANES:] - high)
        total[rows, :] = total[rows, :] + (left + right)

    over_pairs(count, add, 4)
    row_finish(top, total, out_ref)


def row_kernel(log_total, pairs, count, tiles, g_ref, out_ref, pot, top, total):
    pot[...] = log_total - joined_lse(g_ref)
    top[...] = jnp.full(top.shape, LOWEST, jnp.float32)
    total[...] = jnp.zeros(total.shape, jnp.float32)

    def scores(index, col):
        left = tiles[index, :, :LANES] + pot[pl.ds(2 * col, 1), :]
        right = tiles[index, :, LANES:] + pot[pl.ds(2 * col + 1, 1), :]
        return left, right

    def highest(index):
        row, col = block_at(pairs, index)
        rows = pl.ds(row, BLOCK)
        left, right = scores(index, col)
        top[rows, :] = jnp.maximum(top[rows, :], jnp.maximum(left, right))

    over_pairs(count, highest, 4)
    widen_top(top)

    def add(index):
        row, col = block_at(pairs, index)
        rows = pl.ds(row, BLOCK)
        left, right = scores(index, col)
        high = top[rows, :]
        total[rows, :] = total[rows, :] + (jnp.exp2(left - high) + jnp.exp2(right - high))

    over_pairs(count, add, 4)
    row_finish(top, total, out_ref)


def col_kernel(log_total, pairs, count, tiles, g_ref, out_ref, pot_ref, pot, top, total):
    line = log_total - joined_lse(g_ref)
    pot_ref[...] = line * TO_POT
    for k in range(CHUNKS):
        pot[pl.ds(k * LANES, LANES), :] = jnp.broadcast_to(line[k : k + 1, :], (LANES, LANES)).T
    top[...] = jnp.full(top.shape, LOWEST, jnp.float32)
    total[...] = jnp.zeros(total.shape, jnp.float32)

    def scores(index, row):
        rows = pl.ds(row, BLOCK)
        high = pot[rows, :]
        tile = tiles[index]
        return tile + jnp.concatenate([high, high], axis=1)

    def highest(index):
        row, col = block_at(pairs, index)
        score = scores(index, row)
        top[col] = jnp.maximum(top[col], jnp.max(score.reshape(BLOCK // 8, 8, BLOCK), axis=0))

    over_pairs(count, highest, 4)
    for k in range(BLK):
        top[k] = jnp.broadcast_to(jnp.max(top[k], axis=0, keepdims=True), (8, BLOCK))

    def add(index):
        row, col = block_at(pairs, index)
        score = scores(index, row).reshape(BLOCK // 8, 8, BLOCK)
        total[col] = total[col] + jnp.sum(jnp.exp2(score - top[col][None]), axis=0)

    over_pairs(count, add, 4)
    lines = []
    for k in range(BLK):
        lse = top[k][0:1] + log2(jnp.sum(total[k], axis=0, keepdims=True))
        lines += [lse[:, :LANES], lse[:, LANES:]]
    out = jnp.concatenate(lines, axis=0)
    out_ref[...] = jnp.broadcast_to(out[None], out_ref.shape)


def last_kernel(log_total, g_ref, pot_ref):
    pot_ref[...] = (log_total - joined_lse(g_ref)) * TO_POT


def smem():
    return pl.BlockSpec(memory_space=pltpu.SMEM)


def vmem():
    return pl.BlockSpec(memory_space=pltpu.VMEM)


def f32(*shape):
    return jax.ShapeDtypeStruct(shape, jnp.float32)


def params(limit=VMEM_LIMIT):
    return pltpu.CompilerParams(vmem_limit_bytes=limit)


def peer_order(axes, core):
    rows = [(z + 2 * core) % 8 for z in Z_ORDER]
    if axes == ("z",):
        return rows
    return [rows[k % 8] * 4 + (X_ORDER[(k // 8 + k) % 4] + 2 * core) % 4 for k in range(32)]


def exchange(x, axes):
    groups = [[2 * k + core for k in peer_order(axes, core)] for core in range(2)]
    return lax.all_to_all(x, axes + ("c",), 0, 0, axis_index_groups=groups)


def on_device(source_embed, target_embed, source_labels, target_labels, pair_blocks, pair_count):
    pairs = pair_blocks.reshape(-1)
    count = pair_count.reshape(-1)
    n_src, n_tgt = lax.axis_size(SRC), lax.axis_size(TGT)

    def call(kernel, out_shape, *args, name):
        return pl.pallas_call(
            kernel,
            out_shape=out_shape,
            in_specs=[vmem()] * len(args),
            out_specs=jax.tree.map(lambda _: vmem(), out_shape),
            compiler_params=params(),
            name=name,
        )(*args)

    n_x, n_z = lax.axis_size("x"), lax.axis_size("z")
    part = target_embed.shape[0]
    near, tgt_group = pl.pallas_call(
        first_kernel,
        out_shape=(
            jax.ShapeDtypeStruct((n_z,) + target_embed.shape, jnp.bfloat16),
            f32(16, LANES),
        ),
        in_specs=[vmem(), vmem()],
        out_specs=(pl.BlockSpec(memory_space=pl.ANY), vmem()),
        scratch_shapes=[pltpu.SemaphoreType.DMA((n_z,))],
        compiler_params=params(FULL_VMEM),
        name="first",
    )(target_embed, target_labels[None])
    near = exchange(near, ("z",))

    def around(x, axis):
        n = lax.axis_size(axis)
        return [x] + [
            lax.ppermute(x, axis, [((i + far) % n, i) for i in range(n)]) for far in range(1, n)
        ]

    src_group, src_sq = call(
        source_group_kernel,
        (f32(40, LANES), f32(1, ROWS)),
        source_embed,
        source_labels[None],
        tgt_group,
        name="source_group",
    )

    near, packets = lax.optimization_barrier((near, around(src_group, "x")))
    pieces = around(near, "x")
    src_group, tgt_near = pl.pallas_call(
        functools.partial(near_kernel, part),
        out_shape=(f32(40, LANES), f32(n_tgt, 8, LANES)),
        in_specs=[smem()] + [vmem()] * (n_x + 1),
        out_specs=(vmem(), vmem()),
        scratch_shapes=[pltpu.VMEM((n_x, 40, LANES), jnp.float32)],
        compiler_params=params(),
        name="near",
    )(lax.axis_index("x").reshape(1), *packets, tgt_group)
    tgt_near = lax.all_to_all(tgt_near, TGT, 0, 0)
    tgt_near, source_tall = lax.optimization_barrier((tgt_near, source_embed.T))
    stats = call(middle_kernel, f32(n_z, 40, LANES), tgt_near, src_group, name="middle")
    stats = exchange(stats, ("z",))

    tall = pltpu.VMEM((ROWS, LANES), jnp.float32)
    wide = pltpu.VMEM((BLK, 8, BLOCK), jnp.float32)
    log_src = math.log2(ROWS * n_src)
    log_tgt = math.log2(ROWS * n_tgt)
    label_cost, tiles, sent = pl.pallas_call(
        functools.partial(cost_kernel, n_x, part * n_x),
        out_shape=(
            f32(CLASSES, CLASSES),
            f32(MAXP, BLOCK, BLOCK),
            f32(n_tgt, CHUNKS, LANES),
        ),
        in_specs=[smem()] * 3 + [vmem()] * (5 + n_x),
        out_specs=(vmem(), vmem(), vmem()),
        scratch_shapes=[
            pltpu.VMEM((16, ROWS), jnp.bfloat16),
            pltpu.VMEM((WIDTH, ROWS), jnp.bfloat16),
            pltpu.VMEM((16, ROWS), jnp.bfloat16),
            tall,
            tall,
        ],
        compiler_params=params(),
        name="cost_rows",
    )(
        pairs,
        count,
        jnp.stack([lax.axis_index("x"), lax.axis_index("c")]),
        stats,
        src_sq,
        source_labels[None],
        source_tall,
        *pieces,
        target_labels[None],
    )

    def columns(got):
        return pl.pallas_call(
            functools.partial(col_kernel, log_tgt),
            out_shape=(f32(n_src, CHUNKS, LANES), f32(CHUNKS, LANES)),
            in_specs=[smem(), smem(), vmem(), vmem()],
            out_specs=(vmem(), vmem()),
            scratch_shapes=[tall, wide, wide],
            compiler_params=params(),
            name="columns",
        )(pairs, count, tiles, got)

    def rows(got):
        return pl.pallas_call(
            functools.partial(row_kernel, log_src),
            out_shape=f32(n_tgt, CHUNKS, LANES),
            in_specs=[smem(), smem(), vmem(), vmem()],
            out_specs=vmem(),
            scratch_shapes=[pltpu.VMEM((CHUNKS, LANES), jnp.float32), tall, tall],
            compiler_params=params(),
            name="rows",
        )(pairs, count, tiles, got)

    sent, _ = columns(lax.all_to_all(sent, TGT, 0, 0))
    sent = rows(exchange(sent, SRC))
    sent, src_pot = columns(lax.all_to_all(sent, TGT, 0, 0))
    tgt_pot = pl.pallas_call(
        functools.partial(last_kernel, log_src),
        out_shape=f32(CHUNKS, LANES),
        in_specs=[vmem()],
        out_specs=vmem(),
        compiler_params=params(),
        name="last",
    )(exchange(sent, SRC))
    return (src_pot.reshape(-1), tgt_pot.reshape(-1), label_cost)


def solution(mesh):
    fine = Mesh(np.asarray(mesh.devices).reshape(8, 4, 4, 2), SRC + TGT)
    return jax.shard_map(
        on_device,
        mesh=fine,
        in_specs=(
            P(None, SRC),
            P(SRC, TGT),
            P(SRC),
            P(TGT),
            P(SRC, TGT, None, None),
            P(SRC, TGT),
        ),
        out_specs=(P(SRC), P(TGT), P()),
        check_vma=False,
    )
```

```python
import functools
import math

import jax
import jax.numpy as jnp
import numpy as np
from jax import lax
from jax.experimental import pallas as pl
from jax.experimental.pallas import tpu as pltpu
from jax.sharding import Mesh, PartitionSpec as P

CLASSES = 4
BLOCK = 256
ROWS = 2048
BLK = ROWS // BLOCK
LANES = 128
CHUNKS = ROWS // LANES
MAXP = 24
UNROLL = 4
WIDTH = 512

EPSILON = 0.05
LOWEST = -1e30
LOG2E = 1.0 / math.log(2.0)
TO_LOG2 = LOG2E / EPSILON
TO_POT = EPSILON / LOG2E

SRC = ("z", "x")
TGT = ("y", "c")
VMEM_LIMIT = 24 * 1024 * 1024


def log2(x):
    return jnp.log(x) * LOG2E


def repeated_onehot(labels):
    row_id = lax.broadcasted_iota(jnp.int32, (16, 1), 0)
    return jnp.where(row_id < 12, jnp.where(labels == row_id % CLASSES, 1.0, 0.0), 0.0)


def across(onehot, values):
    return lax.dot_general(
        onehot, values, (((1,), (1,)), ((), ())), preferred_element_type=jnp.float32
    )


def class_group(values, onehot, counts):
    part = lax.broadcasted_iota(jnp.int32, (16, 1), 0) // CLASSES
    wide = values.astype(jnp.float32)
    mean = across(onehot, values) / counts
    hi, mid, lo = three_parts(mean)
    parts = jnp.where(
        part == 0, hi, jnp.where(part == 1, mid, jnp.where(part == 2, lo, 0.0))
    ).astype(jnp.bfloat16)
    center = lax.dot_general(
        parts, onehot, (((0,), (0,)), ((), ())), preferred_element_type=jnp.float32
    )
    centered = wide - center
    hi, mid, lo = three_parts(centered * centered)
    spread = sum(across(onehot, p.astype(jnp.bfloat16)) for p in (hi, mid, lo))
    return jnp.where(part == 0, mean, spread)[:8], wide


def first_kernel(embed, labels, near_ref, out_ref, sems):
    copies = [
        pltpu.make_async_copy(embed, near_ref.at[k], sems.at[k]) for k in range(near_ref.shape[0])
    ]
    for copy in copies:
        copy.start()
    onehot = repeated_onehot(labels[...])
    counts = jnp.maximum(jnp.sum(onehot, axis=1, keepdims=True), 1.0)
    group, _ = class_group(embed[...], onehot.astype(jnp.bfloat16), counts)
    out_ref[...] = jnp.zeros(out_ref.shape, jnp.float32)
    out_ref[0:8, 0 : group.shape[1]] = group
    out_ref[8:16, :] = jnp.broadcast_to(counts[:8], (8, LANES))
    for copy in copies:
        copy.wait()


def lower_lanes():
    return lax.broadcasted_iota(jnp.int32, (8, LANES), 1) < LANES // 2


def source_group_kernel(embed, labels, tgt_group, out_ref, sq_ref):
    onehot = repeated_onehot(labels[...])
    counts = jnp.maximum(jnp.sum(onehot, axis=1, keepdims=True), 1.0)
    onehot = onehot.astype(jnp.bfloat16)
    sq = jnp.zeros((1, ROWS), jnp.float32)
    for c in range(WIDTH // LANES):
        group, wide = class_group(embed[c * LANES : (c + 1) * LANES, :], onehot, counts)
        out_ref[8 * c : 8 * c + 8, :] = group
        sq = sq + jnp.sum(wide * wide, axis=0, keepdims=True)
    out_ref[32:40, :] = jnp.where(lower_lanes(), tgt_group[0:8, :], counts[:8])
    sq_ref[...] = sq


def joined_counts(counts):
    total = functools.reduce(jnp.add, counts)
    return total, [c / total for c in counts]


def joined_group(groups, counts, shares):
    row_id = lax.broadcasted_iota(jnp.int32, (8, LANES), 0)
    mean = functools.reduce(jnp.add, [g * w for g, w in zip(groups, shares)])
    between = functools.reduce(
        jnp.add, [(g - mean) * (g - mean) * c for g, c in zip(groups, counts)]
    )
    spread = functools.reduce(jnp.add, groups) + pltpu.roll(between, 4, 0)
    return jnp.where(row_id < CLASSES, mean, spread)


def source_joined(got, order=None):
    peers = got.shape[0]
    order = range(peers) if order is None else order
    half = LANES // 2
    lower = lower_lanes()
    last = [got[k, 32:40, :] for k in order]
    targets = [jnp.where(lower, g, 0.0) for g in last]
    counts = [jnp.where(lower, pltpu.roll(g, half, 1), g) for g in last]
    total, shares = joined_counts(counts)
    groups = [
        joined_group([got[k, 8 * c : 8 * c + 8, :] for k in order], counts, shares)
        for c in range(WIDTH // LANES)
    ]
    return groups, total, targets


def side_by_side(targets, width):
    out = targets[0]
    for k, target in enumerate(targets[1:]):
        out = out + pltpu.roll(target, (k + 1) * width, 1)
    return out


def near_kernel(part, place, *args):
    pieces, (tgt_group, src_ref, tgt_ref, slots) = args[:-4], args[-4:]
    for far, piece in enumerate(pieces):
        slots[lax.rem(place[0] + far, len(pieces))] = piece[...]
    groups, total, targets = source_joined(slots)
    for c, group in enumerate(groups):
        src_ref[8 * c : 8 * c + 8, :] = group
    src_ref[32:40, :] = total
    target = jnp.where(lower_lanes(), side_by_side(targets, part), tgt_group[8:16, :])
    for k in range(tgt_ref.shape[0]):
        tgt_ref[k] = target


def middle_kernel(got, src, out_ref):
    half = LANES // 2
    lower = lower_lanes()
    row_id = lax.broadcasted_iota(jnp.int32, (8, LANES), 0)
    each = [got[k] for k in range(got.shape[0])]
    counts = [jnp.where(lower, pltpu.roll(g, half, 1), g) for g in each]
    total, shares = joined_counts(counts)
    group = joined_group([jnp.where(lower, g, 0.0) for g in each], counts, shares)
    group = jnp.where(row_id < CLASSES, group, group / total)
    last = jnp.where(lower, group, src[32:40, :])
    for k in range(out_ref.shape[0]):
        out_ref[k, 0:32, :] = src[0:32, :]
        out_ref[k, 32:40, :] = last


def label_rows(width, core, got, src_sq, src_lab, label_ref, xa_ref):
    peers = got.shape[0]
    groups, total, targets = source_joined(
        got, [k + core * (peers - 1 - 2 * k) for k in range(peers)]
    )
    row_id = lax.broadcasted_iota(jnp.int32, (8, LANES), 0)
    lane_id = lax.broadcasted_iota(jnp.int32, (8, LANES), 1)
    each = LANES // width
    sides = ([], [])
    for c, group in enumerate(groups):
        tgt = side_by_side(targets[each * c : each * c + each], width)
        for side, stat in zip(sides, (jnp.where(row_id < CLASSES, group, group / total), tgt)):
            side.append(jnp.where(row_id < CLASSES, stat, jnp.sqrt(stat + 1e-06)))

    def distances(one, other):
        out = jnp.zeros((8, LANES), jnp.float32)
        for k in range(CLASSES):
            far = jnp.zeros((8, LANES), jnp.float32)
            for g, h in zip(one, other):
                gap = g - jnp.where(row_id < CLASSES, h[k : k + 1], h[CLASSES + k : CLASSES + k + 1])
                far = far + gap * gap
            far = far + pltpu.roll(far, 4, 0)
            out = jnp.where(lane_id == k, jnp.sum(far, axis=1, keepdims=True), out)
        return out

    label_ref[...] = distances(*sides)[:CLASSES, :CLASSES]
    by_target = distances(*sides[::-1])
    by_target = jnp.concatenate([by_target, by_target], axis=0)
    row_id = lax.broadcasted_iota(jnp.int32, (16, 1), 0)
    part_id = row_id // CLASSES
    labels = src_lab[...]
    u = jnp.broadcast_to(src_sq[...], (16, ROWS))
    for a in range(CLASSES):
        u = u + jnp.where(labels == a, by_target[:, a : a + 1], 0.0)
    hi, mid, lo = three_parts(-0.5 * u)
    ones = jnp.where(row_id < 15, 1.0, 0.0)
    xa_ref[...] = jnp.where(
        part_id == 0, hi, jnp.where(part_id == 1, mid, jnp.where(part_id == 2, lo, ones))
    ).astype(jnp.bfloat16)


def three_parts(v):
    hi = v.astype(jnp.bfloat16).astype(jnp.float32)
    rest = v - hi
    mid = rest.astype(jnp.bfloat16).astype(jnp.float32)
    return hi, mid, rest - mid


def joined_lse(g_ref):
    g = g_ref[...]
    top = jnp.max(g, axis=0)
    return top + log2(jnp.sum(jnp.exp2(g - top[None]), axis=0))


def row_finish(top, total, out_ref):
    lines = []
    for k in range(CHUNKS):
        at = pl.ds(k * LANES, LANES)
        lse = top[at, :] + log2(jnp.sum(total[at, :], axis=1, keepdims=True))
        lines.append(lse.T[0:1, :])
    line = jnp.concatenate(lines, axis=0)
    out_ref[...] = jnp.broadcast_to(line[None], out_ref.shape)


def widen_top(top):
    for k in range(CHUNKS):
        at = pl.ds(k * LANES, LANES)
        top[at, :] = jnp.broadcast_to(jnp.max(top[at, :], axis=1, keepdims=True), (LANES, LANES))


def over_pairs(count, body, unroll):
    def several(step, _):
        for k in range(unroll):
            body(step * unroll + k)
        return 0

    steps = (count[0] + UNROLL - 1) // UNROLL * (UNROLL // unroll)
    lax.fori_loop(0, steps, several, 0)


def block_at(pairs, index):
    row = pl.multiple_of(pairs[2 * index] * BLOCK, BLOCK)
    return row, pairs[2 * index + 1]


def cost_kernel(n_x, n_f, pairs, count, place, got, src_sq, src_lab, xt, *args):
    pieces, (tgt_lab, label_ref, tiles, out_ref, xa, y, ya, top, total) = args[:n_x], args[n_x:]
    label_rows(n_f, place[1], got, src_sq, src_lab, label_ref, xa)
    row_id = lax.broadcasted_iota(jnp.int32, (16, 1), 0)
    part = row_id // CLASSES
    cls = row_id % CLASSES

    tgt_sq = jnp.zeros((16, ROWS), jnp.float32)
    for far, piece in enumerate(pieces):
        at = lax.rem(place[0] + far, n_x)
        for k in range(piece.shape[0]):
            z = k + place[1] * (piece.shape[0] - 1 - 2 * k)
            y[pl.ds(pl.multiple_of((z * n_x + at) * 16, 16), 16), :] = piece[k]
            v = piece[k].astype(jnp.float32)
            tgt_sq = tgt_sq + v * v

    hi, mid, lo = three_parts(-0.5 * jnp.sum(tgt_sq, axis=0, keepdims=True))
    onehot = jnp.where(tgt_lab[...] == cls, 1.0, 0.0)
    ya[...] = jnp.where(
        part < 3,
        onehot,
        jnp.where(cls == 0, hi, jnp.where(cls == 1, mid, jnp.where(cls == 2, lo, 0.0))),
    ).astype(jnp.bfloat16)

    top[...] = jnp.full(top.shape, LOWEST, jnp.float32)
    total[...] = jnp.zeros(total.shape, jnp.float32)

    def build(index):
        row, col = block_at(pairs, index)
        rows = pl.ds(row, BLOCK)
        cols = pl.ds(pl.multiple_of(col * BLOCK, BLOCK), BLOCK)
        cross = jnp.dot(xt[rows, :], y[:, cols], preferred_element_type=jnp.float32)
        extra = lax.dot_general(
            xa[:, rows], ya[:, cols], (((0,), (0,)), ((), ())), preferred_element_type=jnp.float32
        )
        tile = (cross + extra) * (2.0 * TO_LOG2) + jnp.where(index < count[0], 0.0, LOWEST)
        tiles[index] = tile
        top[rows, :] = jnp.maximum(top[rows, :], jnp.maximum(tile[:, :LANES], tile[:, LANES:]))

    over_pairs(count, build, 4)
    widen_top(top)

    def add(index):
        row, _ = block_at(pairs, index)
        rows = pl.ds(row, BLOCK)
        high = top[rows, :]
        left = jnp.exp2(tiles[index, :, :LANES] - high)
        right = jnp.exp2(tiles[index, :, LANES:] - high)
        total[rows, :] = total[rows, :] + (left + right)

    over_pairs(count, add, 4)
    row_finish(top, total, out_ref)


def row_kernel(log_total, pairs, count, tiles, g_ref, out_ref, pot, top, total):
    pot[...] = log_total - joined_lse(g_ref)
    top[...] = jnp.full(top.shape, LOWEST, jnp.float32)
    total[...] = jnp.zeros(total.shape, jnp.float32)

    def scores(index, col):
        left = tiles[index, :, :LANES] + pot[pl.ds(2 * col, 1), :]
        right = tiles[index, :, LANES:] + pot[pl.ds(2 * col + 1, 1), :]
        return left, right

    def highest(index):
        row, col = block_at(pairs, index)
        rows = pl.ds(row, BLOCK)
        left, right = scores(index, col)
        top[rows, :] = jnp.maximum(top[rows, :], jnp.maximum(left, right))

    over_pairs(count, highest, 4)
    widen_top(top)

    def add(index):
        row, col = block_at(pairs, index)
        rows = pl.ds(row, BLOCK)
        left, right = scores(index, col)
        high = top[rows, :]
        total[rows, :] = total[rows, :] + (jnp.exp2(left - high) + jnp.exp2(right - high))

    over_pairs(count, add, 4)
    row_finish(top, total, out_ref)


def col_kernel(log_total, pairs, count, tiles, g_ref, out_ref, pot_ref, pot, top, total):
    line = log_total - joined_lse(g_ref)
    pot_ref[...] = line * TO_POT
    for k in range(CHUNKS):
        pot[pl.ds(k * LANES, LANES), :] = jnp.broadcast_to(line[k : k + 1, :], (LANES, LANES)).T
    top[...] = jnp.full(top.shape, LOWEST, jnp.float32)
    total[...] = jnp.zeros(total.shape, jnp.float32)

    def scores(index, row):
        rows = pl.ds(row, BLOCK)
        high = pot[rows, :]
        tile = tiles[index]
        return tile + jnp.concatenate([high, high], axis=1)

    def highest(index):
        row, col = block_at(pairs, index)
        score = scores(index, row)
        top[col] = jnp.maximum(top[col], jnp.max(score.reshape(BLOCK // 8, 8, BLOCK), axis=0))

    over_pairs(count, highest, 4)
    for k in range(BLK):
        top[k] = jnp.broadcast_to(jnp.max(top[k], axis=0, keepdims=True), (8, BLOCK))

    def add(index):
        row, col = block_at(pairs, index)
        score = scores(index, row).reshape(BLOCK // 8, 8, BLOCK)
        total[col] = total[col] + jnp.sum(jnp.exp2(score - top[col][None]), axis=0)

    over_pairs(count, add, 4)
    lines = []
    for k in range(BLK):
        lse = top[k][0:1] + log2(jnp.sum(total[k], axis=0, keepdims=True))
        lines += [lse[:, :LANES], lse[:, LANES:]]
    out = jnp.concatenate(lines, axis=0)
    out_ref[...] = jnp.broadcast_to(out[None], out_ref.shape)


def last_kernel(log_total, g_ref, pot_ref):
    pot_ref[...] = (log_total - joined_lse(g_ref)) * TO_POT


def smem():
    return pl.BlockSpec(memory_space=pltpu.SMEM)


def vmem():
    return pl.BlockSpec(memory_space=pltpu.VMEM)


def f32(*shape):
    return jax.ShapeDtypeStruct(shape, jnp.float32)


def params():
    return pltpu.CompilerParams(vmem_limit_bytes=VMEM_LIMIT)


def both_ways(x, axes):
    n = x.shape[0]
    groups = [[2 * k for k in range(n)], [2 * k + 1 for k in reversed(range(n))]]
    return lax.all_to_all(x, axes + ("c",), 0, 0, axis_index_groups=groups)


def on_device(source_embed, target_embed, source_labels, target_labels, pair_blocks, pair_count):
    pairs = pair_blocks.reshape(-1)
    count = pair_count.reshape(-1)
    n_src, n_tgt = lax.axis_size(SRC), lax.axis_size(TGT)

    def call(kernel, out_shape, *args, name):
        return pl.pallas_call(
            kernel,
            out_shape=out_shape,
            in_specs=[vmem()] * len(args),
            out_specs=jax.tree.map(lambda _: vmem(), out_shape),
            compiler_params=params(),
            name=name,
        )(*args)

    n_x, n_z = lax.axis_size("x"), lax.axis_size("z")
    part = target_embed.shape[0]
    near, tgt_group = pl.pallas_call(
        first_kernel,
        out_shape=(
            jax.ShapeDtypeStruct((n_z,) + target_embed.shape, jnp.bfloat16),
            f32(16, LANES),
        ),
        in_specs=[vmem(), vmem()],
        out_specs=(pl.BlockSpec(memory_space=pl.ANY), vmem()),
        scratch_shapes=[pltpu.SemaphoreType.DMA((n_z,))],
        compiler_params=params(),
        name="first",
    )(target_embed, target_labels[None])
    near = both_ways(near, ("z",))

    def around(x, axis):
        n = lax.axis_size(axis)
        return [x] + [
            lax.ppermute(x, axis, [((i + far) % n, i) for i in range(n)]) for far in range(1, n)
        ]

    src_group, src_sq = call(
        source_group_kernel,
        (f32(40, LANES), f32(1, ROWS)),
        source_embed,
        source_labels[None],
        tgt_group,
        name="source_group",
    )

    near, packets = lax.optimization_barrier((near, around(src_group, "x")))
    pieces = around(near, "x")
    src_group, tgt_near = pl.pallas_call(
        functools.partial(near_kernel, part),
        out_shape=(f32(40, LANES), f32(n_tgt, 8, LANES)),
        in_specs=[smem()] + [vmem()] * (n_x + 1),
        out_specs=(vmem(), vmem()),
        scratch_shapes=[pltpu.VMEM((n_x, 40, LANES), jnp.float32)],
        compiler_params=params(),
        name="near",
    )(lax.axis_index("x").reshape(1), *packets, tgt_group)
    tgt_near = lax.all_to_all(tgt_near, TGT, 0, 0)
    tgt_near, source_tall = lax.optimization_barrier((tgt_near, source_embed.T))
    stats = call(middle_kernel, f32(n_z, 40, LANES), tgt_near, src_group, name="middle")
    stats = both_ways(stats, ("z",))

    tall = pltpu.VMEM((ROWS, LANES), jnp.float32)
    wide = pltpu.VMEM((BLK, 8, BLOCK), jnp.float32)
    log_src = math.log2(ROWS * n_src)
    log_tgt = math.log2(ROWS * n_tgt)
    label_cost, tiles, sent = pl.pallas_call(
        functools.partial(cost_kernel, n_x, part * n_x),
        out_shape=(
            f32(CLASSES, CLASSES),
            f32(MAXP, BLOCK, BLOCK),
            f32(n_tgt, CHUNKS, LANES),
        ),
        in_specs=[smem()] * 3 + [vmem()] * (5 + n_x),
        out_specs=(vmem(), vmem(), vmem()),
        scratch_shapes=[
            pltpu.VMEM((16, ROWS), jnp.bfloat16),
            pltpu.VMEM((WIDTH, ROWS), jnp.bfloat16),
            pltpu.VMEM((16, ROWS), jnp.bfloat16),
            tall,
            tall,
        ],
        compiler_params=params(),
        name="cost_rows",
    )(
        pairs,
        count,
        jnp.stack([lax.axis_index("x"), lax.axis_index("c")]),
        stats,
        src_sq,
        source_labels[None],
        source_tall,
        *pieces,
        target_labels[None],
    )

    def columns(got):
        return pl.pallas_call(
            functools.partial(col_kernel, log_tgt),
            out_shape=(f32(n_src, CHUNKS, LANES), f32(CHUNKS, LANES)),
            in_specs=[smem(), smem(), vmem(), vmem()],
            out_specs=(vmem(), vmem()),
            scratch_shapes=[tall, wide, wide],
            compiler_params=params(),
            name="columns",
        )(pairs, count, tiles, got)

    def rows(got):
        return pl.pallas_call(
            functools.partial(row_kernel, log_src),
            out_shape=f32(n_tgt, CHUNKS, LANES),
            in_specs=[smem(), smem(), vmem(), vmem()],
            out_specs=vmem(),
            scratch_shapes=[pltpu.VMEM((CHUNKS, LANES), jnp.float32), tall, tall],
            compiler_params=params(),
            name="rows",
        )(pairs, count, tiles, got)

    sent, _ = columns(lax.all_to_all(sent, TGT, 0, 0))
    sent = rows(both_ways(sent, SRC))
    sent, src_pot = columns(lax.all_to_all(sent, TGT, 0, 0))
    tgt_pot = pl.pallas_call(
        functools.partial(last_kernel, log_src),
        out_shape=f32(CHUNKS, LANES),
        in_specs=[vmem()],
        out_specs=vmem(),
        compiler_params=params(),
        name="last",
    )(both_ways(sent, SRC))
    return (src_pot.reshape(-1), tgt_pot.reshape(-1), label_cost)


def solution(mesh):
    fine = Mesh(np.asarray(mesh.devices).reshape(8, 4, 4, 2), SRC + TGT)
    return jax.shard_map(
        on_device,
        mesh=fine,
        in_specs=(
            P(None, SRC),
            P(SRC, TGT),
            P(SRC),
            P(TGT),
            P(SRC, TGT, None, None),
            P(SRC, TGT),
        ),
        out_specs=(P(SRC), P(TGT), P()),
        check_vma=False,
    )
```

```python
import functools
import math

import jax
import jax.numpy as jnp
import numpy as np
from jax import lax
from jax.experimental import pallas as pl
from jax.experimental.pallas import tpu as pltpu
from jax.sharding import Mesh, PartitionSpec as P

CLASSES = 4
BLOCK = 256
ROWS = 2048
BLK = ROWS // BLOCK
LANES = 128
CHUNKS = ROWS // LANES
MAXP = 24
UNROLL = 4
WIDTH = 512

EPSILON = 0.05
LOWEST = -1e30
LOG2E = 1.0 / math.log(2.0)
TO_LOG2 = LOG2E / EPSILON
TO_POT = EPSILON / LOG2E

SRC = ("z", "x")
TGT = ("y", "c")
VMEM_LIMIT = 24 * 1024 * 1024


def log2(x):
    return jnp.log(x) * LOG2E


def repeated_onehot(labels):
    row_id = lax.broadcasted_iota(jnp.int32, (16, 1), 0)
    return jnp.where(row_id < 12, jnp.where(labels == row_id % CLASSES, 1.0, 0.0), 0.0)


def across(onehot, values):
    return lax.dot_general(
        onehot, values, (((1,), (1,)), ((), ())), preferred_element_type=jnp.float32
    )


def class_group(values, onehot, counts):
    part = lax.broadcasted_iota(jnp.int32, (16, 1), 0) // CLASSES
    wide = values.astype(jnp.float32)
    mean = across(onehot, values) / counts
    hi, mid, lo = three_parts(mean)
    parts = jnp.where(
        part == 0, hi, jnp.where(part == 1, mid, jnp.where(part == 2, lo, 0.0))
    ).astype(jnp.bfloat16)
    center = lax.dot_general(
        parts, onehot, (((0,), (0,)), ((), ())), preferred_element_type=jnp.float32
    )
    centered = wide - center
    hi, mid, lo = three_parts(centered * centered)
    spread = sum(across(onehot, p.astype(jnp.bfloat16)) for p in (hi, mid, lo))
    return jnp.where(part == 0, mean, spread)[:8], wide


def first_kernel(embed, labels, near_ref, out_ref, sems):
    copies = [
        pltpu.make_async_copy(embed, near_ref.at[k], sems.at[k]) for k in range(near_ref.shape[0])
    ]
    for copy in copies:
        copy.start()
    onehot = repeated_onehot(labels[...])
    counts = jnp.maximum(jnp.sum(onehot, axis=1, keepdims=True), 1.0)
    group, _ = class_group(embed[...], onehot.astype(jnp.bfloat16), counts)
    out_ref[...] = jnp.zeros(out_ref.shape, jnp.float32)
    out_ref[0:8, 0 : group.shape[1]] = group
    out_ref[8:16, :] = jnp.broadcast_to(counts[:8], (8, LANES))
    for copy in copies:
        copy.wait()


def lower_lanes():
    return lax.broadcasted_iota(jnp.int32, (8, LANES), 1) < LANES // 2


def source_group_kernel(embed, labels, tgt_group, out_ref, sq_ref):
    onehot = repeated_onehot(labels[...])
    counts = jnp.maximum(jnp.sum(onehot, axis=1, keepdims=True), 1.0)
    onehot = onehot.astype(jnp.bfloat16)
    sq = jnp.zeros((1, ROWS), jnp.float32)
    for c in range(WIDTH // LANES):
        group, wide = class_group(embed[c * LANES : (c + 1) * LANES, :], onehot, counts)
        out_ref[8 * c : 8 * c + 8, :] = group
        sq = sq + jnp.sum(wide * wide, axis=0, keepdims=True)
    out_ref[32:40, :] = jnp.where(lower_lanes(), tgt_group[0:8, :], counts[:8])
    sq_ref[...] = sq


def joined_counts(counts):
    total = functools.reduce(jnp.add, counts)
    return total, [c / total for c in counts]


def joined_group(groups, counts, shares):
    row_id = lax.broadcasted_iota(jnp.int32, (8, LANES), 0)
    mean = functools.reduce(jnp.add, [g * w for g, w in zip(groups, shares)])
    between = functools.reduce(
        jnp.add, [(g - mean) * (g - mean) * c for g, c in zip(groups, counts)]
    )
    spread = functools.reduce(jnp.add, groups) + pltpu.roll(between, 4, 0)
    return jnp.where(row_id < CLASSES, mean, spread)


def source_joined(got, order=None):
    peers = got.shape[0]
    order = range(peers) if order is None else order
    half = LANES // 2
    lower = lower_lanes()
    last = [got[k, 32:40, :] for k in order]
    targets = [jnp.where(lower, g, 0.0) for g in last]
    counts = [jnp.where(lower, pltpu.roll(g, half, 1), g) for g in last]
    total, shares = joined_counts(counts)
    groups = [
        joined_group([got[k, 8 * c : 8 * c + 8, :] for k in order], counts, shares)
        for c in range(WIDTH // LANES)
    ]
    return groups, total, targets


def side_by_side(targets, width):
    out = targets[0]
    for k, target in enumerate(targets[1:]):
        out = out + pltpu.roll(target, (k + 1) * width, 1)
    return out


def near_kernel(part, place, *args):
    pieces, (tgt_group, src_ref, tgt_ref, slots) = args[:-4], args[-4:]
    for far, piece in enumerate(pieces):
        slots[lax.rem(place[0] + far, len(pieces))] = piece[...]
    groups, total, targets = source_joined(slots)
    for c, group in enumerate(groups):
        src_ref[8 * c : 8 * c + 8, :] = group
    src_ref[32:40, :] = total
    target = jnp.where(lower_lanes(), side_by_side(targets, part), tgt_group[8:16, :])
    for k in range(tgt_ref.shape[0]):
        tgt_ref[k] = target


def middle_kernel(got, src, out_ref):
    half = LANES // 2
    lower = lower_lanes()
    row_id = lax.broadcasted_iota(jnp.int32, (8, LANES), 0)
    each = [got[k] for k in range(got.shape[0])]
    counts = [jnp.where(lower, pltpu.roll(g, half, 1), g) for g in each]
    total, shares = joined_counts(counts)
    group = joined_group([jnp.where(lower, g, 0.0) for g in each], counts, shares)
    group = jnp.where(row_id < CLASSES, group, group / total)
    last = jnp.where(lower, group, src[32:40, :])
    for k in range(out_ref.shape[0]):
        out_ref[k, 0:32, :] = src[0:32, :]
        out_ref[k, 32:40, :] = last


def label_rows(width, core, got, src_sq, src_lab, label_ref, xa_ref):
    peers = got.shape[0]
    groups, total, targets = source_joined(
        got, [k + core * (peers - 1 - 2 * k) for k in range(peers)]
    )
    row_id = lax.broadcasted_iota(jnp.int32, (8, LANES), 0)
    lane_id = lax.broadcasted_iota(jnp.int32, (8, LANES), 1)
    each = LANES // width
    sides = ([], [])
    for c, group in enumerate(groups):
        tgt = side_by_side(targets[each * c : each * c + each], width)
        for side, stat in zip(sides, (jnp.where(row_id < CLASSES, group, group / total), tgt)):
            side.append(jnp.where(row_id < CLASSES, stat, jnp.sqrt(stat + 1e-06)))

    def distances(one, other):
        out = jnp.zeros((8, LANES), jnp.float32)
        for k in range(CLASSES):
            far = jnp.zeros((8, LANES), jnp.float32)
            for g, h in zip(one, other):
                gap = g - jnp.where(row_id < CLASSES, h[k : k + 1], h[CLASSES + k : CLASSES + k + 1])
                far = far + gap * gap
            far = far + pltpu.roll(far, 4, 0)
            out = jnp.where(lane_id == k, jnp.sum(far, axis=1, keepdims=True), out)
        return out

    label_ref[...] = distances(*sides)[:CLASSES, :CLASSES]
    by_target = distances(*sides[::-1])
    by_target = jnp.concatenate([by_target, by_target], axis=0)
    row_id = lax.broadcasted_iota(jnp.int32, (16, 1), 0)
    part_id = row_id // CLASSES
    labels = src_lab[...]
    u = jnp.broadcast_to(src_sq[...], (16, ROWS))
    for a in range(CLASSES):
        u = u + jnp.where(labels == a, by_target[:, a : a + 1], 0.0)
    hi, mid, lo = three_parts(-0.5 * u)
    ones = jnp.where(row_id < 15, 1.0, 0.0)
    xa_ref[...] = jnp.where(
        part_id == 0, hi, jnp.where(part_id == 1, mid, jnp.where(part_id == 2, lo, ones))
    ).astype(jnp.bfloat16)


def three_parts(v):
    hi = v.astype(jnp.bfloat16).astype(jnp.float32)
    rest = v - hi
    mid = rest.astype(jnp.bfloat16).astype(jnp.float32)
    return hi, mid, rest - mid


def joined_lse(g_ref):
    g = g_ref[...]
    top = jnp.max(g, axis=0)
    return top + log2(jnp.sum(jnp.exp2(g - top[None]), axis=0))


def row_finish(top, total, out_ref):
    lines = []
    for k in range(CHUNKS):
        at = pl.ds(k * LANES, LANES)
        lse = top[at, :] + log2(jnp.sum(total[at, :], axis=1, keepdims=True))
        lines.append(lse.T[0:1, :])
    line = jnp.concatenate(lines, axis=0)
    out_ref[...] = jnp.broadcast_to(line[None], out_ref.shape)


def widen_top(top):
    for k in range(CHUNKS):
        at = pl.ds(k * LANES, LANES)
        top[at, :] = jnp.broadcast_to(jnp.max(top[at, :], axis=1, keepdims=True), (LANES, LANES))


def over_pairs(count, body, unroll):
    def several(step, _):
        for k in range(unroll):
            body(step * unroll + k)
        return 0

    steps = (count[0] + UNROLL - 1) // UNROLL * (UNROLL // unroll)
    lax.fori_loop(0, steps, several, 0)


def block_at(pairs, index):
    row = pl.multiple_of(pairs[2 * index] * BLOCK, BLOCK)
    return row, pairs[2 * index + 1]


def cost_kernel(n_x, n_f, pairs, count, place, got, src_sq, src_lab, xt, *args):
    pieces, (tgt_lab, label_ref, tiles, out_ref, xa, y, ya, top, total) = args[:n_x], args[n_x:]
    label_rows(n_f, place[1], got, src_sq, src_lab, label_ref, xa)
    row_id = lax.broadcasted_iota(jnp.int32, (16, 1), 0)
    part = row_id // CLASSES
    cls = row_id % CLASSES

    tgt_sq = jnp.zeros((16, ROWS), jnp.float32)
    for far, piece in enumerate(pieces):
        at = lax.rem(place[0] + far, n_x)
        for k in range(piece.shape[0]):
            z = k + place[1] * (piece.shape[0] - 1 - 2 * k)
            y[pl.ds(pl.multiple_of((z * n_x + at) * 16, 16), 16), :] = piece[k]
            v = piece[k].astype(jnp.float32)
            tgt_sq = tgt_sq + v * v

    hi, mid, lo = three_parts(-0.5 * jnp.sum(tgt_sq, axis=0, keepdims=True))
    onehot = jnp.where(tgt_lab[...] == cls, 1.0, 0.0)
    ya[...] = jnp.where(
        part < 3,
        onehot,
        jnp.where(cls == 0, hi, jnp.where(cls == 1, mid, jnp.where(cls == 2, lo, 0.0))),
    ).astype(jnp.bfloat16)

    top[...] = jnp.full(top.shape, LOWEST, jnp.float32)
    total[...] = jnp.zeros(total.shape, jnp.float32)

    def build(index):
        row, col = block_at(pairs, index)
        rows = pl.ds(row, BLOCK)
        cols = pl.ds(pl.multiple_of(col * BLOCK, BLOCK), BLOCK)
        cross = jnp.dot(xt[rows, :], y[:, cols], preferred_element_type=jnp.float32)
        extra = lax.dot_general(
            xa[:, rows], ya[:, cols], (((0,), (0,)), ((), ())), preferred_element_type=jnp.float32
        )
        tile = (cross + extra) * (2.0 * TO_LOG2) + jnp.where(index < count[0], 0.0, LOWEST)
        tiles[index] = tile
        top[rows, :] = jnp.maximum(top[rows, :], jnp.maximum(tile[:, :LANES], tile[:, LANES:]))

    over_pairs(count, build, 4)
    widen_top(top)

    def add(index):
        row, _ = block_at(pairs, index)
        rows = pl.ds(row, BLOCK)
        high = top[rows, :]
        left = jnp.exp2(tiles[index, :, :LANES] - high)
        right = jnp.exp2(tiles[index, :, LANES:] - high)
        total[rows, :] = total[rows, :] + (left + right)

    over_pairs(count, add, 4)
    row_finish(top, total, out_ref)


def row_kernel(log_total, pairs, count, tiles, g_ref, out_ref, pot, top, total):
    pot[...] = log_total - joined_lse(g_ref)
    top[...] = jnp.full(top.shape, LOWEST, jnp.float32)
    total[...] = jnp.zeros(total.shape, jnp.float32)

    def scores(index, col):
        left = tiles[index, :, :LANES] + pot[pl.ds(2 * col, 1), :]
        right = tiles[index, :, LANES:] + pot[pl.ds(2 * col + 1, 1), :]
        return left, right

    def highest(index):
        row, col = block_at(pairs, index)
        rows = pl.ds(row, BLOCK)
        left, right = scores(index, col)
        top[rows, :] = jnp.maximum(top[rows, :], jnp.maximum(left, right))

    over_pairs(count, highest, 4)
    widen_top(top)

    def add(index):
        row, col = block_at(pairs, index)
        rows = pl.ds(row, BLOCK)
        left, right = scores(index, col)
        high = top[rows, :]
        total[rows, :] = total[rows, :] + (jnp.exp2(left - high) + jnp.exp2(right - high))

    over_pairs(count, add, 4)
    row_finish(top, total, out_ref)


def col_kernel(log_total, pairs, count, tiles, g_ref, out_ref, pot_ref, pot, top, total):
    line = log_total - joined_lse(g_ref)
    pot_ref[...] = line * TO_POT
    for k in range(CHUNKS):
        pot[pl.ds(k * LANES, LANES), :] = jnp.broadcast_to(line[k : k + 1, :], (LANES, LANES)).T
    top[...] = jnp.full(top.shape, LOWEST, jnp.float32)
    total[...] = jnp.zeros(total.shape, jnp.float32)

    def scores(index, row):
        rows = pl.ds(row, BLOCK)
        high = pot[rows, :]
        tile = tiles[index]
        return tile + jnp.concatenate([high, high], axis=1)

    def highest(index):
        row, col = block_at(pairs, index)
        score = scores(index, row)
        top[col] = jnp.maximum(top[col], jnp.max(score.reshape(BLOCK // 8, 8, BLOCK), axis=0))

    over_pairs(count, highest, 4)
    for k in range(BLK):
        top[k] = jnp.broadcast_to(jnp.max(top[k], axis=0, keepdims=True), (8, BLOCK))

    def add(index):
        row, col = block_at(pairs, index)
        score = scores(index, row).reshape(BLOCK // 8, 8, BLOCK)
        total[col] = total[col] + jnp.sum(jnp.exp2(score - top[col][None]), axis=0)

    over_pairs(count, add, 4)
    lines = []
    for k in range(BLK):
        lse = top[k][0:1] + log2(jnp.sum(total[k], axis=0, keepdims=True))
        lines += [lse[:, :LANES], lse[:, LANES:]]
    out = jnp.concatenate(lines, axis=0)
    out_ref[...] = jnp.broadcast_to(out[None], out_ref.shape)


def last_kernel(log_total, g_ref, pot_ref):
    pot_ref[...] = (log_total - joined_lse(g_ref)) * TO_POT


def smem():
    return pl.BlockSpec(memory_space=pltpu.SMEM)


def vmem():
    return pl.BlockSpec(memory_space=pltpu.VMEM)


def f32(*shape):
    return jax.ShapeDtypeStruct(shape, jnp.float32)


def params():
    return pltpu.CompilerParams(vmem_limit_bytes=VMEM_LIMIT)


def both_ways(x, axes):
    n = x.shape[0]
    groups = [[2 * k for k in range(n)], [2 * k + 1 for k in reversed(range(n))]]
    return lax.all_to_all(x, axes + ("c",), 0, 0, axis_index_groups=groups)


def on_device(source_embed, target_embed, source_labels, target_labels, pair_blocks, pair_count):
    pairs = pair_blocks.reshape(-1)
    count = pair_count.reshape(-1)
    n_src, n_tgt = lax.axis_size(SRC), lax.axis_size(TGT)

    def call(kernel, out_shape, *args, name):
        return pl.pallas_call(
            kernel,
            out_shape=out_shape,
            in_specs=[vmem()] * len(args),
            out_specs=jax.tree.map(lambda _: vmem(), out_shape),
            compiler_params=params(),
            name=name,
        )(*args)

    n_x, n_z = lax.axis_size("x"), lax.axis_size("z")
    part = target_embed.shape[0]
    near, tgt_group = pl.pallas_call(
        first_kernel,
        out_shape=(
            jax.ShapeDtypeStruct((n_z,) + target_embed.shape, jnp.bfloat16),
            f32(16, LANES),
        ),
        in_specs=[vmem(), vmem()],
        out_specs=(pl.BlockSpec(memory_space=pl.ANY), vmem()),
        scratch_shapes=[pltpu.SemaphoreType.DMA((n_z,))],
        compiler_params=params(),
        name="first",
    )(target_embed, target_labels[None])
    near = both_ways(near, ("z",))

    def around(x, axis):
        n = lax.axis_size(axis)
        return [x] + [
            lax.ppermute(x, axis, [((i + far) % n, i) for i in range(n)]) for far in range(1, n)
        ]

    src_group, src_sq = call(
        source_group_kernel,
        (f32(40, LANES), f32(1, ROWS)),
        source_embed,
        source_labels[None],
        tgt_group,
        name="source_group",
    )

    near, packets = lax.optimization_barrier((near, around(src_group, "x")))
    pieces = around(near, "x")
    src_group, tgt_near = pl.pallas_call(
        functools.partial(near_kernel, part),
        out_shape=(f32(40, LANES), f32(n_tgt, 8, LANES)),
        in_specs=[smem()] + [vmem()] * (n_x + 1),
        out_specs=(vmem(), vmem()),
        scratch_shapes=[pltpu.VMEM((n_x, 40, LANES), jnp.float32)],
        compiler_params=params(),
        name="near",
    )(lax.axis_index("x").reshape(1), *packets, tgt_group)
    tgt_near = lax.all_to_all(tgt_near, TGT, 0, 0)
    tgt_near, source_tall = lax.optimization_barrier((tgt_near, source_embed.T))
    stats = call(middle_kernel, f32(n_z, 40, LANES), tgt_near, src_group, name="middle")
    stats = both_ways(stats, ("z",))

    tall = pltpu.VMEM((ROWS, LANES), jnp.float32)
    wide = pltpu.VMEM((BLK, 8, BLOCK), jnp.float32)
    log_src = math.log2(ROWS * n_src)
    log_tgt = math.log2(ROWS * n_tgt)
    label_cost, tiles, sent = pl.pallas_call(
        functools.partial(cost_kernel, n_x, part * n_x),
        out_shape=(
            f32(CLASSES, CLASSES),
            f32(MAXP, BLOCK, BLOCK),
            f32(n_tgt, CHUNKS, LANES),
        ),
        in_specs=[smem()] * 3 + [vmem()] * (5 + n_x),
        out_specs=(vmem(), vmem(), vmem()),
        scratch_shapes=[
            pltpu.VMEM((16, ROWS), jnp.bfloat16),
            pltpu.VMEM((WIDTH, ROWS), jnp.bfloat16),
            pltpu.VMEM((16, ROWS), jnp.bfloat16),
            tall,
            tall,
        ],
        compiler_params=params(),
        name="cost_rows",
    )(
        pairs,
        count,
        jnp.stack([lax.axis_index("x"), lax.axis_index("c")]),
        stats,
        src_sq,
        source_labels[None],
        source_tall,
        *pieces,
        target_labels[None],
    )

    def columns(got):
        return pl.pallas_call(
            functools.partial(col_kernel, log_tgt),
            out_shape=(f32(n_src, CHUNKS, LANES), f32(CHUNKS, LANES)),
            in_specs=[smem(), smem(), vmem(), vmem()],
            out_specs=(vmem(), vmem()),
            scratch_shapes=[tall, wide, wide],
            compiler_params=params(),
            name="columns",
        )(pairs, count, tiles, got)

    def rows(got):
        return pl.pallas_call(
            functools.partial(row_kernel, log_src),
            out_shape=f32(n_tgt, CHUNKS, LANES),
            in_specs=[smem(), smem(), vmem(), vmem()],
            out_specs=vmem(),
            scratch_shapes=[pltpu.VMEM((CHUNKS, LANES), jnp.float32), tall, tall],
            compiler_params=params(),
            name="rows",
        )(pairs, count, tiles, got)

    sent, _ = columns(lax.all_to_all(sent, TGT, 0, 0))
    sent = rows(lax.all_to_all(sent, SRC, 0, 0))
    sent, src_pot = columns(lax.all_to_all(sent, TGT, 0, 0))
    tgt_pot = pl.pallas_call(
        functools.partial(last_kernel, log_src),
        out_shape=f32(CHUNKS, LANES),
        in_specs=[vmem()],
        out_specs=vmem(),
        compiler_params=params(),
        name="last",
    )(lax.all_to_all(sent, SRC, 0, 0))
    return (src_pot.reshape(-1), tgt_pot.reshape(-1), label_cost)


def solution(mesh):
    fine = Mesh(np.asarray(mesh.devices).reshape(8, 4, 4, 2), SRC + TGT)
    return jax.shard_map(
        on_device,
        mesh=fine,
        in_specs=(
            P(None, SRC),
            P(SRC, TGT),
            P(SRC),
            P(TGT),
            P(SRC, TGT, None, None),
            P(SRC, TGT),
        ),
        out_specs=(P(SRC), P(TGT), P()),
        check_vma=False,
    )
```

```python
import functools
import math

import jax
import jax.numpy as jnp
import numpy as np
from jax import lax
from jax.experimental import pallas as pl
from jax.experimental.pallas import tpu as pltpu
from jax.sharding import Mesh, PartitionSpec as P

CLASSES = 4
BLOCK = 256
ROWS = 2048
BLK = ROWS // BLOCK
LANES = 128
CHUNKS = ROWS // LANES
MAXP = 24
UNROLL = 8
WIDTH = 512

EPSILON = 0.05
LOWEST = -1e30
LOG2E = 1.0 / math.log(2.0)
TO_LOG2 = LOG2E / EPSILON
TO_POT = EPSILON / LOG2E

SRC = ("z", "x")
TGT = ("y", "c")
VMEM_LIMIT = 24 * 1024 * 1024


def log2(x):
    return jnp.log(x) * LOG2E


def repeated_onehot(labels):
    row_id = lax.broadcasted_iota(jnp.int32, (16, 1), 0)
    return jnp.where(row_id < 12, jnp.where(labels == row_id % CLASSES, 1.0, 0.0), 0.0)


def across(onehot, values):
    return lax.dot_general(
        onehot, values, (((1,), (1,)), ((), ())), preferred_element_type=jnp.float32
    )


def class_group(values, onehot, counts):
    part = lax.broadcasted_iota(jnp.int32, (16, 1), 0) // CLASSES
    wide = values.astype(jnp.float32)
    mean = across(onehot, values) / counts
    hi, mid, lo = three_parts(mean)
    parts = jnp.where(
        part == 0, hi, jnp.where(part == 1, mid, jnp.where(part == 2, lo, 0.0))
    ).astype(jnp.bfloat16)
    center = lax.dot_general(
        parts, onehot, (((0,), (0,)), ((), ())), preferred_element_type=jnp.float32
    )
    centered = wide - center
    hi, mid, lo = three_parts(centered * centered)
    spread = sum(across(onehot, p.astype(jnp.bfloat16)) for p in (hi, mid, lo))
    return jnp.where(part == 0, mean, spread)[:8], wide


def first_kernel(embed, labels, near_ref, out_ref, sems):
    copies = [
        pltpu.make_async_copy(embed, near_ref.at[k], sems.at[k]) for k in range(near_ref.shape[0])
    ]
    for copy in copies:
        copy.start()
    onehot = repeated_onehot(labels[...])
    counts = jnp.maximum(jnp.sum(onehot, axis=1, keepdims=True), 1.0)
    group, _ = class_group(embed[...], onehot.astype(jnp.bfloat16), counts)
    out_ref[...] = jnp.zeros(out_ref.shape, jnp.float32)
    out_ref[0:8, 0 : group.shape[1]] = group
    out_ref[8:16, :] = jnp.broadcast_to(counts[:8], (8, LANES))
    for copy in copies:
        copy.wait()


def lower_lanes():
    return lax.broadcasted_iota(jnp.int32, (8, LANES), 1) < LANES // 2


def source_group_kernel(embed, labels, tgt_group, out_ref, sq_ref):
    onehot = repeated_onehot(labels[...])
    counts = jnp.maximum(jnp.sum(onehot, axis=1, keepdims=True), 1.0)
    onehot = onehot.astype(jnp.bfloat16)
    sq = jnp.zeros((1, ROWS), jnp.float32)
    for c in range(WIDTH // LANES):
        group, wide = class_group(embed[c * LANES : (c + 1) * LANES, :], onehot, counts)
        out_ref[8 * c : 8 * c + 8, :] = group
        sq = sq + jnp.sum(wide * wide, axis=0, keepdims=True)
    out_ref[32:40, :] = jnp.where(lower_lanes(), tgt_group[0:8, :], counts[:8])
    sq_ref[...] = sq


def joined_counts(counts):
    total = functools.reduce(jnp.add, counts)
    return total, [c / total for c in counts]


def joined_group(groups, counts, shares):
    row_id = lax.broadcasted_iota(jnp.int32, (8, LANES), 0)
    mean = functools.reduce(jnp.add, [g * w for g, w in zip(groups, shares)])
    between = functools.reduce(
        jnp.add, [(g - mean) * (g - mean) * c for g, c in zip(groups, counts)]
    )
    spread = functools.reduce(jnp.add, groups) + pltpu.roll(between, 4, 0)
    return jnp.where(row_id < CLASSES, mean, spread)


def source_joined(got, order=None):
    peers = got.shape[0]
    order = range(peers) if order is None else order
    half = LANES // 2
    lower = lower_lanes()
    last = [got[k, 32:40, :] for k in order]
    targets = [jnp.where(lower, g, 0.0) for g in last]
    counts = [jnp.where(lower, pltpu.roll(g, half, 1), g) for g in last]
    total, shares = joined_counts(counts)
    groups = [
        joined_group([got[k, 8 * c : 8 * c + 8, :] for k in order], counts, shares)
        for c in range(WIDTH // LANES)
    ]
    return groups, total, targets


def side_by_side(targets, width):
    out = targets[0]
    for k, target in enumerate(targets[1:]):
        out = out + pltpu.roll(target, (k + 1) * width, 1)
    return out


def near_kernel(part, place, *args):
    pieces, (tgt_group, src_ref, tgt_ref, slots) = args[:-4], args[-4:]
    for far, piece in enumerate(pieces):
        slots[lax.rem(place[0] + far, len(pieces))] = piece[...]
    groups, total, targets = source_joined(slots)
    for c, group in enumerate(groups):
        src_ref[8 * c : 8 * c + 8, :] = group
    src_ref[32:40, :] = total
    target = jnp.where(lower_lanes(), side_by_side(targets, part), tgt_group[8:16, :])
    for k in range(tgt_ref.shape[0]):
        tgt_ref[k] = target


def middle_kernel(got, src, out_ref):
    half = LANES // 2
    lower = lower_lanes()
    row_id = lax.broadcasted_iota(jnp.int32, (8, LANES), 0)
    each = [got[k] for k in range(got.shape[0])]
    counts = [jnp.where(lower, pltpu.roll(g, half, 1), g) for g in each]
    total, shares = joined_counts(counts)
    group = joined_group([jnp.where(lower, g, 0.0) for g in each], counts, shares)
    group = jnp.where(row_id < CLASSES, group, group / total)
    last = jnp.where(lower, group, src[32:40, :])
    for k in range(out_ref.shape[0]):
        out_ref[k, 0:32, :] = src[0:32, :]
        out_ref[k, 32:40, :] = last


def label_rows(width, core, got, src_sq, src_lab, label_ref, xa_ref):
    peers = got.shape[0]
    groups, total, targets = source_joined(
        got, [k + core * (peers - 1 - 2 * k) for k in range(peers)]
    )
    row_id = lax.broadcasted_iota(jnp.int32, (8, LANES), 0)
    lane_id = lax.broadcasted_iota(jnp.int32, (8, LANES), 1)
    each = LANES // width
    sides = ([], [])
    for c, group in enumerate(groups):
        tgt = side_by_side(targets[each * c : each * c + each], width)
        for side, stat in zip(sides, (jnp.where(row_id < CLASSES, group, group / total), tgt)):
            side.append(jnp.where(row_id < CLASSES, stat, jnp.sqrt(stat + 1e-06)))

    def distances(one, other):
        out = jnp.zeros((8, LANES), jnp.float32)
        for k in range(CLASSES):
            far = jnp.zeros((8, LANES), jnp.float32)
            for g, h in zip(one, other):
                gap = g - jnp.where(row_id < CLASSES, h[k : k + 1], h[CLASSES + k : CLASSES + k + 1])
                far = far + gap * gap
            far = far + pltpu.roll(far, 4, 0)
            out = jnp.where(lane_id == k, jnp.sum(far, axis=1, keepdims=True), out)
        return out

    label_ref[...] = distances(*sides)[:CLASSES, :CLASSES]
    by_target = distances(*sides[::-1])
    by_target = jnp.concatenate([by_target, by_target], axis=0)
    row_id = lax.broadcasted_iota(jnp.int32, (16, 1), 0)
    part_id = row_id // CLASSES
    labels = src_lab[...]
    u = jnp.broadcast_to(src_sq[...], (16, ROWS))
    for a in range(CLASSES):
        u = u + jnp.where(labels == a, by_target[:, a : a + 1], 0.0)
    hi, mid, lo = three_parts(-0.5 * u)
    ones = jnp.where(row_id < 15, 1.0, 0.0)
    xa_ref[...] = jnp.where(
        part_id == 0, hi, jnp.where(part_id == 1, mid, jnp.where(part_id == 2, lo, ones))
    ).astype(jnp.bfloat16)


def three_parts(v):
    hi = v.astype(jnp.bfloat16).astype(jnp.float32)
    rest = v - hi
    mid = rest.astype(jnp.bfloat16).astype(jnp.float32)
    return hi, mid, rest - mid


def joined_lse(g_ref):
    g = g_ref[...]
    top = jnp.max(g, axis=0)
    return top + log2(jnp.sum(jnp.exp2(g - top[None]), axis=0))


def row_finish(top, total, out_ref):
    lines = []
    for k in range(CHUNKS):
        at = pl.ds(k * LANES, LANES)
        lse = top[at, :] + log2(jnp.sum(total[at, :], axis=1, keepdims=True))
        lines.append(lse.T[0:1, :])
    line = jnp.concatenate(lines, axis=0)
    out_ref[...] = jnp.broadcast_to(line[None], out_ref.shape)


def widen_top(top):
    for k in range(CHUNKS):
        at = pl.ds(k * LANES, LANES)
        top[at, :] = jnp.broadcast_to(jnp.max(top[at, :], axis=1, keepdims=True), (LANES, LANES))


def over_pairs(count, body, unroll):
    def several(step, _):
        for k in range(unroll):
            body(step * unroll + k)
        return 0

    steps = (count[0] + UNROLL - 1) // UNROLL * (UNROLL // unroll)
    lax.fori_loop(0, steps, several, 0)


def block_at(pairs, index):
    row = pl.multiple_of(pairs[2 * index] * BLOCK, BLOCK)
    return row, pairs[2 * index + 1]


def cost_kernel(n_x, n_f, pairs, count, place, got, src_sq, src_lab, xt, *args):
    pieces, (tgt_lab, label_ref, tiles, out_ref, xa, y, ya, top, total) = args[:n_x], args[n_x:]
    label_rows(n_f, place[1], got, src_sq, src_lab, label_ref, xa)
    row_id = lax.broadcasted_iota(jnp.int32, (16, 1), 0)
    part = row_id // CLASSES
    cls = row_id % CLASSES

    tgt_sq = jnp.zeros((16, ROWS), jnp.float32)
    for far, piece in enumerate(pieces):
        at = lax.rem(place[0] + far, n_x)
        for k in range(piece.shape[0]):
            z = k + place[1] * (piece.shape[0] - 1 - 2 * k)
            y[pl.ds(pl.multiple_of((z * n_x + at) * 16, 16), 16), :] = piece[k]
            v = piece[k].astype(jnp.float32)
            tgt_sq = tgt_sq + v * v

    hi, mid, lo = three_parts(-0.5 * jnp.sum(tgt_sq, axis=0, keepdims=True))
    onehot = jnp.where(tgt_lab[...] == cls, 1.0, 0.0)
    ya[...] = jnp.where(
        part < 3,
        onehot,
        jnp.where(cls == 0, hi, jnp.where(cls == 1, mid, jnp.where(cls == 2, lo, 0.0))),
    ).astype(jnp.bfloat16)

    top[...] = jnp.full(top.shape, LOWEST, jnp.float32)
    total[...] = jnp.zeros(total.shape, jnp.float32)

    def build(index):
        row, col = block_at(pairs, index)
        rows = pl.ds(row, BLOCK)
        cols = pl.ds(pl.multiple_of(col * BLOCK, BLOCK), BLOCK)
        cross = jnp.dot(xt[rows, :], y[:, cols], preferred_element_type=jnp.float32)
        extra = lax.dot_general(
            xa[:, rows], ya[:, cols], (((0,), (0,)), ((), ())), preferred_element_type=jnp.float32
        )
        tile = (cross + extra) * (2.0 * TO_LOG2) + jnp.where(index < count[0], 0.0, LOWEST)
        tiles[index] = tile
        top[rows, :] = jnp.maximum(top[rows, :], jnp.maximum(tile[:, :LANES], tile[:, LANES:]))

    over_pairs(count, build, 8)
    widen_top(top)

    def add(index):
        row, _ = block_at(pairs, index)
        rows = pl.ds(row, BLOCK)
        high = top[rows, :]
        left = jnp.exp2(tiles[index, :, :LANES] - high)
        right = jnp.exp2(tiles[index, :, LANES:] - high)
        total[rows, :] = total[rows, :] + (left + right)

    over_pairs(count, add, 4)
    row_finish(top, total, out_ref)


def row_kernel(log_total, pairs, count, tiles, g_ref, out_ref, pot, top, total):
    pot[...] = log_total - joined_lse(g_ref)
    top[...] = jnp.full(top.shape, LOWEST, jnp.float32)
    total[...] = jnp.zeros(total.shape, jnp.float32)

    def scores(index, col):
        left = tiles[index, :, :LANES] + pot[pl.ds(2 * col, 1), :]
        right = tiles[index, :, LANES:] + pot[pl.ds(2 * col + 1, 1), :]
        return left, right

    def highest(index):
        row, col = block_at(pairs, index)
        rows = pl.ds(row, BLOCK)
        left, right = scores(index, col)
        top[rows, :] = jnp.maximum(top[rows, :], jnp.maximum(left, right))

    over_pairs(count, highest, 4)
    widen_top(top)

    def add(index):
        row, col = block_at(pairs, index)
        rows = pl.ds(row, BLOCK)
        left, right = scores(index, col)
        high = top[rows, :]
        total[rows, :] = total[rows, :] + (jnp.exp2(left - high) + jnp.exp2(right - high))

    over_pairs(count, add, 4)
    row_finish(top, total, out_ref)


def col_kernel(log_total, pairs, count, tiles, g_ref, out_ref, pot_ref, pot, top, total):
    line = log_total - joined_lse(g_ref)
    pot_ref[...] = line * TO_POT
    for k in range(CHUNKS):
        pot[pl.ds(k * LANES, LANES), :] = jnp.broadcast_to(line[k : k + 1, :], (LANES, LANES)).T
    top[...] = jnp.full(top.shape, LOWEST, jnp.float32)
    total[...] = jnp.zeros(total.shape, jnp.float32)

    def scores(index, row):
        rows = pl.ds(row, BLOCK)
        high = pot[rows, :]
        tile = tiles[index]
        return tile + jnp.concatenate([high, high], axis=1)

    def highest(index):
        row, col = block_at(pairs, index)
        score = scores(index, row)
        top[col] = jnp.maximum(top[col], jnp.max(score.reshape(BLOCK // 8, 8, BLOCK), axis=0))

    over_pairs(count, highest, 4)
    for k in range(BLK):
        top[k] = jnp.broadcast_to(jnp.max(top[k], axis=0, keepdims=True), (8, BLOCK))

    def add(index):
        row, col = block_at(pairs, index)
        score = scores(index, row).reshape(BLOCK // 8, 8, BLOCK)
        total[col] = total[col] + jnp.sum(jnp.exp2(score - top[col][None]), axis=0)

    over_pairs(count, add, 4)
    lines = []
    for k in range(BLK):
        lse = top[k][0:1] + log2(jnp.sum(total[k], axis=0, keepdims=True))
        lines += [lse[:, :LANES], lse[:, LANES:]]
    out = jnp.concatenate(lines, axis=0)
    out_ref[...] = jnp.broadcast_to(out[None], out_ref.shape)


def last_kernel(log_total, g_ref, pot_ref):
    pot_ref[...] = (log_total - joined_lse(g_ref)) * TO_POT


def smem():
    return pl.BlockSpec(memory_space=pltpu.SMEM)


def vmem():
    return pl.BlockSpec(memory_space=pltpu.VMEM)


def f32(*shape):
    return jax.ShapeDtypeStruct(shape, jnp.float32)


def params():
    return pltpu.CompilerParams(vmem_limit_bytes=VMEM_LIMIT)


def both_ways(x, axes):
    n = x.shape[0]
    groups = [[2 * k for k in range(n)], [2 * k + 1 for k in reversed(range(n))]]
    return lax.all_to_all(x, axes + ("c",), 0, 0, axis_index_groups=groups)


def on_device(source_embed, target_embed, source_labels, target_labels, pair_blocks, pair_count):
    pairs = pair_blocks.reshape(-1)
    count = pair_count.reshape(-1)
    n_src, n_tgt = lax.axis_size(SRC), lax.axis_size(TGT)

    def call(kernel, out_shape, *args, name):
        return pl.pallas_call(
            kernel,
            out_shape=out_shape,
            in_specs=[vmem()] * len(args),
            out_specs=jax.tree.map(lambda _: vmem(), out_shape),
            compiler_params=params(),
            name=name,
        )(*args)

    n_x, n_z = lax.axis_size("x"), lax.axis_size("z")
    part = target_embed.shape[0]
    near, tgt_group = pl.pallas_call(
        first_kernel,
        out_shape=(
            jax.ShapeDtypeStruct((n_z,) + target_embed.shape, jnp.bfloat16),
            f32(16, LANES),
        ),
        in_specs=[vmem(), vmem()],
        out_specs=(pl.BlockSpec(memory_space=pl.ANY), vmem()),
        scratch_shapes=[pltpu.SemaphoreType.DMA((n_z,))],
        compiler_params=params(),
        name="first",
    )(target_embed, target_labels[None])
    near = both_ways(near, ("z",))

    def around(x, axis):
        n = lax.axis_size(axis)
        return [x] + [
            lax.ppermute(x, axis, [((i + far) % n, i) for i in range(n)]) for far in range(1, n)
        ]

    src_group, src_sq = call(
        source_group_kernel,
        (f32(40, LANES), f32(1, ROWS)),
        source_embed,
        source_labels[None],
        tgt_group,
        name="source_group",
    )

    near, packets = lax.optimization_barrier((near, around(src_group, "x")))
    pieces = around(near, "x")
    src_group, tgt_near = pl.pallas_call(
        functools.partial(near_kernel, part),
        out_shape=(f32(40, LANES), f32(n_tgt, 8, LANES)),
        in_specs=[smem()] + [vmem()] * (n_x + 1),
        out_specs=(vmem(), vmem()),
        scratch_shapes=[pltpu.VMEM((n_x, 40, LANES), jnp.float32)],
        compiler_params=params(),
        name="near",
    )(lax.axis_index("x").reshape(1), *packets, tgt_group)
    tgt_near = lax.all_to_all(tgt_near, TGT, 0, 0)
    tgt_near, source_tall = lax.optimization_barrier((tgt_near, source_embed.T))
    stats = call(middle_kernel, f32(n_z, 40, LANES), tgt_near, src_group, name="middle")
    stats = both_ways(stats, ("z",))

    tall = pltpu.VMEM((ROWS, LANES), jnp.float32)
    wide = pltpu.VMEM((BLK, 8, BLOCK), jnp.float32)
    log_src = math.log2(ROWS * n_src)
    log_tgt = math.log2(ROWS * n_tgt)
    label_cost, tiles, sent = pl.pallas_call(
        functools.partial(cost_kernel, n_x, part * n_x),
        out_shape=(
            f32(CLASSES, CLASSES),
            f32(MAXP, BLOCK, BLOCK),
            f32(n_tgt, CHUNKS, LANES),
        ),
        in_specs=[smem()] * 3 + [vmem()] * (5 + n_x),
        out_specs=(vmem(), vmem(), vmem()),
        scratch_shapes=[
            pltpu.VMEM((16, ROWS), jnp.bfloat16),
            pltpu.VMEM((WIDTH, ROWS), jnp.bfloat16),
            pltpu.VMEM((16, ROWS), jnp.bfloat16),
            tall,
            tall,
        ],
        compiler_params=params(),
        name="cost_rows",
    )(
        pairs,
        count,
        jnp.stack([lax.axis_index("x"), lax.axis_index("c")]),
        stats,
        src_sq,
        source_labels[None],
        source_tall,
        *pieces,
        target_labels[None],
    )

    def columns(got):
        return pl.pallas_call(
            functools.partial(col_kernel, log_tgt),
            out_shape=(f32(n_src, CHUNKS, LANES), f32(CHUNKS, LANES)),
            in_specs=[smem(), smem(), vmem(), vmem()],
            out_specs=(vmem(), vmem()),
            scratch_shapes=[tall, wide, wide],
            compiler_params=params(),
            name="columns",
        )(pairs, count, tiles, got)

    def rows(got):
        return pl.pallas_call(
            functools.partial(row_kernel, log_src),
            out_shape=f32(n_tgt, CHUNKS, LANES),
            in_specs=[smem(), smem(), vmem(), vmem()],
            out_specs=vmem(),
            scratch_shapes=[pltpu.VMEM((CHUNKS, LANES), jnp.float32), tall, tall],
            compiler_params=params(),
            name="rows",
        )(pairs, count, tiles, got)

    sent, _ = columns(lax.all_to_all(sent, TGT, 0, 0))
    sent = rows(lax.all_to_all(sent, SRC, 0, 0))
    sent, src_pot = columns(lax.all_to_all(sent, TGT, 0, 0))
    tgt_pot = pl.pallas_call(
        functools.partial(last_kernel, log_src),
        out_shape=f32(CHUNKS, LANES),
        in_specs=[vmem()],
        out_specs=vmem(),
        compiler_params=params(),
        name="last",
    )(lax.all_to_all(sent, SRC, 0, 0))
    return (src_pot.reshape(-1), tgt_pot.reshape(-1), label_cost)


def solution(mesh):
    fine = Mesh(np.asarray(mesh.devices).reshape(8, 4, 4, 2), SRC + TGT)
    return jax.shard_map(
        on_device,
        mesh=fine,
        in_specs=(
            P(None, SRC),
            P(SRC, TGT),
            P(SRC),
            P(TGT),
            P(SRC, TGT, None, None),
            P(SRC, TGT),
        ),
        out_specs=(P(SRC), P(TGT), P()),
        check_vma=False,
    )
```

```python
import functools
import math

import jax
import jax.numpy as jnp
import numpy as np
from jax import lax
from jax.experimental import pallas as pl
from jax.experimental.pallas import tpu as pltpu
from jax.sharding import Mesh, PartitionSpec as P

CLASSES = 4
BLOCK = 256
ROWS = 2048
BLK = ROWS // BLOCK
LANES = 128
CHUNKS = ROWS // LANES
MAXP = 24
UNROLL = 12
WIDTH = 512

EPSILON = 0.05
LOWEST = -1e30
LOG2E = 1.0 / math.log(2.0)
TO_LOG2 = LOG2E / EPSILON
TO_POT = EPSILON / LOG2E

SRC = ("z", "x")
TGT = ("y", "c")
VMEM_LIMIT = 24 * 1024 * 1024


def log2(x):
    return jnp.log(x) * LOG2E


def repeated_onehot(labels):
    row_id = lax.broadcasted_iota(jnp.int32, (16, 1), 0)
    return jnp.where(row_id < 12, jnp.where(labels == row_id % CLASSES, 1.0, 0.0), 0.0)


def across(onehot, values):
    return lax.dot_general(
        onehot, values, (((1,), (1,)), ((), ())), preferred_element_type=jnp.float32
    )


def class_group(values, onehot, counts):
    part = lax.broadcasted_iota(jnp.int32, (16, 1), 0) // CLASSES
    wide = values.astype(jnp.float32)
    mean = across(onehot, values) / counts
    hi, mid, lo = three_parts(mean)
    parts = jnp.where(
        part == 0, hi, jnp.where(part == 1, mid, jnp.where(part == 2, lo, 0.0))
    ).astype(jnp.bfloat16)
    center = lax.dot_general(
        parts, onehot, (((0,), (0,)), ((), ())), preferred_element_type=jnp.float32
    )
    centered = wide - center
    hi, mid, lo = three_parts(centered * centered)
    spread = sum(across(onehot, p.astype(jnp.bfloat16)) for p in (hi, mid, lo))
    return jnp.where(part == 0, mean, spread)[:8], wide


def first_kernel(embed, labels, near_ref, out_ref, sems):
    copies = [
        pltpu.make_async_copy(embed, near_ref.at[k], sems.at[k]) for k in range(near_ref.shape[0])
    ]
    for copy in copies:
        copy.start()
    onehot = repeated_onehot(labels[...])
    counts = jnp.maximum(jnp.sum(onehot, axis=1, keepdims=True), 1.0)
    group, _ = class_group(embed[...], onehot.astype(jnp.bfloat16), counts)
    out_ref[...] = jnp.zeros(out_ref.shape, jnp.float32)
    out_ref[0:8, 0 : group.shape[1]] = group
    out_ref[8:16, :] = jnp.broadcast_to(counts[:8], (8, LANES))
    for copy in copies:
        copy.wait()


def lower_lanes():
    return lax.broadcasted_iota(jnp.int32, (8, LANES), 1) < LANES // 2


def source_group_kernel(embed, labels, tgt_group, out_ref, sq_ref):
    onehot = repeated_onehot(labels[...])
    counts = jnp.maximum(jnp.sum(onehot, axis=1, keepdims=True), 1.0)
    onehot = onehot.astype(jnp.bfloat16)
    sq = jnp.zeros((1, ROWS), jnp.float32)
    for c in range(WIDTH // LANES):
        group, wide = class_group(embed[c * LANES : (c + 1) * LANES, :], onehot, counts)
        out_ref[8 * c : 8 * c + 8, :] = group
        sq = sq + jnp.sum(wide * wide, axis=0, keepdims=True)
    out_ref[32:40, :] = jnp.where(lower_lanes(), tgt_group[0:8, :], counts[:8])
    sq_ref[...] = sq


def joined_counts(counts):
    total = functools.reduce(jnp.add, counts)
    return total, [c / total for c in counts]


def joined_group(groups, counts, shares):
    row_id = lax.broadcasted_iota(jnp.int32, (8, LANES), 0)
    mean = functools.reduce(jnp.add, [g * w for g, w in zip(groups, shares)])
    between = functools.reduce(
        jnp.add, [(g - mean) * (g - mean) * c for g, c in zip(groups, counts)]
    )
    spread = functools.reduce(jnp.add, groups) + pltpu.roll(between, 4, 0)
    return jnp.where(row_id < CLASSES, mean, spread)


def source_joined(got, order=None):
    peers = got.shape[0]
    order = range(peers) if order is None else order
    half = LANES // 2
    lower = lower_lanes()
    last = [got[k, 32:40, :] for k in order]
    targets = [jnp.where(lower, g, 0.0) for g in last]
    counts = [jnp.where(lower, pltpu.roll(g, half, 1), g) for g in last]
    total, shares = joined_counts(counts)
    groups = [
        joined_group([got[k, 8 * c : 8 * c + 8, :] for k in order], counts, shares)
        for c in range(WIDTH // LANES)
    ]
    return groups, total, targets


def side_by_side(targets, width):
    out = targets[0]
    for k, target in enumerate(targets[1:]):
        out = out + pltpu.roll(target, (k + 1) * width, 1)
    return out


def near_kernel(part, place, *args):
    pieces, (tgt_group, src_ref, tgt_ref, slots) = args[:-4], args[-4:]
    for far, piece in enumerate(pieces):
        slots[lax.rem(place[0] + far, len(pieces))] = piece[...]
    groups, total, targets = source_joined(slots)
    for c, group in enumerate(groups):
        src_ref[8 * c : 8 * c + 8, :] = group
    src_ref[32:40, :] = total
    target = jnp.where(lower_lanes(), side_by_side(targets, part), tgt_group[8:16, :])
    for k in range(tgt_ref.shape[0]):
        tgt_ref[k] = target


def middle_kernel(got, src, out_ref):
    half = LANES // 2
    lower = lower_lanes()
    row_id = lax.broadcasted_iota(jnp.int32, (8, LANES), 0)
    each = [got[k] for k in range(got.shape[0])]
    counts = [jnp.where(lower, pltpu.roll(g, half, 1), g) for g in each]
    total, shares = joined_counts(counts)
    group = joined_group([jnp.where(lower, g, 0.0) for g in each], counts, shares)
    group = jnp.where(row_id < CLASSES, group, group / total)
    last = jnp.where(lower, group, src[32:40, :])
    for k in range(out_ref.shape[0]):
        out_ref[k, 0:32, :] = src[0:32, :]
        out_ref[k, 32:40, :] = last


def label_rows(width, core, got, src_sq, src_lab, label_ref, xa_ref):
    peers = got.shape[0]
    groups, total, targets = source_joined(
        got, [k + core * (peers - 1 - 2 * k) for k in range(peers)]
    )
    row_id = lax.broadcasted_iota(jnp.int32, (8, LANES), 0)
    lane_id = lax.broadcasted_iota(jnp.int32, (8, LANES), 1)
    each = LANES // width
    sides = ([], [])
    for c, group in enumerate(groups):
        tgt = side_by_side(targets[each * c : each * c + each], width)
        for side, stat in zip(sides, (jnp.where(row_id < CLASSES, group, group / total), tgt)):
            side.append(jnp.where(row_id < CLASSES, stat, jnp.sqrt(stat + 1e-06)))

    def distances(one, other):
        out = jnp.zeros((8, LANES), jnp.float32)
        for k in range(CLASSES):
            far = jnp.zeros((8, LANES), jnp.float32)
            for g, h in zip(one, other):
                gap = g - jnp.where(row_id < CLASSES, h[k : k + 1], h[CLASSES + k : CLASSES + k + 1])
                far = far + gap * gap
            far = far + pltpu.roll(far, 4, 0)
            out = jnp.where(lane_id == k, jnp.sum(far, axis=1, keepdims=True), out)
        return out

    label_ref[...] = distances(*sides)[:CLASSES, :CLASSES]
    by_target = distances(*sides[::-1])
    by_target = jnp.concatenate([by_target, by_target], axis=0)
    row_id = lax.broadcasted_iota(jnp.int32, (16, 1), 0)
    part_id = row_id // CLASSES
    labels = src_lab[...]
    u = jnp.broadcast_to(src_sq[...], (16, ROWS))
    for a in range(CLASSES):
        u = u + jnp.where(labels == a, by_target[:, a : a + 1], 0.0)
    hi, mid, lo = three_parts(-0.5 * u)
    ones = jnp.where(row_id < 15, 1.0, 0.0)
    xa_ref[...] = jnp.where(
        part_id == 0, hi, jnp.where(part_id == 1, mid, jnp.where(part_id == 2, lo, ones))
    ).astype(jnp.bfloat16)


def three_parts(v):
    hi = v.astype(jnp.bfloat16).astype(jnp.float32)
    rest = v - hi
    mid = rest.astype(jnp.bfloat16).astype(jnp.float32)
    return hi, mid, rest - mid


def joined_lse(g_ref):
    g = g_ref[...]
    top = jnp.max(g, axis=0)
    return top + log2(jnp.sum(jnp.exp2(g - top[None]), axis=0))


def row_finish(top, total, out_ref):
    lines = []
    for k in range(CHUNKS):
        at = pl.ds(k * LANES, LANES)
        lse = top[at, :] + log2(jnp.sum(total[at, :], axis=1, keepdims=True))
        lines.append(lse.T[0:1, :])
    line = jnp.concatenate(lines, axis=0)
    out_ref[...] = jnp.broadcast_to(line[None], out_ref.shape)


def widen_top(top):
    for k in range(CHUNKS):
        at = pl.ds(k * LANES, LANES)
        top[at, :] = jnp.broadcast_to(jnp.max(top[at, :], axis=1, keepdims=True), (LANES, LANES))


def over_pairs(count, body, unroll):
    def several(step, _):
        for k in range(unroll):
            body(step * unroll + k)
        return 0

    steps = (count[0] + UNROLL - 1) // UNROLL * (UNROLL // unroll)
    lax.fori_loop(0, steps, several, 0)


def block_at(pairs, index):
    row = pl.multiple_of(pairs[2 * index] * BLOCK, BLOCK)
    return row, pairs[2 * index + 1]


def cost_kernel(n_x, n_f, pairs, count, place, got, src_sq, src_lab, xt, *args):
    pieces, (tgt_lab, label_ref, tiles, out_ref, xa, y, ya, top, total) = args[:n_x], args[n_x:]
    label_rows(n_f, place[1], got, src_sq, src_lab, label_ref, xa)
    row_id = lax.broadcasted_iota(jnp.int32, (16, 1), 0)
    part = row_id // CLASSES
    cls = row_id % CLASSES

    tgt_sq = jnp.zeros((16, ROWS), jnp.float32)
    for far, piece in enumerate(pieces):
        at = lax.rem(place[0] + far, n_x)
        for k in range(piece.shape[0]):
            z = k + place[1] * (piece.shape[0] - 1 - 2 * k)
            y[pl.ds(pl.multiple_of((z * n_x + at) * 16, 16), 16), :] = piece[k]
            v = piece[k].astype(jnp.float32)
            tgt_sq = tgt_sq + v * v

    hi, mid, lo = three_parts(-0.5 * jnp.sum(tgt_sq, axis=0, keepdims=True))
    onehot = jnp.where(tgt_lab[...] == cls, 1.0, 0.0)
    ya[...] = jnp.where(
        part < 3,
        onehot,
        jnp.where(cls == 0, hi, jnp.where(cls == 1, mid, jnp.where(cls == 2, lo, 0.0))),
    ).astype(jnp.bfloat16)

    top[...] = jnp.full(top.shape, LOWEST, jnp.float32)
    total[...] = jnp.zeros(total.shape, jnp.float32)

    def build(index):
        row, col = block_at(pairs, index)
        rows = pl.ds(row, BLOCK)
        cols = pl.ds(pl.multiple_of(col * BLOCK, BLOCK), BLOCK)
        cross = jnp.dot(xt[rows, :], y[:, cols], preferred_element_type=jnp.float32)
        extra = lax.dot_general(
            xa[:, rows], ya[:, cols], (((0,), (0,)), ((), ())), preferred_element_type=jnp.float32
        )
        tile = (cross + extra) * (2.0 * TO_LOG2) + jnp.where(index < count[0], 0.0, LOWEST)
        tiles[index] = tile
        top[rows, :] = jnp.maximum(top[rows, :], jnp.maximum(tile[:, :LANES], tile[:, LANES:]))

    over_pairs(count, build, 12)
    widen_top(top)

    def add(index):
        row, _ = block_at(pairs, index)
        rows = pl.ds(row, BLOCK)
        high = top[rows, :]
        left = jnp.exp2(tiles[index, :, :LANES] - high)
        right = jnp.exp2(tiles[index, :, LANES:] - high)
        total[rows, :] = total[rows, :] + (left + right)

    over_pairs(count, add, 4)
    row_finish(top, total, out_ref)


def row_kernel(log_total, pairs, count, tiles, g_ref, out_ref, pot, top, total):
    pot[...] = log_total - joined_lse(g_ref)
    top[...] = jnp.full(top.shape, LOWEST, jnp.float32)
    total[...] = jnp.zeros(total.shape, jnp.float32)

    def scores(index, col):
        left = tiles[index, :, :LANES] + pot[pl.ds(2 * col, 1), :]
        right = tiles[index, :, LANES:] + pot[pl.ds(2 * col + 1, 1), :]
        return left, right

    def highest(index):
        row, col = block_at(pairs, index)
        rows = pl.ds(row, BLOCK)
        left, right = scores(index, col)
        top[rows, :] = jnp.maximum(top[rows, :], jnp.maximum(left, right))

    over_pairs(count, highest, 4)
    widen_top(top)

    def add(index):
        row, col = block_at(pairs, index)
        rows = pl.ds(row, BLOCK)
        left, right = scores(index, col)
        high = top[rows, :]
        total[rows, :] = total[rows, :] + (jnp.exp2(left - high) + jnp.exp2(right - high))

    over_pairs(count, add, 4)
    row_finish(top, total, out_ref)


def col_kernel(log_total, pairs, count, tiles, g_ref, out_ref, pot_ref, pot, top, total):
    line = log_total - joined_lse(g_ref)
    pot_ref[...] = line * TO_POT
    for k in range(CHUNKS):
        pot[pl.ds(k * LANES, LANES), :] = jnp.broadcast_to(line[k : k + 1, :], (LANES, LANES)).T
    top[...] = jnp.full(top.shape, LOWEST, jnp.float32)
    total[...] = jnp.zeros(total.shape, jnp.float32)

    def scores(index, row):
        rows = pl.ds(row, BLOCK)
        high = pot[rows, :]
        tile = tiles[index]
        return tile + jnp.concatenate([high, high], axis=1)

    def highest(index):
        row, col = block_at(pairs, index)
        score = scores(index, row)
        top[col] = jnp.maximum(top[col], jnp.max(score.reshape(BLOCK // 8, 8, BLOCK), axis=0))

    over_pairs(count, highest, 4)
    for k in range(BLK):
        top[k] = jnp.broadcast_to(jnp.max(top[k], axis=0, keepdims=True), (8, BLOCK))

    def add(index):
        row, col = block_at(pairs, index)
        score = scores(index, row).reshape(BLOCK // 8, 8, BLOCK)
        total[col] = total[col] + jnp.sum(jnp.exp2(score - top[col][None]), axis=0)

    over_pairs(count, add, 4)
    lines = []
    for k in range(BLK):
        lse = top[k][0:1] + log2(jnp.sum(total[k], axis=0, keepdims=True))
        lines += [lse[:, :LANES], lse[:, LANES:]]
    out = jnp.concatenate(lines, axis=0)
    out_ref[...] = jnp.broadcast_to(out[None], out_ref.shape)


def last_kernel(log_total, g_ref, pot_ref):
    pot_ref[...] = (log_total - joined_lse(g_ref)) * TO_POT


def smem():
    return pl.BlockSpec(memory_space=pltpu.SMEM)


def vmem():
    return pl.BlockSpec(memory_space=pltpu.VMEM)


def f32(*shape):
    return jax.ShapeDtypeStruct(shape, jnp.float32)


def params():
    return pltpu.CompilerParams(vmem_limit_bytes=VMEM_LIMIT)


def both_ways(x, axes):
    n = x.shape[0]
    groups = [[2 * k for k in range(n)], [2 * k + 1 for k in reversed(range(n))]]
    return lax.all_to_all(x, axes + ("c",), 0, 0, axis_index_groups=groups)


def on_device(source_embed, target_embed, source_labels, target_labels, pair_blocks, pair_count):
    pairs = pair_blocks.reshape(-1)
    count = pair_count.reshape(-1)
    n_src, n_tgt = lax.axis_size(SRC), lax.axis_size(TGT)

    def call(kernel, out_shape, *args, name):
        return pl.pallas_call(
            kernel,
            out_shape=out_shape,
            in_specs=[vmem()] * len(args),
            out_specs=jax.tree.map(lambda _: vmem(), out_shape),
            compiler_params=params(),
            name=name,
        )(*args)

    n_x, n_z = lax.axis_size("x"), lax.axis_size("z")
    part = target_embed.shape[0]
    near, tgt_group = pl.pallas_call(
        first_kernel,
        out_shape=(
            jax.ShapeDtypeStruct((n_z,) + target_embed.shape, jnp.bfloat16),
            f32(16, LANES),
        ),
        in_specs=[vmem(), vmem()],
        out_specs=(pl.BlockSpec(memory_space=pl.ANY), vmem()),
        scratch_shapes=[pltpu.SemaphoreType.DMA((n_z,))],
        compiler_params=params(),
        name="first",
    )(target_embed, target_labels[None])
    near = both_ways(near, ("z",))

    def around(x, axis):
        n = lax.axis_size(axis)
        return [x] + [
            lax.ppermute(x, axis, [((i + far) % n, i) for i in range(n)]) for far in range(1, n)
        ]

    src_group, src_sq = call(
        source_group_kernel,
        (f32(40, LANES), f32(1, ROWS)),
        source_embed,
        source_labels[None],
        tgt_group,
        name="source_group",
    )

    near, packets = lax.optimization_barrier((near, around(src_group, "x")))
    pieces = around(near, "x")
    src_group, tgt_near = pl.pallas_call(
        functools.partial(near_kernel, part),
        out_shape=(f32(40, LANES), f32(n_tgt, 8, LANES)),
        in_specs=[smem()] + [vmem()] * (n_x + 1),
        out_specs=(vmem(), vmem()),
        scratch_shapes=[pltpu.VMEM((n_x, 40, LANES), jnp.float32)],
        compiler_params=params(),
        name="near",
    )(lax.axis_index("x").reshape(1), *packets, tgt_group)
    tgt_near = lax.all_to_all(tgt_near, TGT, 0, 0)
    tgt_near, source_tall = lax.optimization_barrier((tgt_near, source_embed.T))
    stats = call(middle_kernel, f32(n_z, 40, LANES), tgt_near, src_group, name="middle")
    stats = both_ways(stats, ("z",))

    tall = pltpu.VMEM((ROWS, LANES), jnp.float32)
    wide = pltpu.VMEM((BLK, 8, BLOCK), jnp.float32)
    log_src = math.log2(ROWS * n_src)
    log_tgt = math.log2(ROWS * n_tgt)
    label_cost, tiles, sent = pl.pallas_call(
        functools.partial(cost_kernel, n_x, part * n_x),
        out_shape=(
            f32(CLASSES, CLASSES),
            f32(MAXP, BLOCK, BLOCK),
            f32(n_tgt, CHUNKS, LANES),
        ),
        in_specs=[smem()] * 3 + [vmem()] * (5 + n_x),
        out_specs=(vmem(), vmem(), vmem()),
        scratch_shapes=[
            pltpu.VMEM((16, ROWS), jnp.bfloat16),
            pltpu.VMEM((WIDTH, ROWS), jnp.bfloat16),
            pltpu.VMEM((16, ROWS), jnp.bfloat16),
            tall,
            tall,
        ],
        compiler_params=params(),
        name="cost_rows",
    )(
        pairs,
        count,
        jnp.stack([lax.axis_index("x"), lax.axis_index("c")]),
        stats,
        src_sq,
        source_labels[None],
        source_tall,
        *pieces,
        target_labels[None],
    )

    def columns(got):
        return pl.pallas_call(
            functools.partial(col_kernel, log_tgt),
            out_shape=(f32(n_src, CHUNKS, LANES), f32(CHUNKS, LANES)),
            in_specs=[smem(), smem(), vmem(), vmem()],
            out_specs=(vmem(), vmem()),
            scratch_shapes=[tall, wide, wide],
            compiler_params=params(),
            name="columns",
        )(pairs, count, tiles, got)

    def rows(got):
        return pl.pallas_call(
            functools.partial(row_kernel, log_src),
            out_shape=f32(n_tgt, CHUNKS, LANES),
            in_specs=[smem(), smem(), vmem(), vmem()],
            out_specs=vmem(),
            scratch_shapes=[pltpu.VMEM((CHUNKS, LANES), jnp.float32), tall, tall],
            compiler_params=params(),
            name="rows",
        )(pairs, count, tiles, got)

    sent, _ = columns(lax.all_to_all(sent, TGT, 0, 0))
    sent = rows(lax.all_to_all(sent, SRC, 0, 0))
    sent, src_pot = columns(lax.all_to_all(sent, TGT, 0, 0))
    tgt_pot = pl.pallas_call(
        functools.partial(last_kernel, log_src),
        out_shape=f32(CHUNKS, LANES),
        in_specs=[vmem()],
        out_specs=vmem(),
        compiler_params=params(),
        name="last",
    )(lax.all_to_all(sent, SRC, 0, 0))
    return (src_pot.reshape(-1), tgt_pot.reshape(-1), label_cost)


def solution(mesh):
    fine = Mesh(np.asarray(mesh.devices).reshape(8, 4, 4, 2), SRC + TGT)
    return jax.shard_map(
        on_device,
        mesh=fine,
        in_specs=(
            P(None, SRC),
            P(SRC, TGT),
            P(SRC),
            P(TGT),
            P(SRC, TGT, None, None),
            P(SRC, TGT),
        ),
        out_specs=(P(SRC), P(TGT), P()),
        check_vma=False,
    )
```

```python
import functools
import math

import jax
import jax.numpy as jnp
import numpy as np
from jax import lax
from jax.experimental import pallas as pl
from jax.experimental.pallas import tpu as pltpu
from jax.sharding import Mesh, PartitionSpec as P

CLASSES = 4
BLOCK = 256
ROWS = 2048
BLK = ROWS // BLOCK
LANES = 128
CHUNKS = ROWS // LANES
MAXP = 24
UNROLL = 8
WIDTH = 512

EPSILON = 0.05
LOWEST = -1e30
LOG2E = 1.0 / math.log(2.0)
TO_LOG2 = LOG2E / EPSILON
TO_POT = EPSILON / LOG2E

SRC = ("z", "x")
TGT = ("y", "c")
VMEM_LIMIT = 24 * 1024 * 1024


def log2(x):
    return jnp.log(x) * LOG2E


def repeated_onehot(labels):
    row_id = lax.broadcasted_iota(jnp.int32, (16, 1), 0)
    return jnp.where(row_id < 12, jnp.where(labels == row_id % CLASSES, 1.0, 0.0), 0.0)


def across(onehot, values):
    return lax.dot_general(
        onehot, values, (((1,), (1,)), ((), ())), preferred_element_type=jnp.float32
    )


def class_group(values, onehot, counts):
    part = lax.broadcasted_iota(jnp.int32, (16, 1), 0) // CLASSES
    wide = values.astype(jnp.float32)
    mean = across(onehot, values) / counts
    hi, mid, lo = three_parts(mean)
    parts = jnp.where(
        part == 0, hi, jnp.where(part == 1, mid, jnp.where(part == 2, lo, 0.0))
    ).astype(jnp.bfloat16)
    center = lax.dot_general(
        parts, onehot, (((0,), (0,)), ((), ())), preferred_element_type=jnp.float32
    )
    centered = wide - center
    hi, mid, lo = three_parts(centered * centered)
    spread = sum(across(onehot, p.astype(jnp.bfloat16)) for p in (hi, mid, lo))
    return jnp.where(part == 0, mean, spread)[:8], wide


def first_kernel(embed, labels, near_ref, out_ref, sems):
    copies = [
        pltpu.make_async_copy(embed, near_ref.at[k], sems.at[k]) for k in range(near_ref.shape[0])
    ]
    for copy in copies:
        copy.start()
    onehot = repeated_onehot(labels[...])
    counts = jnp.maximum(jnp.sum(onehot, axis=1, keepdims=True), 1.0)
    group, _ = class_group(embed[...], onehot.astype(jnp.bfloat16), counts)
    out_ref[...] = jnp.zeros(out_ref.shape, jnp.float32)
    out_ref[0:8, 0 : group.shape[1]] = group
    out_ref[8:16, :] = jnp.broadcast_to(counts[:8], (8, LANES))
    for copy in copies:
        copy.wait()


def lower_lanes():
    return lax.broadcasted_iota(jnp.int32, (8, LANES), 1) < LANES // 2


def source_group_kernel(embed, labels, tgt_group, out_ref, sq_ref):
    onehot = repeated_onehot(labels[...])
    counts = jnp.maximum(jnp.sum(onehot, axis=1, keepdims=True), 1.0)
    onehot = onehot.astype(jnp.bfloat16)
    sq = jnp.zeros((1, ROWS), jnp.float32)
    for c in range(WIDTH // LANES):
        group, wide = class_group(embed[c * LANES : (c + 1) * LANES, :], onehot, counts)
        out_ref[8 * c : 8 * c + 8, :] = group
        sq = sq + jnp.sum(wide * wide, axis=0, keepdims=True)
    out_ref[32:40, :] = jnp.where(lower_lanes(), tgt_group[0:8, :], counts[:8])
    sq_ref[...] = sq


def joined_counts(counts):
    total = functools.reduce(jnp.add, counts)
    return total, [c / total for c in counts]


def joined_group(groups, counts, shares):
    row_id = lax.broadcasted_iota(jnp.int32, (8, LANES), 0)
    mean = functools.reduce(jnp.add, [g * w for g, w in zip(groups, shares)])
    between = functools.reduce(
        jnp.add, [(g - mean) * (g - mean) * c for g, c in zip(groups, counts)]
    )
    spread = functools.reduce(jnp.add, groups) + pltpu.roll(between, 4, 0)
    return jnp.where(row_id < CLASSES, mean, spread)


def source_joined(got, order=None):
    peers = got.shape[0]
    order = range(peers) if order is None else order
    half = LANES // 2
    lower = lower_lanes()
    last = [got[k, 32:40, :] for k in order]
    targets = [jnp.where(lower, g, 0.0) for g in last]
    counts = [jnp.where(lower, pltpu.roll(g, half, 1), g) for g in last]
    total, shares = joined_counts(counts)
    groups = [
        joined_group([got[k, 8 * c : 8 * c + 8, :] for k in order], counts, shares)
        for c in range(WIDTH // LANES)
    ]
    return groups, total, targets


def side_by_side(targets, width):
    out = targets[0]
    for k, target in enumerate(targets[1:]):
        out = out + pltpu.roll(target, (k + 1) * width, 1)
    return out


def near_kernel(part, place, *args):
    pieces, (tgt_group, src_ref, tgt_ref, slots) = args[:-4], args[-4:]
    for far, piece in enumerate(pieces):
        slots[lax.rem(place[0] + far, len(pieces))] = piece[...]
    groups, total, targets = source_joined(slots)
    for c, group in enumerate(groups):
        src_ref[8 * c : 8 * c + 8, :] = group
    src_ref[32:40, :] = total
    target = jnp.where(lower_lanes(), side_by_side(targets, part), tgt_group[8:16, :])
    for k in range(tgt_ref.shape[0]):
        tgt_ref[k] = target


def middle_kernel(got, src, out_ref):
    half = LANES // 2
    lower = lower_lanes()
    row_id = lax.broadcasted_iota(jnp.int32, (8, LANES), 0)
    each = [got[k] for k in range(got.shape[0])]
    counts = [jnp.where(lower, pltpu.roll(g, half, 1), g) for g in each]
    total, shares = joined_counts(counts)
    group = joined_group([jnp.where(lower, g, 0.0) for g in each], counts, shares)
    group = jnp.where(row_id < CLASSES, group, group / total)
    last = jnp.where(lower, group, src[32:40, :])
    for k in range(out_ref.shape[0]):
        out_ref[k, 0:32, :] = src[0:32, :]
        out_ref[k, 32:40, :] = last


def label_rows(width, got, src_sq, src_lab, label_ref, xa_ref):
    groups, total, targets = source_joined(got)
    row_id = lax.broadcasted_iota(jnp.int32, (8, LANES), 0)
    lane_id = lax.broadcasted_iota(jnp.int32, (8, LANES), 1)
    each = LANES // width
    sides = ([], [])
    for c, group in enumerate(groups):
        tgt = side_by_side(targets[each * c : each * c + each], width)
        for side, stat in zip(sides, (jnp.where(row_id < CLASSES, group, group / total), tgt)):
            side.append(jnp.where(row_id < CLASSES, stat, jnp.sqrt(stat + 1e-06)))

    def distances(one, other):
        out = jnp.zeros((8, LANES), jnp.float32)
        for k in range(CLASSES):
            far = jnp.zeros((8, LANES), jnp.float32)
            for g, h in zip(one, other):
                gap = g - jnp.where(row_id < CLASSES, h[k : k + 1], h[CLASSES + k : CLASSES + k + 1])
                far = far + gap * gap
            far = far + pltpu.roll(far, 4, 0)
            out = jnp.where(lane_id == k, jnp.sum(far, axis=1, keepdims=True), out)
        return out

    label_ref[...] = distances(*sides)[:CLASSES, :CLASSES]
    by_target = distances(*sides[::-1])
    by_target = jnp.concatenate([by_target, by_target], axis=0)
    row_id = lax.broadcasted_iota(jnp.int32, (16, 1), 0)
    part_id = row_id // CLASSES
    labels = src_lab[...]
    u = jnp.broadcast_to(src_sq[...], (16, ROWS))
    for a in range(CLASSES):
        u = u + jnp.where(labels == a, by_target[:, a : a + 1], 0.0)
    hi, mid, lo = three_parts(-0.5 * u)
    ones = jnp.where(row_id < 15, 1.0, 0.0)
    xa_ref[...] = jnp.where(
        part_id == 0, hi, jnp.where(part_id == 1, mid, jnp.where(part_id == 2, lo, ones))
    ).astype(jnp.bfloat16)


def three_parts(v):
    hi = v.astype(jnp.bfloat16).astype(jnp.float32)
    rest = v - hi
    mid = rest.astype(jnp.bfloat16).astype(jnp.float32)
    return hi, mid, rest - mid


def joined_lse(g_ref):
    g = g_ref[...]
    top = jnp.max(g, axis=0)
    return top + log2(jnp.sum(jnp.exp2(g - top[None]), axis=0))


def row_finish(top, total, out_ref):
    lines = []
    for k in range(CHUNKS):
        at = pl.ds(k * LANES, LANES)
        lse = top[at, :] + log2(jnp.sum(total[at, :], axis=1, keepdims=True))
        lines.append(lse.T[0:1, :])
    line = jnp.concatenate(lines, axis=0)
    out_ref[...] = jnp.broadcast_to(line[None], out_ref.shape)


def widen_top(top):
    for k in range(CHUNKS):
        at = pl.ds(k * LANES, LANES)
        top[at, :] = jnp.broadcast_to(jnp.max(top[at, :], axis=1, keepdims=True), (LANES, LANES))


def over_pairs(count, body, unroll):
    def several(step, _):
        for k in range(unroll):
            body(step * unroll + k)
        return 0

    steps = (count[0] + UNROLL - 1) // UNROLL * (UNROLL // unroll)
    lax.fori_loop(0, steps, several, 0)


def block_at(pairs, index):
    row = pl.multiple_of(pairs[2 * index] * BLOCK, BLOCK)
    return row, pairs[2 * index + 1]


def cost_kernel(n_x, n_f, pairs, count, place, got, src_sq, src_lab, xt, *args):
    pieces, (tgt_lab, label_ref, tiles, out_ref, xa, y, ya, top, total) = args[:n_x], args[n_x:]
    label_rows(n_f, got, src_sq, src_lab, label_ref, xa)
    row_id = lax.broadcasted_iota(jnp.int32, (16, 1), 0)
    part = row_id // CLASSES
    cls = row_id % CLASSES

    tgt_sq = jnp.zeros((16, ROWS), jnp.float32)
    for far, piece in enumerate(pieces):
        at = lax.rem(place[0] + far, n_x)
        for k in range(piece.shape[0]):
            z = k + place[1] * (piece.shape[0] - 1 - 2 * k)
            y[pl.ds(pl.multiple_of((z * n_x + at) * 16, 16), 16), :] = piece[k]
            v = piece[k].astype(jnp.float32)
            tgt_sq = tgt_sq + v * v

    hi, mid, lo = three_parts(-0.5 * jnp.sum(tgt_sq, axis=0, keepdims=True))
    onehot = jnp.where(tgt_lab[...] == cls, 1.0, 0.0)
    ya[...] = jnp.where(
        part < 3,
        onehot,
        jnp.where(cls == 0, hi, jnp.where(cls == 1, mid, jnp.where(cls == 2, lo, 0.0))),
    ).astype(jnp.bfloat16)

    top[...] = jnp.full(top.shape, LOWEST, jnp.float32)
    total[...] = jnp.zeros(total.shape, jnp.float32)

    def build(index):
        row, col = block_at(pairs, index)
        rows = pl.ds(row, BLOCK)
        cols = pl.ds(pl.multiple_of(col * BLOCK, BLOCK), BLOCK)
        cross = jnp.dot(xt[rows, :], y[:, cols], preferred_element_type=jnp.float32)
        extra = lax.dot_general(
            xa[:, rows], ya[:, cols], (((0,), (0,)), ((), ())), preferred_element_type=jnp.float32
        )
        tile = (cross + extra) * (2.0 * TO_LOG2) + jnp.where(index < count[0], 0.0, LOWEST)
        tiles[index] = tile
        top[rows, :] = jnp.maximum(top[rows, :], jnp.maximum(tile[:, :LANES], tile[:, LANES:]))

    over_pairs(count, build, 8)
    widen_top(top)

    def add(index):
        row, _ = block_at(pairs, index)
        rows = pl.ds(row, BLOCK)
        high = top[rows, :]
        left = jnp.exp2(tiles[index, :, :LANES] - high)
        right = jnp.exp2(tiles[index, :, LANES:] - high)
        total[rows, :] = total[rows, :] + (left + right)

    over_pairs(count, add, 4)
    row_finish(top, total, out_ref)


def row_kernel(log_total, pairs, count, tiles, g_ref, out_ref, pot, top, total):
    pot[...] = log_total - joined_lse(g_ref)
    top[...] = jnp.full(top.shape, LOWEST, jnp.float32)
    total[...] = jnp.zeros(total.shape, jnp.float32)

    def scores(index, col):
        left = tiles[index, :, :LANES] + pot[pl.ds(2 * col, 1), :]
        right = tiles[index, :, LANES:] + pot[pl.ds(2 * col + 1, 1), :]
        return left, right

    def highest(index):
        row, col = block_at(pairs, index)
        rows = pl.ds(row, BLOCK)
        left, right = scores(index, col)
        top[rows, :] = jnp.maximum(top[rows, :], jnp.maximum(left, right))

    over_pairs(count, highest, 4)
    widen_top(top)

    def add(index):
        row, col = block_at(pairs, index)
        rows = pl.ds(row, BLOCK)
        left, right = scores(index, col)
        high = top[rows, :]
        total[rows, :] = total[rows, :] + (jnp.exp2(left - high) + jnp.exp2(right - high))

    over_pairs(count, add, 4)
    row_finish(top, total, out_ref)


def col_kernel(log_total, pairs, count, tiles, g_ref, out_ref, pot_ref, pot, top, total):
    line = log_total - joined_lse(g_ref)
    pot_ref[...] = line * TO_POT
    for k in range(CHUNKS):
        pot[pl.ds(k * LANES, LANES), :] = jnp.broadcast_to(line[k : k + 1, :], (LANES, LANES)).T
    top[...] = jnp.full(top.shape, LOWEST, jnp.float32)
    total[...] = jnp.zeros(total.shape, jnp.float32)

    def scores(index, row):
        rows = pl.ds(row, BLOCK)
        high = pot[rows, :]
        tile = tiles[index]
        return tile + jnp.concatenate([high, high], axis=1)

    def highest(index):
        row, col = block_at(pairs, index)
        score = scores(index, row)
        top[col] = jnp.maximum(top[col], jnp.max(score.reshape(BLOCK // 8, 8, BLOCK), axis=0))

    over_pairs(count, highest, 4)
    for k in range(BLK):
        top[k] = jnp.broadcast_to(jnp.max(top[k], axis=0, keepdims=True), (8, BLOCK))

    def add(index):
        row, col = block_at(pairs, index)
        score = scores(index, row).reshape(BLOCK // 8, 8, BLOCK)
        total[col] = total[col] + jnp.sum(jnp.exp2(score - top[col][None]), axis=0)

    over_pairs(count, add, 4)
    lines = []
    for k in range(BLK):
        lse = top[k][0:1] + log2(jnp.sum(total[k], axis=0, keepdims=True))
        lines += [lse[:, :LANES], lse[:, LANES:]]
    out = jnp.concatenate(lines, axis=0)
    out_ref[...] = jnp.broadcast_to(out[None], out_ref.shape)


def last_kernel(log_total, g_ref, pot_ref):
    pot_ref[...] = (log_total - joined_lse(g_ref)) * TO_POT


def smem():
    return pl.BlockSpec(memory_space=pltpu.SMEM)


def vmem():
    return pl.BlockSpec(memory_space=pltpu.VMEM)


def f32(*shape):
    return jax.ShapeDtypeStruct(shape, jnp.float32)


def params():
    return pltpu.CompilerParams(vmem_limit_bytes=VMEM_LIMIT)


def both_ways(x, axes):
    n = x.shape[0]
    groups = [[2 * k for k in range(n)], [2 * k + 1 for k in reversed(range(n))]]
    return lax.all_to_all(x, axes + ("c",), 0, 0, axis_index_groups=groups)


def on_device(source_embed, target_embed, source_labels, target_labels, pair_blocks, pair_count):
    pairs = pair_blocks.reshape(-1)
    count = pair_count.reshape(-1)
    n_src, n_tgt = lax.axis_size(SRC), lax.axis_size(TGT)

    def call(kernel, out_shape, *args, name):
        return pl.pallas_call(
            kernel,
            out_shape=out_shape,
            in_specs=[vmem()] * len(args),
            out_specs=jax.tree.map(lambda _: vmem(), out_shape),
            compiler_params=params(),
            name=name,
        )(*args)

    n_x, n_z = lax.axis_size("x"), lax.axis_size("z")
    part = target_embed.shape[0]
    near, tgt_group = pl.pallas_call(
        first_kernel,
        out_shape=(
            jax.ShapeDtypeStruct((n_z,) + target_embed.shape, jnp.bfloat16),
            f32(16, LANES),
        ),
        in_specs=[vmem(), vmem()],
        out_specs=(pl.BlockSpec(memory_space=pl.ANY), vmem()),
        scratch_shapes=[pltpu.SemaphoreType.DMA((n_z,))],
        compiler_params=params(),
        name="first",
    )(target_embed, target_labels[None])
    near = both_ways(near, ("z",))

    def around(x, axis):
        n = lax.axis_size(axis)
        return [x] + [
            lax.ppermute(x, axis, [((i + far) % n, i) for i in range(n)]) for far in range(1, n)
        ]

    src_group, src_sq = call(
        source_group_kernel,
        (f32(40, LANES), f32(1, ROWS)),
        source_embed,
        source_labels[None],
        tgt_group,
        name="source_group",
    )

    near, packets = lax.optimization_barrier((near, around(src_group, "x")))
    pieces = around(near, "x")
    src_group, tgt_near = pl.pallas_call(
        functools.partial(near_kernel, part),
        out_shape=(f32(40, LANES), f32(n_tgt, 8, LANES)),
        in_specs=[smem()] + [vmem()] * (n_x + 1),
        out_specs=(vmem(), vmem()),
        scratch_shapes=[pltpu.VMEM((n_x, 40, LANES), jnp.float32)],
        compiler_params=params(),
        name="near",
    )(lax.axis_index("x").reshape(1), *packets, tgt_group)
    tgt_near = lax.all_to_all(tgt_near, TGT, 0, 0)
    tgt_near, source_tall = lax.optimization_barrier((tgt_near, source_embed.T))
    stats = call(middle_kernel, f32(n_z, 40, LANES), tgt_near, src_group, name="middle")
    stats = lax.all_to_all(stats, "z", 0, 0)

    tall = pltpu.VMEM((ROWS, LANES), jnp.float32)
    wide = pltpu.VMEM((BLK, 8, BLOCK), jnp.float32)
    log_src = math.log2(ROWS * n_src)
    log_tgt = math.log2(ROWS * n_tgt)
    label_cost, tiles, sent = pl.pallas_call(
        functools.partial(cost_kernel, n_x, part * n_x),
        out_shape=(
            f32(CLASSES, CLASSES),
            f32(MAXP, BLOCK, BLOCK),
            f32(n_tgt, CHUNKS, LANES),
        ),
        in_specs=[smem()] * 3 + [vmem()] * (5 + n_x),
        out_specs=(vmem(), vmem(), vmem()),
        scratch_shapes=[
            pltpu.VMEM((16, ROWS), jnp.bfloat16),
            pltpu.VMEM((WIDTH, ROWS), jnp.bfloat16),
            pltpu.VMEM((16, ROWS), jnp.bfloat16),
            tall,
            tall,
        ],
        compiler_params=params(),
        name="cost_rows",
    )(
        pairs,
        count,
        jnp.stack([lax.axis_index("x"), lax.axis_index("c")]),
        stats,
        src_sq,
        source_labels[None],
        source_tall,
        *pieces,
        target_labels[None],
    )

    def columns(got):
        return pl.pallas_call(
            functools.partial(col_kernel, log_tgt),
            out_shape=(f32(n_src, CHUNKS, LANES), f32(CHUNKS, LANES)),
            in_specs=[smem(), smem(), vmem(), vmem()],
            out_specs=(vmem(), vmem()),
            scratch_shapes=[tall, wide, wide],
            compiler_params=params(),
            name="columns",
        )(pairs, count, tiles, got)

    def rows(got):
        return pl.pallas_call(
            functools.partial(row_kernel, log_src),
            out_shape=f32(n_tgt, CHUNKS, LANES),
            in_specs=[smem(), smem(), vmem(), vmem()],
            out_specs=vmem(),
            scratch_shapes=[pltpu.VMEM((CHUNKS, LANES), jnp.float32), tall, tall],
            compiler_params=params(),
            name="rows",
        )(pairs, count, tiles, got)

    sent, _ = columns(lax.all_to_all(sent, TGT, 0, 0))
    sent = rows(lax.all_to_all(sent, SRC, 0, 0))
    sent, src_pot = columns(lax.all_to_all(sent, TGT, 0, 0))
    tgt_pot = pl.pallas_call(
        functools.partial(last_kernel, log_src),
        out_shape=f32(CHUNKS, LANES),
        in_specs=[vmem()],
        out_specs=vmem(),
        compiler_params=params(),
        name="last",
    )(lax.all_to_all(sent, SRC, 0, 0))
    return (src_pot.reshape(-1), tgt_pot.reshape(-1), label_cost)


def solution(mesh):
    fine = Mesh(np.asarray(mesh.devices).reshape(8, 4, 4, 2), SRC + TGT)
    return jax.shard_map(
        on_device,
        mesh=fine,
        in_specs=(
            P(None, SRC),
            P(SRC, TGT),
            P(SRC),
            P(TGT),
            P(SRC, TGT, None, None),
            P(SRC, TGT),
        ),
        out_specs=(P(SRC), P(TGT), P()),
        check_vma=False,
    )
```
